32 devices in a mesh: row: 8 (over y, x, core), col: 4 (over z).
Axes of the slice: x: 2, y: 2, z: 4, core: 2. Of those that a mesh axis runs over, the one named last changes fastest.
Arguments:
- features: bfloat16 [8, 4, 128, 128], P('row', 'col'), may hold values from -6 to 6
- tiles: bfloat16 [8, 4, 128, 128, 128], P('row', 'col'), may hold values from -0.3984375 to 0.3984375
- tile_coords: int32 [8, 4, 128, 2], P('row', 'col'), may hold values from 0 to 7, as said below
- tile_count: int32 [8, 4], P('row', 'col'), may hold values from 1 to 128, as said below
- batch_mask: int32 [8, 4, 128], P('row', 'col'), may hold values 0 or 1
- history: bfloat16 [8, 4, 128, 256], P('row', 'col'), may hold values from 0 to 1.5
- weight_one: bfloat16 [128, 256], replicated, may hold values from -0.5 to 0.5
- bias_one: float32 [256], replicated, may hold values from -3 to 3
- weight_two: bfloat16 [256, 172], replicated, may hold values from -0.375 to 0.375
- bias_two: float32 [172], replicated, may hold values from -3 to 3
Outputs:
- new_history: bfloat16 [8, 4, 128, 256], P('row', 'col')
- logits: float32 [8, 4, 128, 172], P('row', 'col')
The draws below stay inside these ranges and needn't reach their ends.
Inputs may be any that keep to these rules, and one draw needn't show every extreme that they name: `tile_coords`: column 0 is below 4 and column 1 below 8; coordinates may repeat. `tile_count`: some device has all 128 slots live.
All inputs are finite; a program needn't handle non-finite values. No bound on the sum of `batch_mask` on one device may be relied on, other than what follows from the above.
Results may differ from the reference program's by a relative error of at most 0.024.
Values may be sent and summed in bfloat16 or wider, within the bound.
No kernel may reach another device: no remote copies, remote signals or barrier semaphores. Data moves between devices by JAX's collectives and lax.ppermute only.
A program may use at most 64 MiB of HBM per device.

```python
import jax
import jax.numpy as jnp
from jax import lax

BLOCK = 128
F_IN = 128
HID = 256
CLASSES = 172
TILES_DEV = 128
N_ROW = 8
N_COL = 4


def draw_tile_coords(key, part):
    first_key, second_key = jax.random.split(jax.random.fold_in(key, 11))
    block_rows = jax.random.randint(first_key, (N_ROW, N_COL, TILES_DEV, 1), 0, N_COL)
    block_cols = jax.random.randint(second_key, (N_ROW, N_COL, TILES_DEV, 1), 0, N_ROW)
    return jnp.concatenate([block_rows, block_cols], axis=-1).astype(jnp.int32)


def draw_tile_count(key, part):
    first_key, second_key, third_key = jax.random.split(jax.random.fold_in(key, 23), 3)
    first_draw = jax.random.randint(first_key, (N_ROW * N_COL,), 1, TILES_DEV + 1)
    second_draw = jax.random.randint(second_key, (N_ROW * N_COL,), 1, TILES_DEV + 1)
    fullest = jax.random.randint(third_key, (), 0, N_ROW * N_COL)
    counts = jnp.minimum(first_draw, second_draw).at[fullest].set(TILES_DEV)
    return counts.reshape(N_ROW, N_COL).astype(jnp.int32)


def with_ends(entries, rng, least, largest):
    index_at = [jax.random.randint(jax.random.fold_in(rng, axis), (), 0, length) for axis, length in enumerate(entries.shape)]
    main_axis = entries.shape.index(max(entries.shape))
    next_to = index_at[:main_axis] + [(index_at[main_axis] + 1) % entries.shape[main_axis]] + index_at[main_axis + 1:]
    return entries.at[tuple(index_at)].set(least).at[tuple(next_to)].set(largest)


def level_of(rng, shape, cuts, least, high):
    factor_of, own = 1.0, jax.random.fold_in(rng, 6)
    for dim, parts in cuts:
        heights = jnp.exp(jax.random.uniform(jax.random.fold_in(own, dim), (parts,), jnp.float32, least / len(cuts), high / len(cuts)))
        factor_of = factor_of * jnp.repeat(heights, shape[dim] // parts).reshape([-1 if axis == dim else 1 for axis in range(len(shape))])
    return factor_of


def gaussian(stream_key, extent, width, limit, cuts=(), kind=jnp.bfloat16):
    loudness = level_of(stream_key, extent, cuts, -0.22, 0.18) if cuts else 1.0
    array = jax.random.normal(stream_key, extent, jnp.float32) * width * loudness
    return jnp.minimum(jnp.maximum(array, -limit), limit).astype(kind)


def setup_inputs(seed: int = 0) -> dict:
    splits = jax.random.split(jax.random.key(seed), 11)
    return {
        "features": gaussian(splits[0], (N_ROW, N_COL, BLOCK, F_IN), 1.0, 6.0, ((0, 8), (1, 4))),
        "tiles": gaussian(splits[1], (N_ROW, N_COL, TILES_DEV, BLOCK, BLOCK), 0.05, 0.3984375, ((0, 8), (1, 4))),
        "tile_coords": draw_tile_coords(jax.random.fold_in(splits[10], 71), 0),
        "tile_count": draw_tile_count(jax.random.fold_in(splits[10], 71), 0),
        "batch_mask": with_ends((jax.random.randint(splits[4], (N_ROW, N_COL, BLOCK), 0, 2) < 1).astype(jnp.int32), jax.random.fold_in(splits[4], 1), 0, 1),
        "history": jnp.clip(1.5 * jax.random.uniform(splits[5], (N_ROW, N_COL, BLOCK, HID), jnp.float32) ** level_of(splits[5], (N_ROW, N_COL, BLOCK, HID), ((0, 8), (1, 4)), -0.2, 0.2), 0.0, 1.5).astype(jnp.bfloat16),
        "weight_one": gaussian(splits[6], (F_IN, HID), F_IN ** -0.5, 0.5),
        "bias_one": gaussian(splits[7], (HID,), 0.5, 3.0, (), jnp.float32),
        "weight_two": gaussian(splits[8], (HID, CLASSES), HID ** -0.5, 0.375),
        "bias_two": gaussian(splits[9], (CLASSES,), 0.5, 3.0, (), jnp.float32),
    }


def partial_sums(node_data, tiles, tile_coords, tile_count):
    row_blocks = node_data.shape[1]
    slots = tiles.shape[2]
    col_ids = jnp.arange(row_blocks, dtype=jnp.int32)

    def one_device(tile_set, coord_set, live_total, col_index):
        sources = node_data[coord_set[:, 1], col_index].astype(jnp.float32)
        products = jnp.einsum("tij,tjf->tif", tile_set.astype(jnp.float32), sources, precision=lax.Precision.HIGHEST)
        alive = (jnp.arange(slots, dtype=jnp.int32) < live_total).astype(jnp.float32)
        placing = (coord_set[:, 0][None, :] == col_ids[:, None]).astype(jnp.float32) * alive[None, :]
        summed = jnp.einsum("rt,tif->rif", placing, products, precision=lax.Precision.HIGHEST)
        rounded = lax.optimization_barrier(summed.astype(jnp.bfloat16))
        return rounded.astype(jnp.float32)

    def one_row(packed):
        tile_row, coord_row, count_row = packed
        pieces = jax.vmap(one_device)(tile_row, coord_row, count_row, col_ids)
        return jnp.sum(pieces, axis=0)

    return lax.map(one_row, (tiles, tile_coords, tile_count))


def reference(features, tiles, tile_coords, tile_count, batch_mask, history, weight_one, bias_one, weight_two, bias_two):
    agg_one = (features.astype(jnp.float32) + partial_sums(features, tiles, tile_coords, tile_count)).astype(jnp.bfloat16)
    pre_one = jnp.einsum("rcif,fh->rcih", agg_one.astype(jnp.float32), weight_one.astype(jnp.float32), precision=lax.Precision.HIGHEST)
    hidden = jax.nn.relu(pre_one + bias_one).astype(jnp.bfloat16)
    new_history = jnp.where(batch_mask[..., None] == 1, hidden, history)
    pre_two = jnp.einsum("rcih,hk->rcik", new_history.astype(jnp.float32), weight_two.astype(jnp.float32), precision=lax.Precision.HIGHEST)
    projected = lax.optimization_barrier(pre_two.astype(jnp.bfloat16))
    logits = projected.astype(jnp.float32) + partial_sums(projected, tiles, tile_coords, tile_count) + bias_two
    return new_history, logits
```

```python
import functools

import jax
import jax.numpy as jnp
from jax import lax
from jax.experimental import pallas as pl
from jax.experimental.pallas import tpu as pltpu
from jax.sharding import PartitionSpec as P

BF16 = jnp.bfloat16
F32 = jnp.float32
VMEM_LIMIT = 48 * 1024 * 1024


def partner(index, slot, size):
    if size & (size - 1) == 0:
        return index ^ slot
    return (index + slot) % size


def slot_of(owner, index, size):
    if size & (size - 1) == 0:
        return owner ^ index
    return lax.rem(owner - index + size, size)


def fetch_all(block, axis, size):
    held = [block]
    for slot in range(1, size):
        pairs = [(partner(i, slot, size), i) for i in range(size)]
        held.append(lax.ppermute(block, axis, pairs))
    return held


def send_each(blocks, axis, size):
    arrived = []
    for slot in range(1, size):
        pairs = [(i, partner(i, slot, size)) for i in range(size)]
        arrived.append(lax.ppermute(blocks[slot], axis, pairs))
    return arrived


def call(kernel, out_shape, operands, specs=None, scratch=(), cost=None):
    vmem = pl.BlockSpec(memory_space=pltpu.VMEM)
    return pl.pallas_call(
        kernel,
        out_shape=out_shape,
        in_specs=specs or [vmem] * len(operands),
        out_specs=jax.tree.map(lambda _: vmem, out_shape),
        scratch_shapes=list(scratch),
        cost_estimate=cost,
        compiler_params=pltpu.CompilerParams(vmem_limit_bytes=VMEM_LIMIT),
    )(*operands)


def dot_nt(left, right):
    return lax.dot_general(left, right, (((1,), (1,)), ((), ())), preferred_element_type=F32)


def build_kernel(
    n_row, n_col, chunks,
    coords_ref, count_ref, mask_ref, bias_ref, tiles_ref,
    dense_ref, mask_out_ref, bias_out_ref,
    tile_buf, even, odd, wide, sems,
):
    slots, block = tile_buf.shape[0], tile_buf.shape[1]
    per = slots // chunks
    copies = [
        pltpu.make_async_copy(
            tiles_ref.at[pl.ds(i * per, per)], tile_buf.at[pl.ds(i * per, per)], sems.at[i]
        )
        for i in range(chunks)
    ]
    for copy in copies:
        copy.start()
    row, col = lax.axis_index("row"), lax.axis_index("col")
    live = count_ref[0, 0]
    even[...] = jnp.zeros_like(even)
    odd[...] = jnp.zeros_like(odd)
    mask_rows = jnp.broadcast_to(mask_ref[...].astype(F32), (block, block))
    mask_out_ref[...] = mask_rows.T
    classes = bias_ref.shape[1]
    wide[...] = jnp.zeros_like(wide)
    wide[:, :classes] = jnp.broadcast_to(bias_ref[...], (block, classes))
    bias_out_ref[...] = wide[...].T[:classes]

    def place(t):
        a, b = coords_ref[0, t], coords_ref[1, t]
        k, j = slot_of(a, col, n_col), slot_of(b, row, n_row)
        return jnp.where(t < live, k * n_row + j, n_row * n_col)

    for i in range(chunks):
        copies[i].wait()

        @pl.loop(0, per // 2, unroll=4)
        def _(pair):
            t = i * per + 2 * pair
            first, second = place(t), place(t + 1)
            even[first] += tile_buf[t].astype(F32)
            odd[second] += tile_buf[t + 1].astype(F32)

    for k in range(n_col):
        for j in range(n_row):
            at = k * n_row + j
            dense_ref[k * block : (k + 1) * block, j * block : (j + 1) * block] = (
                even[at] + odd[at]
            ).astype(BF16)


def layer_one_kernel(n_row, dense_ref, *refs):
    block = refs[0].shape[0]
    inputs, outputs, gathered = refs[:n_row], refs[n_row:-1], refs[-1]
    for j in range(n_row):
        gathered[j * block : (j + 1) * block, :] = inputs[j][...]
    for k, out in enumerate(outputs):
        out[...] = jnp.dot(
            dense_ref[k * block : (k + 1) * block, :], gathered[...], preferred_element_type=F32
        ).astype(BF16)


def hidden_kernel(n_col, *refs):
    parts = refs[:n_col]
    feat, w_one, b_one, w_two, mask, history, pushed_ref, proj_ref = refs[n_col:]
    total = feat[...].astype(F32)
    for part in parts:
        total += part[...].astype(F32)
    pre = jnp.dot(total.astype(BF16), w_one[...], preferred_element_type=F32) + b_one[...]
    hidden = jnp.maximum(pre, 0.0)
    chosen = jnp.concatenate([mask[...]] * (hidden.shape[1] // mask.shape[1]), axis=1) == 1.0
    pushed = jnp.where(chosen, hidden, history[...].astype(F32)).astype(BF16)
    pushed_ref[...] = pushed
    proj_ref[...] = dot_nt(w_two[...], pushed).astype(BF16)


def layer_two_kernel(n_row, dense_ref, *refs):
    block = refs[0].shape[1]
    inputs, outputs, gathered = refs[:n_row], refs[n_row:-1], refs[-1]
    for j in range(n_row):
        gathered[:, j * block : (j + 1) * block] = inputs[j][...]
    for k, out in enumerate(outputs):
        out[...] = dot_nt(gathered[...], dense_ref[k * block : (k + 1) * block, :]).astype(BF16)


def logits_kernel(n_col, *refs):
    parts = refs[:n_col]
    proj, bias, out = refs[n_col:]
    total = proj[...].astype(F32) + bias[...]
    for part in parts:
        total += part[...].astype(F32)
    out[...] = total


def tiles_kernel(
    n_row, n_col, transposed, coords_ref, count_ref, tiles_ref, stacked_ref, out_ref, total, sem
):
    row, col = lax.axis_index("row"), lax.axis_index("col")
    tile_buf = tiles_ref
    total[...] = jnp.zeros_like(total)

    @pl.loop(0, count_ref[0, 0])
    def _(t):
        k = slot_of(coords_ref[0, t], col, n_col)
        j = slot_of(coords_ref[1, t], row, n_row)
        if transposed:
            total[k] += dot_nt(stacked_ref[j], tile_buf[t])
        else:
            total[k] += jnp.dot(tile_buf[t], stacked_ref[j], preferred_element_type=F32)

    out_ref[...] = total[...].astype(BF16)


def on_device(
    n_row, n_col,
    features, tiles, tile_coords, tile_count, batch_mask, history,
    weight_one, bias_one, weight_two, bias_two,
):
    feat, tile_set, hist = features[0, 0], tiles[0, 0], history[0, 0]
    coords = tile_coords[0, 0].T
    slots, block = tile_set.shape[0], tile_set.shape[1]
    f_in, hid, classes = feat.shape[1], weight_one.shape[1], weight_two.shape[1]
    w_two_t = weight_two.T
    dense_form = n_row * n_col <= slots
    places = n_row * n_col
    smem = pl.BlockSpec(memory_space=pltpu.SMEM)
    vmem = pl.BlockSpec(memory_space=pltpu.VMEM)
    anywhere = pl.BlockSpec(memory_space=pl.ANY)
    shape = jax.ShapeDtypeStruct

    held_one = fetch_all(feat, "row", n_row)

    if dense_form:
        chunks = 8
        dense, mask_cols, bias_cols = call(
            functools.partial(build_kernel, n_row, n_col, chunks),
            (
                shape((n_col * block, n_row * block), BF16),
                shape((block, block), F32),
                shape((classes, block), F32),
            ),
            (coords, tile_count, batch_mask[0], bias_two[None], tile_set),
            specs=[smem, smem, vmem, vmem, anywhere],
            scratch=[
                pltpu.VMEM((slots, block, block), BF16),
                pltpu.VMEM((places + 1, block, block), F32),
                pltpu.VMEM((places + 1, block, block), F32),
                pltpu.VMEM((block, -(-classes // 128) * 128), F32),
                pltpu.SemaphoreType.DMA((chunks,)),
            ],
        )
        parts_one = call(
            functools.partial(layer_one_kernel, n_row),
            [shape((block, f_in), BF16)] * n_col,
            (dense, *held_one),
            scratch=[pltpu.VMEM((n_row * block, f_in), BF16)],
        )
    else:
        mask_cols = jnp.broadcast_to(batch_mask[0, 0].astype(F32)[:, None], (block, block))
        bias_cols = jnp.broadcast_to(bias_two[:, None], (classes, block))
        summed = call(
            functools.partial(tiles_kernel, n_row, n_col, False),
            shape((n_col, block, f_in), BF16),
            (coords, tile_count, tile_set, jnp.stack(held_one)),
            specs=[smem, smem, vmem, vmem],
            scratch=[pltpu.VMEM((n_col, block, f_in), F32), pltpu.SemaphoreType.DMA(())],
        )
        parts_one = [summed[k] for k in range(n_col)]

    arrived_one = send_each(parts_one, "col", n_col)
    pushed, proj = call(
        functools.partial(hidden_kernel, n_col),
        (shape((block, hid), BF16), shape((classes, block), BF16)),
        (parts_one[0], *arrived_one, feat, weight_one, bias_one[None], w_two_t, mask_cols, hist),
    )
    held_two = fetch_all(proj, "row", n_row)

    if dense_form:
        parts_two = call(
            functools.partial(layer_two_kernel, n_row),
            [shape((classes, block), BF16)] * n_col,
            (dense, *held_two),
            scratch=[pltpu.VMEM((classes, n_row * block), BF16)],
        )
    else:
        summed = call(
            functools.partial(tiles_kernel, n_row, n_col, True),
            shape((n_col, classes, block), BF16),
            (coords, tile_count, tile_set, jnp.stack(held_two)),
            specs=[smem, smem, vmem, vmem],
            scratch=[pltpu.VMEM((n_col, classes, block), F32), pltpu.SemaphoreType.DMA(())],
        )
        parts_two = [summed[k] for k in range(n_col)]

    arrived_two = send_each(parts_two, "col", n_col)
    scores = call(
        functools.partial(logits_kernel, n_col),
        shape((classes, block), F32),
        (parts_two[0], *arrived_two, proj, bias_cols),
    )
    return pushed[None, None], scores.T[None, None]


def solution(mesh):
    sizes = mesh.shape
    return jax.shard_map(
        functools.partial(on_device, sizes["row"], sizes["col"]),
        mesh=mesh,
        in_specs=(
            P("row", "col", None, None),
            P("row", "col", None, None, None),
            P("row", "col", None, None),
            P("row", "col"),
            P("row", "col", None),
            P("row", "col", None, None),
            P(),
            P(),
            P(),
            P(),
        ),
        out_specs=(P("row", "col", None, None), P("row", "col", None, None)),
        check_vma=False,
    )
```

```python
import functools

import jax
import jax.numpy as jnp
from jax import lax
from jax.experimental import pallas as pl
from jax.experimental.pallas import tpu as pltpu
from jax.sharding import PartitionSpec as P

BF16 = jnp.bfloat16
F32 = jnp.float32
VMEM_LIMIT = 48 * 1024 * 1024


def exchange(stacked, axis):
    return lax.all_to_all(stacked, axis, split_axis=0, concat_axis=0, tiled=True)


def call(kernel, out_shape, operands, specs=None, scratch=(), cost=None):
    vmem = pl.BlockSpec(memory_space=pltpu.VMEM)
    return pl.pallas_call(
        kernel,
        out_shape=out_shape,
        in_specs=specs or [vmem] * len(operands),
        out_specs=jax.tree.map(lambda _: vmem, out_shape),
        scratch_shapes=list(scratch),
        cost_estimate=cost,
        compiler_params=pltpu.CompilerParams(vmem_limit_bytes=VMEM_LIMIT),
    )(*operands)


def dot_nt(left, right):
    return lax.dot_general(left, right, (((1,), (1,)), ((), ())), preferred_element_type=F32)


def build_kernel(
    n_row, n_col, chunks,
    count, coords_hbm, mask_hbm, bias_hbm, tiles_hbm,
    dense_ref, mask_out_ref, bias_out_ref,
    coords, mask, bias, tile_buf, even, odd, wide, sems, small_sems,
):
    slots, block = tile_buf.shape[0], tile_buf.shape[1]
    per = slots // chunks
    small = [
        pltpu.make_async_copy(src, dst, small_sems.at[i])
        for i, (src, dst) in enumerate(
            [(coords_hbm, coords), (mask_hbm, mask), (bias_hbm, bias)]
        )
    ]
    copies = [
        pltpu.make_async_copy(
            tiles_hbm.at[pl.ds(i * per, per)], tile_buf.at[pl.ds(i * per, per)], sems.at[i]
        )
        for i in range(chunks)
    ]
    for copy in small + copies:
        copy.start()
    even[...] = jnp.zeros_like(even)
    odd[...] = jnp.zeros_like(odd)
    wide[...] = jnp.zeros_like(wide)
    for copy in small:
        copy.wait()
    live = count[0, 0]
    mask_rows = jnp.broadcast_to(mask[...].astype(F32), (block, block))
    mask_out_ref[...] = mask_rows.T
    classes = bias.shape[1]
    wide[:, :classes] = jnp.broadcast_to(bias[...], (block, classes))
    bias_out_ref[...] = wide[...].T[:classes]

    def place(t):
        return jnp.where(t < live, coords[0, t] * n_row + coords[1, t], n_row * n_col)

    for i in range(chunks):
        copies[i].wait()

        @pl.loop(0, per // 2, unroll=4)
        def _(pair):
            t = i * per + 2 * pair
            first, second = place(t), place(t + 1)
            even[first] += tile_buf[t].astype(F32)
            odd[second] += tile_buf[t + 1].astype(F32)

    for k in range(n_col):
        for j in range(n_row):
            at = k * n_row + j
            dense_ref[k * block : (k + 1) * block, j * block : (j + 1) * block] = (
                even[at] + odd[at]
            ).astype(BF16)


def layer_one_kernel(dense_ref, held_ref, out_ref):
    n_col, block, f_in = out_ref.shape
    gathered = held_ref[...].reshape(-1, f_in)
    for k in range(n_col):
        out_ref[k] = jnp.dot(
            dense_ref[k * block : (k + 1) * block, :], gathered, preferred_element_type=F32
        ).astype(BF16)


def hidden_kernel(
    parts, feat, w_one, b_one, w_two, mask, history, pushed_ref, proj_ref, copies_ref
):
    total = feat[...].astype(F32)
    for k in range(parts.shape[0]):
        total += parts[k].astype(F32)
    pre = jnp.dot(total.astype(BF16), w_one[...], preferred_element_type=F32) + b_one[...]
    hidden = jnp.maximum(pre, 0.0)
    chosen = jnp.concatenate([mask[...]] * (hidden.shape[1] // mask.shape[1]), axis=1) == 1.0
    pushed = jnp.where(chosen, hidden, history[...].astype(F32)).astype(BF16)
    pushed_ref[...] = pushed
    proj = dot_nt(w_two[...], pushed).astype(BF16)
    proj_ref[...] = proj
    for j in range(copies_ref.shape[0]):
        copies_ref[j] = proj


def layer_two_kernel(dense_ref, held_ref, out_ref, gathered):
    n_row, block = held_ref.shape[0], held_ref.shape[2]
    for j in range(n_row):
        gathered[:, j * block : (j + 1) * block] = held_ref[j]
    for k in range(out_ref.shape[0]):
        out_ref[k] = dot_nt(gathered[...], dense_ref[k * block : (k + 1) * block, :]).astype(BF16)


def logits_kernel(parts, proj, bias, out):
    total = proj[...].astype(F32) + bias[...]
    for k in range(parts.shape[0]):
        total += parts[k].astype(F32)
    out[...] = total


def tiles_kernel(
    transposed, coords_ref, count_ref, tiles_ref, stacked_ref, out_ref, total
):
    total[...] = jnp.zeros_like(total)

    @pl.loop(0, count_ref[0, 0])
    def _(t):
        k, j = coords_ref[0, t], coords_ref[1, t]
        if transposed:
            total[k] += dot_nt(stacked_ref[j], tiles_ref[t])
        else:
            total[k] += jnp.dot(tiles_ref[t], stacked_ref[j], preferred_element_type=F32)

    out_ref[...] = total[...].astype(BF16)


def on_device(
    n_row, n_col,
    features, tiles, tile_coords, tile_count, batch_mask, history,
    weight_one, bias_one, weight_two, bias_two,
):
    feat, tile_set, hist = features[0, 0], tiles[0, 0], history[0, 0]
    coords = tile_coords[0, 0].T
    slots, block = tile_set.shape[0], tile_set.shape[1]
    f_in, hid, classes = feat.shape[1], weight_one.shape[1], weight_two.shape[1]
    w_two_t = weight_two.T
    dense_form = n_row * n_col <= slots
    places = n_row * n_col
    smem = pl.BlockSpec(memory_space=pltpu.SMEM)
    vmem = pl.BlockSpec(memory_space=pltpu.VMEM)
    shape = jax.ShapeDtypeStruct

    held_one = exchange(jnp.broadcast_to(feat[None], (n_row, block, f_in)), "row")

    if dense_form:
        chunks = 8
        hbm = pl.BlockSpec(memory_space=pltpu.HBM)
        dense, mask_cols, bias_cols = call(
            functools.partial(build_kernel, n_row, n_col, chunks),
            (
                shape((n_col * block, n_row * block), BF16),
                shape((block, block), F32),
                shape((classes, block), F32),
            ),
            [tile_count]
            + [
                pltpu.with_memory_space_constraint(x, pltpu.HBM)
                for x in (coords, batch_mask[0], bias_two[None], tile_set)
            ],
            specs=[smem] + [hbm] * 4,
            scratch=[
                pltpu.SMEM((2, slots), jnp.int32),
                pltpu.VMEM((1, block), jnp.int32),
                pltpu.VMEM((1, classes), F32),
                pltpu.VMEM((slots, block, block), BF16),
                pltpu.VMEM((places + 1, block, block), F32),
                pltpu.VMEM((places + 1, block, block), F32),
                pltpu.VMEM((block, -(-classes // 128) * 128), F32),
                pltpu.SemaphoreType.DMA((chunks,)),
                pltpu.SemaphoreType.DMA((3,)),
            ],
            cost=pl.CostEstimate(
                flops=slots * block * block, bytes_accessed=2 * slots * block * block, transcendentals=0
            ),
        )
        parts_one = call(
            layer_one_kernel, shape((n_col, block, f_in), BF16), (dense, held_one)
        )
    else:
        mask_cols = jnp.broadcast_to(batch_mask[0, 0].astype(F32)[:, None], (block, block))
        bias_cols = jnp.broadcast_to(bias_two[:, None], (classes, block))
        parts_one = call(
            functools.partial(tiles_kernel, False),
            shape((n_col, block, f_in), BF16),
            (coords, tile_count, tile_set, held_one),
            specs=[smem, smem, vmem, vmem],
            scratch=[pltpu.VMEM((n_col, block, f_in), F32)],
        )

    arrived_one = exchange(parts_one, "col")
    pushed, proj, copies = call(
        hidden_kernel,
        (
            shape((block, hid), BF16),
            shape((classes, block), BF16),
            shape((n_row, classes, block), BF16),
        ),
        (arrived_one, feat, weight_one, bias_one[None], w_two_t, mask_cols, hist),
    )
    held_two = exchange(copies, "row")

    if dense_form:
        parts_two = call(
            layer_two_kernel,
            shape((n_col, classes, block), BF16),
            (dense, held_two),
            scratch=[pltpu.VMEM((classes, n_row * block), BF16)],
        )
    else:
        parts_two = call(
            functools.partial(tiles_kernel, True),
            shape((n_col, classes, block), BF16),
            (coords, tile_count, tile_set, held_two),
            specs=[smem, smem, vmem, vmem],
            scratch=[pltpu.VMEM((n_col, classes, block), F32)],
        )

    arrived_two = exchange(parts_two, "col")
    scores = call(logits_kernel, shape((classes, block), F32), (arrived_two, proj, bias_cols))
    return pushed[None, None], scores.T[None, None]


def solution(mesh):
    sizes = mesh.shape
    return jax.shard_map(
        functools.partial(on_device, sizes["row"], sizes["col"]),
        mesh=mesh,
        in_specs=(
            P("row", "col", None, None),
            P("row", "col", None, None, None),
            P("row", "col", None, None),
            P("row", "col"),
            P("row", "col", None),
            P("row", "col", None, None),
            P(),
            P(),
            P(),
            P(),
        ),
        out_specs=(P("row", "col", None, None), P("row", "col", None, None)),
        check_vma=False,
    )
```

```python
import functools

import jax
import jax.numpy as jnp
from jax import lax
from jax.experimental import pallas as pl
from jax.experimental.pallas import tpu as pltpu
from jax.sharding import PartitionSpec as P

BF16 = jnp.bfloat16
F32 = jnp.float32
VMEM_LIMIT = 48 * 1024 * 1024


def partner(index, slot):
    return index ^ slot


def column_of(slot, size):
    return (slot & 1) * (size // 2) + (slot >> 1)


def permuted(block, axis, size, slot):
    return lax.ppermute(block, axis, [(i, partner(i, slot)) for i in range(size)])


def fetch_chips(block, axis, size):
    return [permuted(block, axis, size, slot) for slot in range(2, size, 2)]


def fetch_core(blocks, axis, size):
    return permuted(blocks, axis, size, 1)


def both_cores(blocks, axis, size):
    return jnp.concatenate([blocks, fetch_core(blocks, axis, size)])


def send_each(blocks, axis, size):
    return [permuted(blocks[slot], axis, size, slot) for slot in reversed(range(1, size))]


def call(kernel, out_shape, operands, specs=None, scratch=(), cost=None):
    vmem = pl.BlockSpec(memory_space=pltpu.VMEM)
    return pl.pallas_call(
        kernel,
        out_shape=out_shape,
        in_specs=specs or [vmem] * len(operands),
        out_specs=jax.tree.map(lambda _: vmem, out_shape),
        scratch_shapes=list(scratch),
        cost_estimate=cost,
        compiler_params=pltpu.CompilerParams(vmem_limit_bytes=VMEM_LIMIT),
    )(*operands)


def dot_nt(left, right):
    return lax.dot_general(left, right, (((1,), (1,)), ((), ())), preferred_element_type=F32)


def build_kernel(
    n_row, n_col, chunks,
    count, coords_hbm, mask_hbm, bias_hbm, tiles_hbm,
    dense_ref, mask_out_ref, bias_out_ref,
    coords, mask, bias, tile_buf, even, odd, wide, sems, small_sems,
):
    slots, block = tile_buf.shape[0], tile_buf.shape[1]
    per = slots // chunks
    small = [
        pltpu.make_async_copy(src, dst, small_sems.at[i])
        for i, (src, dst) in enumerate(
            [(coords_hbm, coords), (mask_hbm, mask), (bias_hbm, bias)]
        )
    ]
    copies = [
        pltpu.make_async_copy(
            tiles_hbm.at[pl.ds(i * per, per)], tile_buf.at[pl.ds(i * per, per)], sems.at[i]
        )
        for i in range(chunks)
    ]
    for copy in small + copies:
        copy.start()
    even[...] = jnp.zeros_like(even)
    odd[...] = jnp.zeros_like(odd)
    wide[...] = jnp.zeros_like(wide)
    for copy in small:
        copy.wait()
    row, col = lax.axis_index("row"), lax.axis_index("col")
    live = count[0, 0]
    mask_rows = jnp.broadcast_to(mask[...].astype(F32), (block, block))
    mask_out_ref[...] = mask_rows.T
    classes = bias.shape[1]
    wide[:, :classes] = jnp.broadcast_to(bias[...], (block, classes))
    bias_out_ref[...] = wide[...].T[:classes]

    def place(t):
        k, j = partner(coords[0, t], col), column_of(partner(coords[1, t], row), n_row)
        return jnp.where(t < live, k * n_row + j, n_row * n_col)

    for i in range(chunks):
        copies[i].wait()

        @pl.loop(0, per // 2, unroll=4)
        def _(pair):
            t = i * per + 2 * pair
            first, second = place(t), place(t + 1)
            even[first] += tile_buf[t].astype(F32)
            odd[second] += tile_buf[t + 1].astype(F32)

    for k in range(n_col):
        for j in range(n_row):
            at = k * n_row + j
            dense_ref[k * block : (k + 1) * block, j * block : (j + 1) * block] = (
                even[at] + odd[at]
            ).astype(BF16)


def join_rows_kernel(*refs):
    out = refs[-1]
    block = refs[0].shape[0]
    for i in range(out.shape[0] // block):
        out[i * block : (i + 1) * block, :] = refs[i][...]


def join_columns_kernel(*refs):
    out = refs[-1]
    block = refs[0].shape[1]
    for i in range(out.shape[1] // block):
        out[:, i * block : (i + 1) * block] = refs[i][...]


def layer_one_kernel(dense_ref, mine_ref, other_ref, *outputs):
    half, block = mine_ref.shape[0], dense_ref.shape[0] // len(outputs)
    for k, out in enumerate(outputs):
        rows = pl.ds(k * block, block)
        total = jnp.dot(dense_ref[rows, :half], mine_ref[...], preferred_element_type=F32)
        total += jnp.dot(dense_ref[rows, half:], other_ref[...], preferred_element_type=F32)
        out[...] = total.astype(BF16)


def hidden_kernel(n_col, *refs):
    parts = refs[:n_col]
    feat, w_one, b_one, w_two, mask, history, pushed_ref, proj_ref = refs[n_col:]
    total = feat[...].astype(F32)
    for part in parts:
        total += part[...].astype(F32)
    pre = jnp.dot(total.astype(BF16), w_one[...], preferred_element_type=F32) + b_one[...]
    hidden = jnp.maximum(pre, 0.0)
    chosen = jnp.concatenate([mask[...]] * (hidden.shape[1] // mask.shape[1]), axis=1) == 1.0
    pushed = jnp.where(chosen, hidden, history[...].astype(F32)).astype(BF16)
    pushed_ref[...] = pushed
    proj_ref[...] = dot_nt(w_two[...], pushed).astype(BF16)


def layer_two_kernel(dense_ref, mine_ref, other_ref, *outputs):
    half, block = mine_ref.shape[1], dense_ref.shape[0] // len(outputs)
    for k, out in enumerate(outputs):
        rows = pl.ds(k * block, block)
        total = dot_nt(mine_ref[...], dense_ref[rows, :half])
        total += dot_nt(other_ref[...], dense_ref[rows, half:])
        out[...] = total.astype(BF16)


def logits_kernel(n_col, *refs):
    parts = refs[:n_col]
    proj, bias, out = refs[n_col:]
    total = proj[...].astype(F32) + bias[...]
    for part in parts:
        total += part[...].astype(F32)
    out[...] = total


def tiles_kernel(
    n_row, n_col, transposed, coords_ref, count_ref, tiles_ref, stacked_ref, out_ref, total
):
    row, col = lax.axis_index("row"), lax.axis_index("col")
    total[...] = jnp.zeros_like(total)

    @pl.loop(0, count_ref[0, 0])
    def _(t):
        k = partner(coords_ref[0, t], col)
        j = column_of(partner(coords_ref[1, t], row), n_row)
        if transposed:
            total[k] += dot_nt(stacked_ref[j], tiles_ref[t])
        else:
            total[k] += jnp.dot(tiles_ref[t], stacked_ref[j], preferred_element_type=F32)

    out_ref[...] = total[...].astype(BF16)


def on_device(
    n_row, n_col,
    features, tiles, tile_coords, tile_count, batch_mask, history,
    weight_one, bias_one, weight_two, bias_two,
):
    feat, tile_set, hist = features[0, 0], tiles[0, 0], history[0, 0]
    coords = tile_coords[0, 0].T
    slots, block = tile_set.shape[0], tile_set.shape[1]
    f_in, hid, classes = feat.shape[1], weight_one.shape[1], weight_two.shape[1]
    w_two_t = weight_two.T
    dense_form = n_row * n_col <= slots
    places = n_row * n_col
    smem = pl.BlockSpec(memory_space=pltpu.SMEM)
    vmem = pl.BlockSpec(memory_space=pltpu.VMEM)
    shape = jax.ShapeDtypeStruct

    chips_one = [feat, *fetch_chips(feat, "row", n_row)]

    if dense_form:
        chunks = 8
        hbm = pl.BlockSpec(memory_space=pltpu.HBM)
        dense, mask_cols, bias_cols = call(
            functools.partial(build_kernel, n_row, n_col, chunks),
            (
                shape((n_col * block, n_row * block), BF16),
                shape((block, block), F32),
                shape((classes, block), F32),
            ),
            [tile_count]
            + [
                pltpu.with_memory_space_constraint(x, pltpu.HBM)
                for x in (coords, batch_mask[0], bias_two[None], tile_set)
            ],
            specs=[smem] + [hbm] * 4,
            scratch=[
                pltpu.SMEM((2, slots), jnp.int32),
                pltpu.VMEM((1, block), jnp.int32),
                pltpu.VMEM((1, classes), F32),
                pltpu.VMEM((slots, block, block), BF16),
                pltpu.VMEM((places + 1, block, block), F32),
                pltpu.VMEM((places + 1, block, block), F32),
                pltpu.VMEM((block, -(-classes // 128) * 128), F32),
                pltpu.SemaphoreType.DMA((chunks,)),
                pltpu.SemaphoreType.DMA((3,)),
            ],
            cost=pl.CostEstimate(
                flops=slots * block * block, bytes_accessed=2 * slots * block * block, transcendentals=0
            ),
        )
        anywhere = pl.BlockSpec(memory_space=pl.ANY)
        mine_one = call(
            join_rows_kernel,
            shape((n_row // 2 * block, f_in), BF16),
            (*chips_one, dense),
            specs=[vmem] * len(chips_one) + [anywhere],
        )
        other_one = fetch_core(mine_one, "row", n_row)
        parts_one = call(
            layer_one_kernel,
            [shape((block, f_in), BF16)] * n_col,
            (dense, mine_one, other_one),
        )
    else:
        mask_cols = jnp.broadcast_to(batch_mask[0, 0].astype(F32)[:, None], (block, block))
        bias_cols = jnp.broadcast_to(bias_two[:, None], (classes, block))
        summed = call(
            functools.partial(tiles_kernel, n_row, n_col, False),
            shape((n_col, block, f_in), BF16),
            (coords, tile_count, tile_set, both_cores(jnp.stack(chips_one), "row", n_row)),
            specs=[smem, smem, vmem, vmem],
            scratch=[pltpu.VMEM((n_col, block, f_in), F32)],
        )
        parts_one = [summed[k] for k in range(n_col)]

    arrived_one = send_each(parts_one, "col", n_col)
    pushed, proj = call(
        functools.partial(hidden_kernel, n_col),
        (shape((block, hid), BF16), shape((classes, block), BF16)),
        (parts_one[0], *arrived_one, feat, weight_one, bias_one[None], w_two_t, mask_cols, hist),
    )
    chips_two = [proj, *fetch_chips(proj, "row", n_row)]

    if dense_form:
        mine_two = call(
            join_columns_kernel, shape((classes, n_row // 2 * block), BF16), chips_two
        )
        other_two = fetch_core(mine_two, "row", n_row)
        parts_two = call(
            layer_two_kernel,
            [shape((classes, block), BF16)] * n_col,
            (dense, mine_two, other_two),
        )
    else:
        summed = call(
            functools.partial(tiles_kernel, n_row, n_col, True),
            shape((n_col, classes, block), BF16),
            (coords, tile_count, tile_set, both_cores(jnp.stack(chips_two), "row", n_row)),
            specs=[smem, smem, vmem, vmem],
            scratch=[pltpu.VMEM((n_col, classes, block), F32)],
        )
        parts_two = [summed[k] for k in range(n_col)]

    arrived_two = send_each(parts_two, "col", n_col)
    scores = call(
        functools.partial(logits_kernel, n_col),
        shape((classes, block), F32),
        (parts_two[0], *arrived_two, proj, bias_cols),
    )
    return pushed[None, None], scores.T[None, None]


def solution(mesh):
    sizes = mesh.shape
    return jax.shard_map(
        functools.partial(on_device, sizes["row"], sizes["col"]),
        mesh=mesh,
        in_specs=(
            P("row", "col", None, None),
            P("row", "col", None, None, None),
            P("row", "col", None, None),
            P("row", "col"),
            P("row", "col", None),
            P("row", "col", None, None),
            P(),
            P(),
            P(),
            P(),
        ),
        out_specs=(P("row", "col", None, None), P("row", "col", None, None)),
        check_vma=False,
    )
```

```python
import functools

import jax
import jax.numpy as jnp
from jax import lax
from jax.experimental import pallas as pl
from jax.experimental.pallas import tpu as pltpu
from jax.sharding import PartitionSpec as P

BF16 = jnp.bfloat16
F32 = jnp.float32
VMEM_LIMIT = 48 * 1024 * 1024


def partner(index, slot):
    return index ^ slot


def column_of(slot, size):
    return (slot & 1) * (size // 2) + (slot >> 1)


def permuted(block, axis, size, slot):
    return lax.ppermute(block, axis, [(i, partner(i, slot)) for i in range(size)])


def fetch_chips(block, axis, size):
    return [permuted(block, axis, size, slot) for slot in range(2, size, 2)]


def fetch_core(blocks, axis, size):
    return permuted(blocks, axis, size, 1)


def both_cores(blocks, axis, size):
    return jnp.concatenate([blocks, fetch_core(blocks, axis, size)])


def send_each(blocks, axis, size):
    return [permuted(blocks[slot], axis, size, slot) for slot in reversed(range(1, size))]


def call(kernel, out_shape, operands, specs=None, scratch=(), cost=None):
    vmem = pl.BlockSpec(memory_space=pltpu.VMEM)
    return pl.pallas_call(
        kernel,
        out_shape=out_shape,
        in_specs=specs or [vmem] * len(operands),
        out_specs=jax.tree.map(lambda _: vmem, out_shape),
        scratch_shapes=list(scratch),
        cost_estimate=cost,
        compiler_params=pltpu.CompilerParams(vmem_limit_bytes=VMEM_LIMIT),
    )(*operands)


def dot_nt(left, right):
    return lax.dot_general(left, right, (((1,), (1,)), ((), ())), preferred_element_type=F32)


def build_kernel(
    n_row, n_col, half, chunks,
    count, coords_hbm, tiles_hbm, *refs,
):
    dense_ref, coords, tile_buf, first, second, sems, coords_sem = refs[-7:]
    slots, rows, block = tile_buf.shape
    per, part = slots // chunks, rows // 2
    copies = [
        pltpu.make_async_copy(
            tiles_hbm.at[pl.ds(i * per, per), pl.ds(half * rows, rows)],
            tile_buf.at[pl.ds(i * per, per)],
            sems.at[i],
        )
        for i in range(chunks)
    ]
    coords_copy = pltpu.make_async_copy(coords_hbm, coords, coords_sem)
    coords_copy.start()
    for copy in copies:
        copy.start()
    row, col = lax.axis_index("row"), lax.axis_index("col")
    first[...] = jnp.zeros_like(first)
    second[...] = jnp.zeros_like(second)
    live = jnp.max(count[...])
    coords_copy.wait()

    def place(t):
        k, j = partner(coords[0, t], col), column_of(partner(coords[1, t], row), n_row)
        return jnp.where(t < live, k * n_row + j, n_row * n_col)

    for i in range(chunks):
        copies[i].wait()

        @pl.loop(0, per, unroll=8)
        def _(step):
            t = i * per + step
            at = place(t)
            first[at] += tile_buf[t, :part].astype(F32)
            second[at] += tile_buf[t, part:].astype(F32)

    for k in range(n_col):
        for j in range(n_row):
            at = k * n_row + j
            columns = slice(j * block, (j + 1) * block)
            dense_ref[k * rows : k * rows + part, columns] = first[at].astype(BF16)
            dense_ref[k * rows + part : (k + 1) * rows, columns] = second[at].astype(BF16)


def columns_kernel(mask, bias, mask_out, bias_out, wide):
    block, classes = mask_out.shape[0], bias.shape[1]
    mask_out[...] = jnp.broadcast_to(mask[...].astype(F32), (block, block)).T
    wide[...] = jnp.zeros_like(wide)
    wide[:, :classes] = jnp.broadcast_to(bias[...], (block, classes))
    bias_out[...] = wide[...].T[:classes]


def join_rows_kernel(*refs):
    out = refs[-1]
    block = refs[0].shape[0]
    for i in range(out.shape[0] // block):
        out[i * block : (i + 1) * block, :] = refs[i][...]


def join_columns_kernel(*refs):
    out = refs[-1]
    block = refs[0].shape[1]
    for i in range(out.shape[1] // block):
        out[:, i * block : (i + 1) * block] = refs[i][...]


def layer_one_kernel(upper_ref, lower_ref, mine_ref, other_ref, *outputs):
    half, rows = mine_ref.shape[0], upper_ref.shape[0] // len(outputs)
    for k, out in enumerate(outputs):
        at = pl.ds(k * rows, rows)
        for i, dense_ref in enumerate((upper_ref, lower_ref)):
            total = jnp.dot(dense_ref[at, :half], mine_ref[...], preferred_element_type=F32)
            total += jnp.dot(dense_ref[at, half:], other_ref[...], preferred_element_type=F32)
            out[i * rows : (i + 1) * rows, :] = total.astype(BF16)


def hidden_kernel(n_col, *refs):
    parts = refs[:n_col]
    feat, w_one, b_one, w_two, mask, history, pushed_ref, proj_ref = refs[n_col:]
    total = feat[...].astype(F32)
    for part in parts:
        total += part[...].astype(F32)
    pre = jnp.dot(total.astype(BF16), w_one[...], preferred_element_type=F32) + b_one[...]
    hidden = jnp.maximum(pre, 0.0)
    chosen = jnp.concatenate([mask[...]] * (hidden.shape[1] // mask.shape[1]), axis=1) == 1.0
    pushed = jnp.where(chosen, hidden, history[...].astype(F32)).astype(BF16)
    pushed_ref[...] = pushed
    proj_ref[...] = dot_nt(w_two[...], pushed).astype(BF16)


def layer_two_kernel(upper_ref, lower_ref, mine_ref, other_ref, *outputs):
    half, rows = mine_ref.shape[1], upper_ref.shape[0] // len(outputs)
    for k, out in enumerate(outputs):
        at = pl.ds(k * rows, rows)
        dense = jnp.concatenate([upper_ref[at, :], lower_ref[at, :]], axis=0)
        total = dot_nt(mine_ref[...], dense[:, :half])
        total += dot_nt(other_ref[...], dense[:, half:])
        out[...] = total.astype(BF16)


def logits_kernel(n_col, *refs):
    parts = refs[:n_col]
    proj, bias, out = refs[n_col:]
    total = proj[...].astype(F32) + bias[...]
    for part in parts:
        total += part[...].astype(F32)
    out[...] = total


def tiles_kernel(
    n_row, n_col, transposed, coords_ref, count_ref, tiles_ref, stacked_ref, out_ref, total
):
    row, col = lax.axis_index("row"), lax.axis_index("col")
    total[...] = jnp.zeros_like(total)

    @pl.loop(0, count_ref[0, 0])
    def _(t):
        k = partner(coords_ref[0, t], col)
        j = column_of(partner(coords_ref[1, t], row), n_row)
        if transposed:
            total[k] += dot_nt(stacked_ref[j], tiles_ref[t])
        else:
            total[k] += jnp.dot(tiles_ref[t], stacked_ref[j], preferred_element_type=F32)

    out_ref[...] = total[...].astype(BF16)


def on_device(
    n_row, n_col,
    features, tiles, tile_coords, tile_count, batch_mask, history,
    weight_one, bias_one, weight_two, bias_two,
):
    feat, tile_set, hist = features[0, 0], tiles[0, 0], history[0, 0]
    coords = tile_coords[0, 0].T
    slots, block = tile_set.shape[0], tile_set.shape[1]
    f_in, hid, classes = feat.shape[1], weight_one.shape[1], weight_two.shape[1]
    w_two_t = weight_two.T
    dense_form = n_row * n_col <= slots
    places = n_row * n_col
    smem = pl.BlockSpec(memory_space=pltpu.SMEM)
    vmem = pl.BlockSpec(memory_space=pltpu.VMEM)
    shape = jax.ShapeDtypeStruct

    chips_one = [feat, *fetch_chips(feat, "row", n_row)]

    if dense_form:
        hbm = pl.BlockSpec(memory_space=pltpu.HBM)
        anywhere = pl.BlockSpec(memory_space=pl.ANY)
        chunks, rows = 4, block // 2

        def build(half, *after):
            return call(
                functools.partial(build_kernel, n_row, n_col, half, chunks),
                shape((n_col * rows, n_row * block), BF16),
                (
                    tile_count,
                    pltpu.with_memory_space_constraint(coords, pltpu.HBM),
                    pltpu.with_memory_space_constraint(tile_set, pltpu.HBM),
                    *after,
                ),
                specs=[vmem, hbm, hbm] + [anywhere] * len(after),
                scratch=[
                    pltpu.SMEM((2, slots), jnp.int32),
                    pltpu.VMEM((slots, rows, block), BF16),
                    pltpu.VMEM((places + 1, rows // 2, block), F32),
                    pltpu.VMEM((places + 1, rows // 2, block), F32),
                    pltpu.SemaphoreType.DMA((chunks,)),
                    pltpu.SemaphoreType.DMA(()),
                ],
                cost=pl.CostEstimate(
                    flops=slots * rows * block,
                    bytes_accessed=2 * slots * rows * block,
                    transcendentals=0,
                ),
            )

        upper = build(0)
        mine_one = call(
            join_rows_kernel,
            shape((n_row // 2 * block, f_in), BF16),
            (*chips_one, upper),
            specs=[vmem] * len(chips_one) + [anywhere],
        )
        other_one = fetch_core(mine_one, "row", n_row)
        lower = build(1, mine_one)
        parts_one = call(
            layer_one_kernel,
            [shape((block, f_in), BF16)] * n_col,
            (upper, lower, mine_one, other_one),
        )
    else:
        summed = call(
            functools.partial(tiles_kernel, n_row, n_col, False),
            shape((n_col, block, f_in), BF16),
            (coords, tile_count, tile_set, both_cores(jnp.stack(chips_one), "row", n_row)),
            specs=[smem, smem, vmem, vmem],
            scratch=[pltpu.VMEM((n_col, block, f_in), F32)],
        )
        parts_one = [summed[k] for k in range(n_col)]

    arrived_one = send_each(parts_one, "col", n_col)
    mask_cols, bias_cols = call(
        columns_kernel,
        (shape((block, block), F32), shape((classes, block), F32)),
        (batch_mask[0], bias_two[None]),
        scratch=[pltpu.VMEM((block, -(-classes // 128) * 128), F32)],
    )
    pushed, proj = call(
        functools.partial(hidden_kernel, n_col),
        (shape((block, hid), BF16), shape((classes, block), BF16)),
        (parts_one[0], *arrived_one, feat, weight_one, bias_one[None], w_two_t, mask_cols, hist),
    )
    chips_two = [proj, *fetch_chips(proj, "row", n_row)]

    if dense_form:
        mine_two = call(
            join_columns_kernel, shape((classes, n_row // 2 * block), BF16), chips_two
        )
        other_two = fetch_core(mine_two, "row", n_row)
        parts_two = call(
            layer_two_kernel,
            [shape((classes, block), BF16)] * n_col,
            (upper, lower, mine_two, other_two),
        )
    else:
        summed = call(
            functools.partial(tiles_kernel, n_row, n_col, True),
            shape((n_col, classes, block), BF16),
            (coords, tile_count, tile_set, both_cores(jnp.stack(chips_two), "row", n_row)),
            specs=[smem, smem, vmem, vmem],
            scratch=[pltpu.VMEM((n_col, classes, block), F32)],
        )
        parts_two = [summed[k] for k in range(n_col)]

    arrived_two = send_each(parts_two, "col", n_col)
    scores = call(
        functools.partial(logits_kernel, n_col),
        shape((classes, block), F32),
        (parts_two[0], *arrived_two, proj, bias_cols),
    )
    return pushed[None, None], scores.T[None, None]


def solution(mesh):
    sizes = mesh.shape
    return jax.shard_map(
        functools.partial(on_device, sizes["row"], sizes["col"]),
        mesh=mesh,
        in_specs=(
            P("row", "col", None, None),
            P("row", "col", None, None, None),
            P("row", "col", None, None),
            P("row", "col"),
            P("row", "col", None),
            P("row", "col", None, None),
            P(),
            P(),
            P(),
            P(),
        ),
        out_specs=(P("row", "col", None, None), P("row", "col", None, None)),
        check_vma=False,
    )
```

```python
import functools

import jax
import jax.numpy as jnp
from jax import lax
from jax.experimental import pallas as pl
from jax.experimental.pallas import tpu as pltpu
from jax.sharding import PartitionSpec as P

BF16 = jnp.bfloat16
F32 = jnp.float32
VMEM_LIMIT = 48 * 1024 * 1024


def partner(index, slot):
    return index ^ slot


def column_of(slot, size):
    return (slot & 1) * (size // 2) + (slot >> 1)


def permuted(block, axis, size, slot):
    return lax.ppermute(block, axis, [(i, partner(i, slot)) for i in range(size)])


def fetch_chips(block, axis, size):
    return [permuted(block, axis, size, slot) for slot in range(2, size, 2)]


def fetch_core(blocks, axis, size):
    return permuted(blocks, axis, size, 1)


def both_cores(blocks, axis, size):
    return jnp.concatenate([blocks, fetch_core(blocks, axis, size)])


def send_plan(size):
    if size == 4:
        return [
            [(1, 2), (2, 1)],
            [(1, 3), (2, 0)],
            [(0, 3), (3, 0)],
            [(0, 1), (3, 2)],
            [(0, 2), (3, 1), (1, 0), (2, 3)],
        ]
    return [[(i, partner(i, slot)) for i in range(size)] for slot in reversed(range(1, size))]


def slot_table(pairs, size):
    table = [0] * size
    for source, target in pairs:
        table[source] = source ^ target
    return table


def send_blocks(blocks, axis, size):
    return [lax.ppermute(x, axis, pairs) for x, pairs in zip(blocks, send_plan(size))]


def sent_slot(plan_pairs, index, size):
    slot = 0
    for i, value in enumerate(slot_table(plan_pairs, size)):
        slot = jnp.where(index == i, value, slot)
    return slot


def call(kernel, out_shape, operands, specs=None, scratch=(), cost=None):
    vmem = pl.BlockSpec(memory_space=pltpu.VMEM)
    return pl.pallas_call(
        kernel,
        out_shape=out_shape,
        in_specs=specs or [vmem] * len(operands),
        out_specs=jax.tree.map(lambda _: vmem, out_shape),
        scratch_shapes=list(scratch),
        cost_estimate=cost,
        compiler_params=pltpu.CompilerParams(vmem_limit_bytes=VMEM_LIMIT),
    )(*operands)


def dot_nt(left, right):
    return lax.dot_general(left, right, (((1,), (1,)), ((), ())), preferred_element_type=F32)


def build_kernel(n_row, n_col, chunks, places_any, tiles_hbm, *refs):
    dense_ref, places, tiles, first, second, sems, places_sem = refs[-7:]
    slots, block = tiles.shape[0], tiles.shape[1]
    per, part = slots // chunks, block // 2
    copies = [
        pltpu.make_async_copy(
            tiles_hbm.at[pl.ds(i * per, per)], tiles.at[pl.ds(i * per, per)], sems.at[i]
        )
        for i in range(chunks)
    ]
    places_copy = pltpu.make_async_copy(places_any, places, places_sem)
    places_copy.start()
    for copy in copies:
        copy.start()
    first[...] = jnp.zeros_like(first)
    second[...] = jnp.zeros_like(second)
    places_copy.wait()

    for i in range(chunks):
        copies[i].wait()

        @pl.loop(0, per, unroll=8)
        def _(step):
            t = i * per + step
            at = places[0, t]
            first[at] += tiles[t, :part].astype(F32)
            second[at] += tiles[t, part:].astype(F32)

    for k in range(n_col):
        for j in range(n_row):
            at = k * n_row + j
            columns = slice(j * block, (j + 1) * block)
            dense_ref[k * block : k * block + part, columns] = first[at].astype(BF16)
            dense_ref[k * block + part : (k + 1) * block, columns] = second[at].astype(BF16)


def prepare_kernel(
    n_row, n_col,
    count, coords_hbm, mask_hbm, bias_hbm, feat_hbm,
    places_out, mask_out, bias_out, feat_out,
    coords, mask, bias, wide, sems,
):
    pairs = [(coords_hbm, coords), (mask_hbm, mask), (bias_hbm, bias), (feat_hbm, feat_out)]
    copies = [
        pltpu.make_async_copy(src, dst, sems.at[i]) for i, (src, dst) in enumerate(pairs)
    ]
    for copy in copies:
        copy.start()
    wide[...] = jnp.zeros_like(wide)
    for copy in copies:
        copy.wait()
    row, col = lax.axis_index("row"), lax.axis_index("col")
    k = partner(coords[0:1, :], col)
    j = column_of(partner(coords[1:2, :], row), n_row)
    slot = lax.broadcasted_iota(jnp.int32, k.shape, 1)
    places_out[...] = jnp.where(slot < count[0, 0], k * n_row + j, n_row * n_col)
    block, classes = mask_out.shape[0], bias.shape[1]
    mask_out[...] = jnp.broadcast_to(mask[...].astype(F32), (block, block)).T
    wide[:, :classes] = jnp.broadcast_to(bias[...], (block, classes))
    bias_out[...] = wide[...].T[:classes]


def join_rows_kernel(*refs):
    out = refs[-1]
    block = refs[0].shape[0]
    for i in range(out.shape[0] // block):
        out[i * block : (i + 1) * block, :] = refs[i][...]


def join_columns_kernel(*refs):
    out = refs[-1]
    block = refs[0].shape[1]
    for i in range(out.shape[1] // block):
        out[:, i * block : (i + 1) * block] = refs[i][...]


def store_sent(n_col, outputs, part):
    col = lax.axis_index("col")
    outputs[0][...] = part(0)
    for out, pairs in zip(outputs[1:], send_plan(n_col)):
        out[...] = part(sent_slot(pairs, col, n_col))


def layer_one_kernel(n_col, dense_ref, mine_ref, other_ref, *refs):
    outputs, scratch = refs[:-1], refs[-1]
    half, block = mine_ref.shape[0], dense_ref.shape[0] // n_col
    for k in range(n_col):
        rows = pl.ds(k * block, block)
        total = jnp.dot(dense_ref[rows, :half], mine_ref[...], preferred_element_type=F32)
        total += jnp.dot(dense_ref[rows, half:], other_ref[...], preferred_element_type=F32)
        scratch[k] = total.astype(BF16)
    store_sent(n_col, outputs, lambda k: scratch[k])


def hidden_kernel(sends, *refs):
    parts = refs[:sends]
    feat, w_one, b_one, w_two, mask, history, pushed_ref, proj_ref = refs[sends:]
    total = feat[...].astype(F32)
    for part in parts:
        total += part[...].astype(F32)
    pre = jnp.dot(total.astype(BF16), w_one[...], preferred_element_type=F32) + b_one[...]
    hidden = jnp.maximum(pre, 0.0)
    chosen = jnp.concatenate([mask[...]] * (hidden.shape[1] // mask.shape[1]), axis=1) == 1.0
    pushed = jnp.where(chosen, hidden, history[...].astype(F32)).astype(BF16)
    pushed_ref[...] = pushed
    proj_ref[...] = dot_nt(w_two[...], pushed).astype(BF16)


def layer_two_kernel(n_col, dense_ref, mine_ref, other_ref, *refs):
    outputs, scratch = refs[:-1], refs[-1]
    half, block = mine_ref.shape[1], dense_ref.shape[0] // n_col
    for k in range(n_col):
        rows = pl.ds(k * block, block)
        total = dot_nt(mine_ref[...], dense_ref[rows, :half])
        total += dot_nt(other_ref[...], dense_ref[rows, half:])
        scratch[k] = total.astype(BF16)
    store_sent(n_col, outputs, lambda k: scratch[k])


def logits_kernel(sends, *refs):
    parts = refs[:sends]
    proj, bias, out = refs[sends:]
    total = proj[...].astype(F32) + bias[...]
    for part in parts:
        total += part[...].astype(F32)
    out[...] = total


def tiles_kernel(
    n_row, n_col, transposed, coords_ref, count_ref, tiles_ref, stacked_ref, out_ref, total
):
    row, col = lax.axis_index("row"), lax.axis_index("col")
    total[...] = jnp.zeros_like(total)

    @pl.loop(0, count_ref[0, 0])
    def _(t):
        k = partner(coords_ref[0, t], col)
        j = column_of(partner(coords_ref[1, t], row), n_row)
        if transposed:
            total[k] += dot_nt(stacked_ref[j], tiles_ref[t])
        else:
            total[k] += jnp.dot(tiles_ref[t], stacked_ref[j], preferred_element_type=F32)

    out_ref[...] = total[...].astype(BF16)


def pick_sent(summed, n_col):
    col = lax.axis_index("col")
    slots = [sent_slot(pairs, col, n_col) for pairs in send_plan(n_col)]
    return [summed[0]] + [lax.dynamic_index_in_dim(summed, k, 0, keepdims=False) for k in slots]


def on_device(
    n_row, n_col,
    features, tiles, tile_coords, tile_count, batch_mask, history,
    weight_one, bias_one, weight_two, bias_two,
):
    feat, tile_set, hist = features[0, 0], tiles[0, 0], history[0, 0]
    coords = tile_coords[0, 0].T
    slots, block = tile_set.shape[0], tile_set.shape[1]
    f_in, hid, classes = feat.shape[1], weight_one.shape[1], weight_two.shape[1]
    w_two_t = weight_two.T
    dense_form = n_row * n_col <= slots
    sends = 1 + len(send_plan(n_col))
    smem = pl.BlockSpec(memory_space=pltpu.SMEM)
    vmem = pl.BlockSpec(memory_space=pltpu.VMEM)
    hbm = pl.BlockSpec(memory_space=pltpu.HBM)
    shape = jax.ShapeDtypeStruct

    in_hbm = lambda x: pltpu.with_memory_space_constraint(x, pltpu.HBM)
    places, mask_cols, bias_cols, feat_near = call(
        functools.partial(prepare_kernel, n_row, n_col),
        (
            shape((1, slots), jnp.int32),
            shape((block, block), F32),
            shape((classes, block), F32),
            shape((block, f_in), BF16),
        ),
        (tile_count, *map(in_hbm, (coords, batch_mask[0], bias_two[None], feat))),
        specs=[smem, hbm, hbm, hbm, hbm],
        scratch=[
            pltpu.VMEM((2, slots), jnp.int32),
            pltpu.VMEM((1, block), jnp.int32),
            pltpu.VMEM((1, classes), F32),
            pltpu.VMEM((block, -(-classes // 128) * 128), F32),
            pltpu.SemaphoreType.DMA((4,)),
        ],
    )
    chips_one = [feat_near, *fetch_chips(feat, "row", n_row)]

    if dense_form:
        anywhere = pl.BlockSpec(memory_space=pl.ANY)
        chunks = 8
        mine_one = call(
            join_rows_kernel,
            shape((n_row // 2 * block, f_in), BF16),
            (*chips_one, places),
            specs=[vmem] * len(chips_one) + [anywhere],
        )
        other_one = fetch_core(mine_one, "row", n_row)
        dense = call(
            functools.partial(build_kernel, n_row, n_col, chunks),
            shape((n_col * block, n_row * block), BF16),
            (places, in_hbm(tile_set), mine_one),
            specs=[anywhere, hbm, anywhere],
            scratch=[
                pltpu.SMEM((1, slots), jnp.int32),
                pltpu.VMEM((slots, block, block), BF16),
                pltpu.VMEM((n_row * n_col + 1, block // 2, block), F32),
                pltpu.VMEM((n_row * n_col + 1, block // 2, block), F32),
                pltpu.SemaphoreType.DMA((chunks,)),
                pltpu.SemaphoreType.DMA(()),
            ],
            cost=pl.CostEstimate(
                flops=slots * block * block,
                bytes_accessed=2 * slots * block * block,
                transcendentals=0,
            ),
        )
        parts_one = call(
            functools.partial(layer_one_kernel, n_col),
            [shape((block, f_in), BF16)] * sends,
            (dense, mine_one, other_one),
            scratch=[pltpu.VMEM((n_col, block, f_in), BF16)],
        )
    else:
        summed = call(
            functools.partial(tiles_kernel, n_row, n_col, False),
            shape((n_col, block, f_in), BF16),
            (coords, tile_count, tile_set, both_cores(jnp.stack(chips_one), "row", n_row)),
            specs=[smem, smem, vmem, vmem],
            scratch=[pltpu.VMEM((n_col, block, f_in), F32)],
        )
        parts_one = pick_sent(summed, n_col)

    arrived_one = send_blocks(parts_one[1:], "col", n_col)
    pushed, proj = call(
        functools.partial(hidden_kernel, sends),
        (shape((block, hid), BF16), shape((classes, block), BF16)),
        (parts_one[0], *arrived_one, feat_near, weight_one, bias_one[None], w_two_t, mask_cols, hist),
    )
    chips_two = [proj, *fetch_chips(proj, "row", n_row)]

    if dense_form:
        mine_two = call(
            join_columns_kernel, shape((classes, n_row // 2 * block), BF16), chips_two
        )
        other_two = fetch_core(mine_two, "row", n_row)
        parts_two = call(
            functools.partial(layer_two_kernel, n_col),
            [shape((classes, block), BF16)] * sends,
            (dense, mine_two, other_two),
            scratch=[pltpu.VMEM((n_col, classes, block), BF16)],
        )
    else:
        summed = call(
            functools.partial(tiles_kernel, n_row, n_col, True),
            shape((n_col, classes, block), BF16),
            (coords, tile_count, tile_set, both_cores(jnp.stack(chips_two), "row", n_row)),
            specs=[smem, smem, vmem, vmem],
            scratch=[pltpu.VMEM((n_col, classes, block), F32)],
        )
        parts_two = pick_sent(summed, n_col)

    arrived_two = send_blocks(parts_two[1:], "col", n_col)
    scores = call(
        functools.partial(logits_kernel, sends),
        shape((classes, block), F32),
        (parts_two[0], *arrived_two, proj, bias_cols),
    )
    return pushed[None, None], scores.T[None, None]


def solution(mesh):
    sizes = mesh.shape
    return jax.shard_map(
        functools.partial(on_device, sizes["row"], sizes["col"]),
        mesh=mesh,
        in_specs=(
            P("row", "col", None, None),
            P("row", "col", None, None, None),
            P("row", "col", None, None),
            P("row", "col"),
            P("row", "col", None),
            P("row", "col", None, None),
            P(),
            P(),
            P(),
            P(),
        ),
        out_specs=(P("row", "col", None, None), P("row", "col", None, None)),
        check_vma=False,
    )
```

```python
import functools

import jax
import jax.numpy as jnp
from jax import lax
from jax.experimental import pallas as pl
from jax.experimental.pallas import tpu as pltpu
from jax.sharding import PartitionSpec as P

BF16 = jnp.bfloat16
F32 = jnp.float32
VMEM_LIMIT = 48 * 1024 * 1024


def partner(index, slot):
    return index ^ slot


def column_of(slot, size):
    return (slot & 1) * (size // 2) + (slot >> 1)


def permuted(block, axis, size, slot):
    return lax.ppermute(block, axis, [(i, partner(i, slot)) for i in range(size)])


def fetch_chips(block, axis, size):
    return [permuted(block, axis, size, slot) for slot in range(2, size, 2)]


def gather_chips(block, axis, size):
    groups = [list(range(core, size, 2)) for core in range(2)]
    return lax.all_gather(block, axis, axis_index_groups=groups)


def fetch_core(blocks, axis, size):
    return permuted(blocks, axis, size, 1)


def by_slot(held):
    chip = lax.axis_index("row") >> 1
    return jnp.take(held, partner(chip, jnp.arange(held.shape[0])), axis=0)


def both_cores(blocks, axis, size):
    return jnp.concatenate([blocks, fetch_core(blocks, axis, size)])


def send_each(blocks, axis, size):
    return [permuted(blocks[slot], axis, size, slot) for slot in reversed(range(1, size))]


def call(kernel, out_shape, operands, specs=None, scratch=(), cost=None):
    vmem = pl.BlockSpec(memory_space=pltpu.VMEM)
    return pl.pallas_call(
        kernel,
        out_shape=out_shape,
        in_specs=specs or [vmem] * len(operands),
        out_specs=jax.tree.map(lambda _: vmem, out_shape),
        scratch_shapes=list(scratch),
        cost_estimate=cost,
        compiler_params=pltpu.CompilerParams(vmem_limit_bytes=VMEM_LIMIT),
    )(*operands)


def dot_nt(left, right):
    return lax.dot_general(left, right, (((1,), (1,)), ((), ())), preferred_element_type=F32)


def build_kernel(
    n_row, n_col, chunks, count, coords_hbm, tiles_hbm, dense_ref, coords, tiles, first, second, sems, coords_sem
):
    slots, block = tiles.shape[0], tiles.shape[1]
    per, part = slots // chunks, block // 2
    copies = [
        pltpu.make_async_copy(
            tiles_hbm.at[pl.ds(i * per, per)], tiles.at[pl.ds(i * per, per)], sems.at[i]
        )
        for i in range(chunks)
    ]
    coords_copy = pltpu.make_async_copy(coords_hbm, coords, coords_sem)
    coords_copy.start()
    for copy in copies:
        copy.start()
    row, col = lax.axis_index("row"), lax.axis_index("col")
    live = count[0, 0]
    first[...] = jnp.zeros_like(first)
    second[...] = jnp.zeros_like(second)
    coords_copy.wait()

    def place(t):
        k, j = partner(coords[0, t], col), column_of(partner(coords[1, t], row), n_row)
        return jnp.where(t < live, k * n_row + j, n_row * n_col)

    for i in range(chunks):
        copies[i].wait()

        @pl.loop(0, per, unroll=8)
        def _(step):
            t = i * per + step
            at = place(t)
            first[at] += tiles[t, :part].astype(F32)
            second[at] += tiles[t, part:].astype(F32)

    for k in range(n_col):
        for j in range(n_row):
            at = k * n_row + j
            columns = slice(j * block, (j + 1) * block)
            dense_ref[k * block : k * block + part, columns] = first[at].astype(BF16)
            dense_ref[k * block + part : (k + 1) * block, columns] = second[at].astype(BF16)


def prepare_ordered_kernel(mask, bias, *refs):
    mask_out, bias_out, wide = refs[-3:]
    block, classes = mask_out.shape[0], bias.shape[1]
    wide[...] = jnp.zeros_like(wide)
    mask_out[...] = jnp.broadcast_to(mask[...].astype(F32), (block, block)).T
    wide[:, :classes] = jnp.broadcast_to(bias[...], (block, classes))
    bias_out[...] = wide[...].T[:classes]


def join_rows_kernel(*refs):
    out = refs[-1]
    block = refs[0].shape[0]
    for i in range(out.shape[0] // block):
        out[i * block : (i + 1) * block, :] = refs[i][...]


def join_columns_kernel(held, out):
    chips, _, block = held.shape
    chip = lax.axis_index("row") >> 1
    for i in range(chips):
        out[:, i * block : (i + 1) * block] = held[partner(chip, i)]


def layer_one_kernel(dense_ref, mine_ref, other_ref, *outputs):
    half, block = mine_ref.shape[0], dense_ref.shape[0] // len(outputs)
    for k, out in enumerate(outputs):
        rows = pl.ds(k * block, block)
        total = jnp.dot(dense_ref[rows, :half], mine_ref[...], preferred_element_type=F32)
        total += jnp.dot(dense_ref[rows, half:], other_ref[...], preferred_element_type=F32)
        out[...] = total.astype(BF16)


def hidden_kernel(sends, *refs):
    parts = refs[:sends]
    feat, w_one, b_one, w_two, mask, history, pushed_ref, proj_ref = refs[sends:]
    total = feat[...].astype(F32)
    for part in parts:
        total += part[...].astype(F32)
    pre = jnp.dot(total.astype(BF16), w_one[...], preferred_element_type=F32) + b_one[...]
    hidden = jnp.maximum(pre, 0.0)
    chosen = jnp.concatenate([mask[...]] * (hidden.shape[1] // mask.shape[1]), axis=1) == 1.0
    pushed = jnp.where(chosen, hidden, history[...].astype(F32)).astype(BF16)
    pushed_ref[...] = pushed
    proj_ref[...] = dot_nt(w_two[...], pushed).astype(BF16)


def layer_two_kernel(dense_ref, mine_ref, other_ref, *outputs):
    half, block = mine_ref.shape[1], dense_ref.shape[0] // len(outputs)
    for k, out in enumerate(outputs):
        rows = pl.ds(k * block, block)
        total = dot_nt(mine_ref[...], dense_ref[rows, :half])
        total += dot_nt(other_ref[...], dense_ref[rows, half:])
        out[...] = total.astype(BF16)


def logits_kernel(sends, *refs):
    parts = refs[:sends]
    proj, bias, out = refs[sends:]
    total = proj[...].astype(F32) + bias[...]
    for part in parts:
        total += part[...].astype(F32)
    out[...] = total


def tiles_kernel(
    n_row, n_col, transposed, coords_ref, count_ref, tiles_ref, stacked_ref, out_ref, total
):
    row, col = lax.axis_index("row"), lax.axis_index("col")
    total[...] = jnp.zeros_like(total)

    @pl.loop(0, count_ref[0, 0])
    def _(t):
        k = partner(coords_ref[0, t], col)
        j = column_of(partner(coords_ref[1, t], row), n_row)
        if transposed:
            total[k] += dot_nt(stacked_ref[j], tiles_ref[t])
        else:
            total[k] += jnp.dot(tiles_ref[t], stacked_ref[j], preferred_element_type=F32)

    out_ref[...] = total[...].astype(BF16)


def on_device(
    n_row, n_col,
    features, tiles, tile_coords, tile_count, batch_mask, history,
    weight_one, bias_one, weight_two, bias_two,
):
    feat, tile_set, hist = features[0, 0], tiles[0, 0], history[0, 0]
    coords = tile_coords[0, 0].T
    slots, block = tile_set.shape[0], tile_set.shape[1]
    f_in, hid, classes = feat.shape[1], weight_one.shape[1], weight_two.shape[1]
    w_two_t = weight_two.T
    dense_form = n_row * n_col <= slots
    smem = pl.BlockSpec(memory_space=pltpu.SMEM)
    vmem = pl.BlockSpec(memory_space=pltpu.VMEM)
    hbm = pl.BlockSpec(memory_space=pltpu.HBM)
    shape = jax.ShapeDtypeStruct

    def prepare(*after):
        return call(
            prepare_ordered_kernel,
            (shape((block, block), F32), shape((classes, block), F32)),
            (batch_mask[0], bias_two[None], *after),
            specs=[vmem] * 2 + [pl.BlockSpec(memory_space=pl.ANY)] * len(after),
            scratch=[pltpu.VMEM((block, -(-classes // 128) * 128), F32)],
        )

    chips_one = [feat, *fetch_chips(feat, "row", n_row)]

    if dense_form:
        anywhere = pl.BlockSpec(memory_space=pl.ANY)
        chunks = 8
        dense = call(
            functools.partial(build_kernel, n_row, n_col, chunks),
            shape((n_col * block, n_row * block), BF16),
            (
                tile_count,
                pltpu.with_memory_space_constraint(coords, pltpu.HBM),
                pltpu.with_memory_space_constraint(tile_set, pltpu.HBM),
            ),
            specs=[smem, hbm, hbm],
            scratch=[
                pltpu.SMEM((2, slots), jnp.int32),
                pltpu.VMEM((slots, block, block), BF16),
                pltpu.VMEM((n_row * n_col + 1, block // 2, block), F32),
                pltpu.VMEM((n_row * n_col + 1, block // 2, block), F32),
                pltpu.SemaphoreType.DMA((chunks,)),
                pltpu.SemaphoreType.DMA(()),
            ],
            cost=pl.CostEstimate(
                flops=slots * block * block,
                bytes_accessed=2 * slots * block * block,
                transcendentals=0,
            ),
        )
        mine_one = call(
            join_rows_kernel,
            shape((n_row // 2 * block, f_in), BF16),
            (*chips_one, dense),
            specs=[vmem] * len(chips_one) + [anywhere],
        )
        other_one = fetch_core(mine_one, "row", n_row)
        mask_cols, bias_cols = prepare(mine_one)
        parts_one = call(
            layer_one_kernel,
            [shape((block, f_in), BF16)] * n_col,
            (dense, mine_one, other_one),
        )
    else:
        mask_cols, bias_cols = prepare()
        summed = call(
            functools.partial(tiles_kernel, n_row, n_col, False),
            shape((n_col, block, f_in), BF16),
            (coords, tile_count, tile_set, both_cores(jnp.stack(chips_one), "row", n_row)),
            specs=[smem, smem, vmem, vmem],
            scratch=[pltpu.VMEM((n_col, block, f_in), F32)],
        )
        parts_one = [summed[k] for k in range(n_col)]

    arrived_one = send_each(parts_one, "col", n_col)
    pushed, proj = call(
        functools.partial(hidden_kernel, n_col),
        (shape((block, hid), BF16), shape((classes, block), BF16)),
        (parts_one[0], *arrived_one, feat, weight_one, bias_one[None], w_two_t, mask_cols, hist),
    )
    chips_two = gather_chips(proj, "row", n_row)

    if dense_form:
        mine_two = call(
            join_columns_kernel, shape((classes, n_row // 2 * block), BF16), (chips_two,)
        )
        other_two = fetch_core(mine_two, "row", n_row)
        parts_two = call(
            layer_two_kernel,
            [shape((classes, block), BF16)] * n_col,
            (dense, mine_two, other_two),
        )
    else:
        summed = call(
            functools.partial(tiles_kernel, n_row, n_col, True),
            shape((n_col, classes, block), BF16),
            (coords, tile_count, tile_set, both_cores(by_slot(chips_two), "row", n_row)),
            specs=[smem, smem, vmem, vmem],
            scratch=[pltpu.VMEM((n_col, classes, block), F32)],
        )
        parts_two = [summed[k] for k in range(n_col)]

    arrived_two = send_each(parts_two, "col", n_col)
    scores = call(
        functools.partial(logits_kernel, n_col),
        shape((classes, block), F32),
        (parts_two[0], *arrived_two, proj, bias_cols),
    )
    return pushed[None, None], scores.T[None, None]


def solution(mesh):
    sizes = mesh.shape
    return jax.shard_map(
        functools.partial(on_device, sizes["row"], sizes["col"]),
        mesh=mesh,
        in_specs=(
            P("row", "col", None, None),
            P("row", "col", None, None, None),
            P("row", "col", None, None),
            P("row", "col"),
            P("row", "col", None),
            P("row", "col", None, None),
            P(),
            P(),
            P(),
            P(),
        ),
        out_specs=(P("row", "col", None, None), P("row", "col", None, None)),
        check_vma=False,
    )
```

```python
import functools

import jax
import jax.numpy as jnp
from jax import lax
from jax.experimental import pallas as pl
from jax.experimental.pallas import tpu as pltpu
from jax.sharding import PartitionSpec as P

BF16 = jnp.bfloat16
F32 = jnp.float32
VMEM_LIMIT = 48 * 1024 * 1024


def partner(index, slot):
    return index ^ slot


def column_of(slot, size):
    return (slot & 1) * (size // 2) + (slot >> 1)


def permuted(block, axis, size, slot):
    return lax.ppermute(block, axis, [(i, partner(i, slot)) for i in range(size)])


def fetch_chips(block, axis, size):
    return [permuted(block, axis, size, slot) for slot in range(2, size, 2)]


def fetch_core(blocks, axis, size):
    return permuted(blocks, axis, size, 1)


def both_cores(blocks, axis, size):
    return jnp.concatenate([blocks, fetch_core(blocks, axis, size)])


def send_each(blocks, axis, size):
    return [permuted(blocks[slot], axis, size, slot) for slot in reversed(range(1, size))]


def call(kernel, out_shape, operands, specs=None, scratch=(), cost=None):
    vmem = pl.BlockSpec(memory_space=pltpu.VMEM)
    return pl.pallas_call(
        kernel,
        out_shape=out_shape,
        in_specs=specs or [vmem] * len(operands),
        out_specs=jax.tree.map(lambda _: vmem, out_shape),
        scratch_shapes=list(scratch),
        cost_estimate=cost,
        compiler_params=pltpu.CompilerParams(vmem_limit_bytes=VMEM_LIMIT),
    )(*operands)


def dot_nt(left, right):
    return lax.dot_general(left, right, (((1,), (1,)), ((), ())), preferred_element_type=F32)


def build_kernel(
    n_row, n_col, chunks, count, coords_hbm, tiles_hbm, dense_ref, coords, tiles, first, second, sems, coords_sem
):
    slots, block = tiles.shape[0], tiles.shape[1]
    per, part = slots // chunks, block // 2
    copies = [
        pltpu.make_async_copy(
            tiles_hbm.at[pl.ds(i * per, per)], tiles.at[pl.ds(i * per, per)], sems.at[i]
        )
        for i in range(chunks)
    ]
    coords_copy = pltpu.make_async_copy(coords_hbm, coords, coords_sem)
    coords_copy.start()
    for copy in copies:
        copy.start()
    row, col = lax.axis_index("row"), lax.axis_index("col")
    live = count[0, 0]
    first[...] = jnp.zeros_like(first)
    second[...] = jnp.zeros_like(second)
    coords_copy.wait()

    def place(t):
        k, j = partner(coords[0, t], col), column_of(partner(coords[1, t], row), n_row)
        return jnp.where(t < live, k * n_row + j, n_row * n_col)

    for i in range(chunks):
        copies[i].wait()

        @pl.loop(0, per, unroll=8)
        def _(step):
            t = i * per + step
            at = place(t)
            first[at] += tiles[t, :part].astype(F32)
            second[at] += tiles[t, part:].astype(F32)

    for k in range(n_col):
        for j in range(n_row):
            at = k * n_row + j
            columns = slice(j * block, (j + 1) * block)
            dense_ref[k * block : k * block + part, columns] = first[at].astype(BF16)
            dense_ref[k * block + part : (k + 1) * block, columns] = second[at].astype(BF16)


def prepare_ordered_kernel(mask, bias, *refs):
    mask_out, bias_out, wide = refs[-3:]
    block, classes = mask_out.shape[0], bias.shape[1]
    wide[...] = jnp.zeros_like(wide)
    mask_out[...] = jnp.broadcast_to(mask[...].astype(F32), (block, block)).T
    wide[:, :classes] = jnp.broadcast_to(bias[...], (block, classes))
    bias_out[...] = wide[...].T[:classes]


def join_rows_kernel(*refs):
    out = refs[-1]
    block = refs[0].shape[0]
    for i in range(out.shape[0] // block):
        out[i * block : (i + 1) * block, :] = refs[i][...]


def join_columns_kernel(*refs):
    out = refs[-1]
    block = refs[0].shape[1]
    for i in range(out.shape[1] // block):
        out[:, i * block : (i + 1) * block] = refs[i][...]


def half_one_kernel(dense_ref, mine_ref, out):
    half = mine_ref.shape[0]
    out[...] = jnp.dot(dense_ref[:, :half], mine_ref[...], preferred_element_type=F32)


def layer_one_kernel(dense_ref, first_ref, other_ref, *outputs):
    half, block = other_ref.shape[0], dense_ref.shape[0] // len(outputs)
    for k, out in enumerate(outputs):
        rows = pl.ds(k * block, block)
        total = jnp.dot(dense_ref[rows, half:], other_ref[...], preferred_element_type=F32)
        out[...] = (first_ref[rows, :] + total).astype(BF16)


def hidden_kernel(sends, *refs):
    parts = refs[:sends]
    feat, w_one, b_one, w_two, mask, history, pushed_ref, proj_ref = refs[sends:]
    total = feat[...].astype(F32)
    for part in parts:
        total += part[...].astype(F32)
    pre = jnp.dot(total.astype(BF16), w_one[...], preferred_element_type=F32) + b_one[...]
    hidden = jnp.maximum(pre, 0.0)
    chosen = jnp.concatenate([mask[...]] * (hidden.shape[1] // mask.shape[1]), axis=1) == 1.0
    pushed = jnp.where(chosen, hidden, history[...].astype(F32)).astype(BF16)
    pushed_ref[...] = pushed
    proj_ref[...] = dot_nt(w_two[...], pushed).astype(BF16)


def write_kernel(value, out):
    out[...] = value[...]


def half_two_kernel(dense_ref, mine_ref, out):
    half = mine_ref.shape[1]
    out[...] = dot_nt(mine_ref[...], dense_ref[:, :half])


def layer_two_kernel(dense_ref, first_ref, other_ref, *outputs):
    half, block = other_ref.shape[1], dense_ref.shape[0] // len(outputs)
    for k, out in enumerate(outputs):
        rows = pl.ds(k * block, block)
        total = dot_nt(other_ref[...], dense_ref[rows, half:])
        out[...] = (first_ref[:, rows] + total).astype(BF16)


def logits_kernel(sends, *refs):
    parts = refs[:sends]
    proj, bias, out = refs[sends:]
    total = proj[...].astype(F32) + bias[...]
    for part in parts:
        total += part[...].astype(F32)
    out[:, 0, :] = total


def tiles_kernel(
    n_row, n_col, transposed, coords_ref, count_ref, tiles_ref, stacked_ref, out_ref, total
):
    row, col = lax.axis_index("row"), lax.axis_index("col")
    total[...] = jnp.zeros_like(total)

    @pl.loop(0, count_ref[0, 0])
    def _(t):
        k = partner(coords_ref[0, t], col)
        j = column_of(partner(coords_ref[1, t], row), n_row)
        if transposed:
            total[k] += dot_nt(stacked_ref[j], tiles_ref[t])
        else:
            total[k] += jnp.dot(tiles_ref[t], stacked_ref[j], preferred_element_type=F32)

    out_ref[...] = total[...].astype(BF16)


def on_device(
    n_row, n_col,
    features, tiles, tile_coords, tile_count, batch_mask, history,
    weight_one, bias_one, weight_two, bias_two,
):
    feat, tile_set, hist = features[0, 0], tiles[0, 0], history[0, 0]
    coords = tile_coords[0, 0].T
    slots, block = tile_set.shape[0], tile_set.shape[1]
    f_in, hid, classes = feat.shape[1], weight_one.shape[1], weight_two.shape[1]
    w_two_t = weight_two.T
    dense_form = n_row * n_col <= slots
    smem = pl.BlockSpec(memory_space=pltpu.SMEM)
    vmem = pl.BlockSpec(memory_space=pltpu.VMEM)
    hbm = pl.BlockSpec(memory_space=pltpu.HBM)
    shape = jax.ShapeDtypeStruct

    def prepare(*after):
        return call(
            prepare_ordered_kernel,
            (shape((block, block), F32), shape((classes, block), F32)),
            (batch_mask[0], bias_two[None], *after),
            specs=[vmem] * 2 + [pl.BlockSpec(memory_space=pl.ANY)] * len(after),
            scratch=[pltpu.VMEM((block, -(-classes // 128) * 128), F32)],
        )

    chips_one = [feat, *fetch_chips(feat, "row", n_row)]

    if dense_form:
        anywhere = pl.BlockSpec(memory_space=pl.ANY)
        chunks = 8
        dense = call(
            functools.partial(build_kernel, n_row, n_col, chunks),
            shape((n_col * block, n_row * block), BF16),
            (
                tile_count,
                pltpu.with_memory_space_constraint(coords, pltpu.HBM),
                pltpu.with_memory_space_constraint(tile_set, pltpu.HBM),
            ),
            specs=[smem, hbm, hbm],
            scratch=[
                pltpu.SMEM((2, slots), jnp.int32),
                pltpu.VMEM((slots, block, block), BF16),
                pltpu.VMEM((n_row * n_col + 1, block // 2, block), F32),
                pltpu.VMEM((n_row * n_col + 1, block // 2, block), F32),
                pltpu.SemaphoreType.DMA((chunks,)),
                pltpu.SemaphoreType.DMA(()),
            ],
            cost=pl.CostEstimate(
                flops=slots * block * block,
                bytes_accessed=2 * slots * block * block,
                transcendentals=0,
            ),
        )
        mine_one = call(
            join_rows_kernel,
            shape((n_row // 2 * block, f_in), BF16),
            (*chips_one, dense),
            specs=[vmem] * len(chips_one) + [anywhere],
        )
        other_one = fetch_core(mine_one, "row", n_row)
        mask_cols, bias_cols = prepare(mine_one)
        half_one = call(half_one_kernel, shape((n_col * block, f_in), F32), (dense, mine_one))
        parts_one = call(
            layer_one_kernel,
            [shape((block, f_in), BF16)] * n_col,
            (dense, half_one, other_one),
        )
    else:
        mask_cols, bias_cols = prepare()
        summed = call(
            functools.partial(tiles_kernel, n_row, n_col, False),
            shape((n_col, block, f_in), BF16),
            (coords, tile_count, tile_set, both_cores(jnp.stack(chips_one), "row", n_row)),
            specs=[smem, smem, vmem, vmem],
            scratch=[pltpu.VMEM((n_col, block, f_in), F32)],
        )
        parts_one = [summed[k] for k in range(n_col)]

    arrived_one = send_each(parts_one, "col", n_col)
    pushed, proj = call(
        functools.partial(hidden_kernel, n_col),
        (shape((block, hid), BF16), shape((classes, block), BF16)),
        (parts_one[0], *arrived_one, feat, weight_one, bias_one[None], w_two_t, mask_cols, hist),
    )
    chips_two = [proj, *fetch_chips(proj, "row", n_row)]
    pushed = call(write_kernel, shape((block, hid), BF16), (pushed,))

    if dense_form:
        mine_two = call(
            join_columns_kernel, shape((classes, n_row // 2 * block), BF16), chips_two
        )
        other_two = fetch_core(mine_two, "row", n_row)
        half_two = call(half_two_kernel, shape((classes, n_col * block), F32), (dense, mine_two))
        parts_two = call(
            layer_two_kernel,
            [shape((classes, block), BF16)] * n_col,
            (dense, half_two, other_two),
        )
    else:
        summed = call(
            functools.partial(tiles_kernel, n_row, n_col, True),
            shape((n_col, classes, block), BF16),
            (coords, tile_count, tile_set, both_cores(jnp.stack(chips_two), "row", n_row)),
            specs=[smem, smem, vmem, vmem],
            scratch=[pltpu.VMEM((n_col, classes, block), F32)],
        )
        parts_two = [summed[k] for k in range(n_col)]

    arrived_two = send_each(parts_two, "col", n_col)
    scores = call(
        functools.partial(logits_kernel, n_col),
        shape((classes, 1, block), F32),
        (parts_two[0], *arrived_two, proj, bias_cols),
    )
    return pushed[None, None], scores.transpose(1, 2, 0)[None]


def solution(mesh):
    sizes = mesh.shape
    return jax.shard_map(
        functools.partial(on_device, sizes["row"], sizes["col"]),
        mesh=mesh,
        in_specs=(
            P("row", "col", None, None),
            P("row", "col", None, None, None),
            P("row", "col", None, None),
            P("row", "col"),
            P("row", "col", None),
            P("row", "col", None, None),
            P(),
            P(),
            P(),
            P(),
        ),
        out_specs=(P("row", "col", None, None), P("row", "col", None, None)),
        check_vma=False,
    )
```

```python
import functools

import jax
import jax.numpy as jnp
from jax import lax
from jax.experimental import pallas as pl
from jax.experimental.pallas import tpu as pltpu
from jax.sharding import PartitionSpec as P

BF16 = jnp.bfloat16
F32 = jnp.float32
VMEM_LIMIT = 48 * 1024 * 1024


def partner(index, slot):
    return index ^ slot


def column_of(slot, size):
    chip, core = slot >> 1, slot & 1
    direct = (core == 1) == (chip > 0)
    return jnp.where(direct, chip, size // 2 + chip)


def permuted(block, axis, size, slot):
    return lax.ppermute(block, axis, [(i, partner(i, slot)) for i in range(size)])


def fetch_chips(block, axis, size):
    return [permuted(block, axis, size, slot) for slot in range(3, size, 2)]


def fetch_core(blocks, axis, size):
    return permuted(blocks, axis, size, 1)


def both_cores(blocks, axis, size):
    return jnp.concatenate([blocks, fetch_core(blocks, axis, size)])


def send_each(blocks, axis, size):
    return [permuted(blocks[slot], axis, size, slot) for slot in reversed(range(1, size))]


def call(kernel, out_shape, operands, specs=None, scratch=(), cost=None):
    vmem = pl.BlockSpec(memory_space=pltpu.VMEM)
    return pl.pallas_call(
        kernel,
        out_shape=out_shape,
        in_specs=specs or [vmem] * len(operands),
        out_specs=jax.tree.map(lambda _: vmem, out_shape),
        scratch_shapes=list(scratch),
        cost_estimate=cost,
        compiler_params=pltpu.CompilerParams(vmem_limit_bytes=VMEM_LIMIT),
    )(*operands)


def dot_nt(left, right):
    return lax.dot_general(left, right, (((1,), (1,)), ((), ())), preferred_element_type=F32)


def build_kernel(
    n_row, n_col, chunks, count, coords_hbm, tiles_hbm, dense_ref, coords, tiles, first, second, sems, coords_sem
):
    slots, block = tiles.shape[0], tiles.shape[1]
    per, part = slots // chunks, block // 2
    copies = [
        pltpu.make_async_copy(
            tiles_hbm.at[pl.ds(i * per, per)], tiles.at[pl.ds(i * per, per)], sems.at[i]
        )
        for i in range(chunks)
    ]
    coords_copy = pltpu.make_async_copy(coords_hbm, coords, coords_sem)
    coords_copy.start()
    for copy in copies:
        copy.start()
    row, col = lax.axis_index("row"), lax.axis_index("col")
    live = count[0, 0]
    first[...] = jnp.zeros_like(first)
    second[...] = jnp.zeros_like(second)
    coords_copy.wait()

    def place(t):
        k, j = partner(coords[0, t], col), column_of(partner(coords[1, t], row), n_row)
        return jnp.where(t < live, k * n_row + j, n_row * n_col)

    for i in range(chunks):
        copies[i].wait()

        @pl.loop(0, per, unroll=8)
        def _(step):
            t = i * per + step
            at = place(t)
            first[at] += tiles[t, :part].astype(F32)
            second[at] += tiles[t, part:].astype(F32)

    for k in range(n_col):
        for j in range(n_row):
            at = k * n_row + j
            columns = slice(j * block, (j + 1) * block)
            dense_ref[k * block : k * block + part, columns] = first[at].astype(BF16)
            dense_ref[k * block + part : (k + 1) * block, columns] = second[at].astype(BF16)


def prepare_ordered_kernel(mask, bias, *refs):
    mask_out, bias_out, wide = refs[-3:]
    block, classes = mask_out.shape[0], bias.shape[1]
    wide[...] = jnp.zeros_like(wide)
    mask_out[...] = jnp.broadcast_to(mask[...].astype(F32), (block, block)).T
    wide[:, :classes] = jnp.broadcast_to(bias[...], (block, classes))
    bias_out[...] = wide[...].T[:classes]


def join_rows_kernel(*refs):
    out = refs[-1]
    block = refs[0].shape[0]
    for i in range(out.shape[0] // block):
        out[i * block : (i + 1) * block, :] = refs[i][...]


def join_columns_kernel(*refs):
    out = refs[-1]
    block = refs[0].shape[1]
    for i in range(out.shape[1] // block):
        out[:, i * block : (i + 1) * block] = refs[i][...]


def half_one_kernel(dense_ref, mine_ref, out):
    half = mine_ref.shape[0]
    out[...] = jnp.dot(dense_ref[:, :half], mine_ref[...], preferred_element_type=F32)


def layer_one_kernel(dense_ref, first_ref, other_ref, *outputs):
    half, block = other_ref.shape[0], dense_ref.shape[0] // len(outputs)
    for k, out in enumerate(outputs):
        rows = pl.ds(k * block, block)
        total = jnp.dot(dense_ref[rows, half:], other_ref[...], preferred_element_type=F32)
        out[...] = (first_ref[rows, :] + total).astype(BF16)


def hidden_kernel(sends, *refs):
    parts = refs[:sends]
    feat, w_one, b_one, w_two, mask, history, pushed_ref, proj_ref = refs[sends:]
    total = feat[...].astype(F32)
    for part in parts:
        total += part[...].astype(F32)
    pre = jnp.dot(total.astype(BF16), w_one[...], preferred_element_type=F32) + b_one[...]
    hidden = jnp.maximum(pre, 0.0)
    chosen = jnp.concatenate([mask[...]] * (hidden.shape[1] // mask.shape[1]), axis=1) == 1.0
    pushed = jnp.where(chosen, hidden, history[...].astype(F32)).astype(BF16)
    pushed_ref[...] = pushed
    proj_ref[...] = dot_nt(w_two[...], pushed).astype(BF16)


def write_kernel(value, out):
    out[...] = value[...]


def half_two_kernel(dense_ref, mine_ref, out):
    half = mine_ref.shape[1]
    out[...] = dot_nt(mine_ref[...], dense_ref[:, :half])


def layer_two_kernel(dense_ref, first_ref, other_ref, *outputs):
    half, block = other_ref.shape[1], dense_ref.shape[0] // len(outputs)
    for k, out in enumerate(outputs):
        rows = pl.ds(k * block, block)
        total = dot_nt(other_ref[...], dense_ref[rows, half:])
        out[...] = (first_ref[:, rows] + total).astype(BF16)


def logits_kernel(sends, *refs):
    parts = refs[:sends]
    proj, bias, out = refs[sends:]
    total = proj[...].astype(F32) + bias[...]
    for part in parts:
        total += part[...].astype(F32)
    out[:, 0, :] = total


def tiles_kernel(
    n_row, n_col, transposed, coords_ref, count_ref, tiles_ref, stacked_ref, out_ref, total
):
    row, col = lax.axis_index("row"), lax.axis_index("col")
    total[...] = jnp.zeros_like(total)

    @pl.loop(0, count_ref[0, 0])
    def _(t):
        k = partner(coords_ref[0, t], col)
        j = column_of(partner(coords_ref[1, t], row), n_row)
        if transposed:
            total[k] += dot_nt(stacked_ref[j], tiles_ref[t])
        else:
            total[k] += jnp.dot(tiles_ref[t], stacked_ref[j], preferred_element_type=F32)

    out_ref[...] = total[...].astype(BF16)


def on_device(
    n_row, n_col,
    features, tiles, tile_coords, tile_count, batch_mask, history,
    weight_one, bias_one, weight_two, bias_two,
):
    feat, tile_set, hist = features[0, 0], tiles[0, 0], history[0, 0]
    coords = tile_coords[0, 0].T
    slots, block = tile_set.shape[0], tile_set.shape[1]
    f_in, hid, classes = feat.shape[1], weight_one.shape[1], weight_two.shape[1]
    w_two_t = weight_two.T
    dense_form = n_row * n_col <= slots
    smem = pl.BlockSpec(memory_space=pltpu.SMEM)
    vmem = pl.BlockSpec(memory_space=pltpu.VMEM)
    hbm = pl.BlockSpec(memory_space=pltpu.HBM)
    shape = jax.ShapeDtypeStruct

    def prepare(*after):
        return call(
            prepare_ordered_kernel,
            (shape((block, block), F32), shape((classes, block), F32)),
            (batch_mask[0], bias_two[None], *after),
            specs=[vmem] * 2 + [pl.BlockSpec(memory_space=pl.ANY)] * len(after),
            scratch=[pltpu.VMEM((block, -(-classes // 128) * 128), F32)],
        )

    chips_one = [feat, *fetch_chips(feat, "row", n_row)]

    if dense_form:
        anywhere = pl.BlockSpec(memory_space=pl.ANY)
        chunks = 8
        dense = call(
            functools.partial(build_kernel, n_row, n_col, chunks),
            shape((n_col * block, n_row * block), BF16),
            (
                tile_count,
                pltpu.with_memory_space_constraint(coords, pltpu.HBM),
                pltpu.with_memory_space_constraint(tile_set, pltpu.HBM),
            ),
            specs=[smem, hbm, hbm],
            scratch=[
                pltpu.SMEM((2, slots), jnp.int32),
                pltpu.VMEM((slots, block, block), BF16),
                pltpu.VMEM((n_row * n_col + 1, block // 2, block), F32),
                pltpu.VMEM((n_row * n_col + 1, block // 2, block), F32),
                pltpu.SemaphoreType.DMA((chunks,)),
                pltpu.SemaphoreType.DMA(()),
            ],
            cost=pl.CostEstimate(
                flops=slots * block * block,
                bytes_accessed=2 * slots * block * block,
                transcendentals=0,
            ),
        )
        mine_one = call(
            join_rows_kernel,
            shape((n_row // 2 * block, f_in), BF16),
            (*chips_one, dense),
            specs=[vmem] * len(chips_one) + [anywhere],
        )
        other_one = fetch_core(mine_one, "row", n_row)
        mask_cols, bias_cols = prepare(mine_one)
        half_one = call(half_one_kernel, shape((n_col * block, f_in), F32), (dense, mine_one))
        parts_one = call(
            layer_one_kernel,
            [shape((block, f_in), BF16)] * n_col,
            (dense, half_one, other_one),
        )
    else:
        mask_cols, bias_cols = prepare()
        summed = call(
            functools.partial(tiles_kernel, n_row, n_col, False),
            shape((n_col, block, f_in), BF16),
            (coords, tile_count, tile_set, both_cores(jnp.stack(chips_one), "row", n_row)),
            specs=[smem, smem, vmem, vmem],
            scratch=[pltpu.VMEM((n_col, block, f_in), F32)],
        )
        parts_one = [summed[k] for k in range(n_col)]

    arrived_one = send_each(parts_one, "col", n_col)
    pushed, proj = call(
        functools.partial(hidden_kernel, n_col),
        (shape((block, hid), BF16), shape((classes, block), BF16)),
        (parts_one[0], *arrived_one, feat, weight_one, bias_one[None], w_two_t, mask_cols, hist),
    )
    chips_two = [proj, *fetch_chips(proj, "row", n_row)]
    pushed = call(write_kernel, shape((block, hid), BF16), (pushed,))

    if dense_form:
        mine_two = call(
            join_columns_kernel, shape((classes, n_row // 2 * block), BF16), chips_two
        )
        other_two = fetch_core(mine_two, "row", n_row)
        half_two = call(half_two_kernel, shape((classes, n_col * block), F32), (dense, mine_two))
        parts_two = call(
            layer_two_kernel,
            [shape((classes, block), BF16)] * n_col,
            (dense, half_two, other_two),
        )
    else:
        summed = call(
            functools.partial(tiles_kernel, n_row, n_col, True),
            shape((n_col, classes, block), BF16),
            (coords, tile_count, tile_set, both_cores(jnp.stack(chips_two), "row", n_row)),
            specs=[smem, smem, vmem, vmem],
            scratch=[pltpu.VMEM((n_col, classes, block), F32)],
        )
        parts_two = [summed[k] for k in range(n_col)]

    arrived_two = send_each(parts_two, "col", n_col)
    scores = call(
        functools.partial(logits_kernel, n_col),
        shape((classes, 1, block), F32),
        (parts_two[0], *arrived_two, proj, bias_cols),
    )
    return pushed[None, None], scores.transpose(1, 2, 0)[None]


def solution(mesh):
    sizes = mesh.shape
    return jax.shard_map(
        functools.partial(on_device, sizes["row"], sizes["col"]),
        mesh=mesh,
        in_specs=(
            P("row", "col", None, None),
            P("row", "col", None, None, None),
            P("row", "col", None, None),
            P("row", "col"),
            P("row", "col", None),
            P("row", "col", None, None),
            P(),
            P(),
            P(),
            P(),
        ),
        out_specs=(P("row", "col", None, None), P("row", "col", None, None)),
        check_vma=False,
    )
```

```python
import functools

import jax
import jax.numpy as jnp
from jax import lax
from jax.experimental import pallas as pl
from jax.experimental.pallas import tpu as pltpu
from jax.sharding import PartitionSpec as P

BF16 = jnp.bfloat16
F32 = jnp.float32
VMEM_LIMIT = 48 * 1024 * 1024


def partner(index, slot):
    return index ^ slot


def column_of(slot, size):
    chip, core = slot >> 1, slot & 1
    direct = (core == 1) == (chip > 0)
    place = jnp.where(chip == 0, 0, jnp.where(chip == 1, size // 2 - 1, chip - 1))
    return jnp.where(direct, place, size // 2 + place)


def permuted(block, axis, size, slot):
    return lax.ppermute(block, axis, [(i, partner(i, slot)) for i in range(size)])


def fetch_chips(block, axis, size):
    return [permuted(block, axis, size, slot) for slot in (*range(5, size, 2), 3)]


def fetch_core(blocks, axis, size):
    return permuted(blocks, axis, size, 1)


def both_cores(blocks, axis, size):
    return jnp.concatenate([blocks, fetch_core(blocks, axis, size)])


def send_each(blocks, axis, size):
    return [permuted(blocks[slot], axis, size, slot) for slot in reversed(range(1, size))]


def call(kernel, out_shape, operands, specs=None, scratch=(), cost=None, out_specs=None):
    vmem = pl.BlockSpec(memory_space=pltpu.VMEM)
    return pl.pallas_call(
        kernel,
        out_shape=out_shape,
        in_specs=specs or [vmem] * len(operands),
        out_specs=out_specs or jax.tree.map(lambda _: vmem, out_shape),
        scratch_shapes=list(scratch),
        cost_estimate=cost,
        compiler_params=pltpu.CompilerParams(vmem_limit_bytes=VMEM_LIMIT),
    )(*operands)


def dot_nt(left, right):
    return lax.dot_general(left, right, (((1,), (1,)), ((), ())), preferred_element_type=F32)


def build_kernel(
    n_row, n_col, chunks, count, coords_hbm, tiles_hbm, dense_ref, coords, tiles, first, second, sems, coords_sem
):
    slots, block = tiles.shape[0], tiles.shape[1]
    per, part = slots // chunks, block // 2
    copies = [
        pltpu.make_async_copy(
            tiles_hbm.at[pl.ds(i * per, per)], tiles.at[pl.ds(i * per, per)], sems.at[i]
        )
        for i in range(chunks)
    ]
    coords_copy = pltpu.make_async_copy(coords_hbm, coords, coords_sem)
    coords_copy.start()
    for copy in copies:
        copy.start()
    row, col = lax.axis_index("row"), lax.axis_index("col")
    live = count[0, 0]
    first[...] = jnp.zeros_like(first)
    second[...] = jnp.zeros_like(second)
    coords_copy.wait()

    def place(t):
        k, j = partner(coords[0, t], col), column_of(partner(coords[1, t], row), n_row)
        return jnp.where(t < live, k * n_row + j, n_row * n_col)

    for i in range(chunks):
        copies[i].wait()

        @pl.loop(0, per, unroll=8)
        def _(step):
            t = i * per + step
            at = place(t)
            first[at] += tiles[t, :part].astype(F32)
            second[at] += tiles[t, part:].astype(F32)

    for k in range(n_col):
        for j in range(n_row):
            at = k * n_row + j
            columns = slice(j * block, (j + 1) * block)
            dense_ref[k * block : k * block + part, columns] = first[at].astype(BF16)
            dense_ref[k * block + part : (k + 1) * block, columns] = second[at].astype(BF16)


def prepare_ordered_kernel(mask, bias, *refs):
    mask_out, bias_out, wide = refs[-3:]
    block, classes = mask_out.shape[0], bias.shape[1]
    wide[...] = jnp.zeros_like(wide)
    mask_out[...] = jnp.broadcast_to(mask[...].astype(F32), (block, block)).T
    wide[:, :classes] = jnp.broadcast_to(bias[...], (block, classes))
    bias_out[...] = wide[...].T[:classes]


def join_rows_kernel(*refs):
    out = refs[-1]
    block = refs[0].shape[0]
    for i in range(out.shape[0] // block):
        out[i * block : (i + 1) * block, :] = refs[i][...]


def half_one_kernel(dense_ref, mine_ref, out):
    half = mine_ref.shape[0]
    out[...] = jnp.dot(dense_ref[:, :half], mine_ref[...], preferred_element_type=F32)


def layer_one_kernel(dense_ref, first_ref, other_ref, *outputs):
    half, block = other_ref.shape[0], dense_ref.shape[0] // len(outputs)
    for k, out in enumerate(outputs):
        rows = pl.ds(k * block, block)
        total = jnp.dot(dense_ref[rows, half:], other_ref[...], preferred_element_type=F32)
        out[...] = (first_ref[rows, :] + total).astype(BF16)


def hidden_kernel(sends, *refs):
    parts = refs[:sends]
    feat, w_one, b_one, w_two, mask, history, pushed_ref, proj_ref = refs[sends:]
    total = feat[...].astype(F32)
    for part in parts:
        total += part[...].astype(F32)
    pre = jnp.dot(total.astype(BF16), w_one[...], preferred_element_type=F32) + b_one[...]
    hidden = jnp.maximum(pre, 0.0)
    chosen = jnp.concatenate([mask[...]] * (hidden.shape[1] // mask.shape[1]), axis=1) == 1.0
    pushed = jnp.where(chosen, hidden, history[...].astype(F32)).astype(BF16)
    pushed_ref[...] = pushed
    proj_ref[...] = dot_nt(w_two[...], pushed).astype(BF16)


def write_kernel(value, out):
    out[...] = value[...]


def lanes(refs, scratch):
    block = refs[0].shape[1]
    for i, ref in enumerate(refs):
        scratch[:, i * block : (i + 1) * block] = ref[...]
    return scratch[...]


def half_two_kernel(dense_ref, *refs):
    blocks, (out, scratch) = refs[:-2], refs[-2:]
    out[...] = dot_nt(lanes(blocks, scratch), dense_ref[:, : scratch.shape[1]])


def layer_two_kernel(n_col, dense_ref, first_ref, *refs):
    blocks, outputs, scratch = refs[: -n_col - 1], refs[-n_col - 1 : -1], refs[-1]
    block, at = blocks[0].shape[1], dense_ref.shape[1] - scratch.shape[1]
    rest = lanes(blocks, scratch)
    for k, out in enumerate(outputs):
        rows = pl.ds(k * block, block)
        out[...] = (first_ref[:, rows] + dot_nt(rest, dense_ref[rows, at:])).astype(BF16)


def logits_kernel(n_col, pieces, *refs):
    parts = refs[:n_col]
    proj, bias, out_hbm, staged, sems = refs[n_col:]
    step = -(-staged.shape[0] // pieces // 16) * 16
    copies = []
    for i in range(pieces):
        rows = slice(i * step, (i + 1) * step if i < pieces - 1 else staged.shape[0])
        total = proj[rows, :].astype(F32) + bias[rows, :]
        for part in parts:
            total += part[rows, :].astype(F32)
        staged[rows, 0, :] = total
        copies.append(pltpu.make_async_copy(staged.at[rows], out_hbm.at[rows], sems.at[i]))
        copies[-1].start()
    for copy in copies:
        copy.wait()


def tiles_kernel(
    n_row, n_col, transposed, coords_ref, count_ref, tiles_ref, stacked_ref, out_ref, total
):
    row, col = lax.axis_index("row"), lax.axis_index("col")
    total[...] = jnp.zeros_like(total)

    @pl.loop(0, count_ref[0, 0])
    def _(t):
        k = partner(coords_ref[0, t], col)
        j = column_of(partner(coords_ref[1, t], row), n_row)
        if transposed:
            total[k] += dot_nt(stacked_ref[j], tiles_ref[t])
        else:
            total[k] += jnp.dot(tiles_ref[t], stacked_ref[j], preferred_element_type=F32)

    out_ref[...] = total[...].astype(BF16)


def on_device(
    n_row, n_col,
    features, tiles, tile_coords, tile_count, batch_mask, history,
    weight_one, bias_one, weight_two, bias_two,
):
    feat, tile_set, hist = features[0, 0], tiles[0, 0], history[0, 0]
    coords = tile_coords[0, 0].T
    slots, block = tile_set.shape[0], tile_set.shape[1]
    f_in, hid, classes = feat.shape[1], weight_one.shape[1], weight_two.shape[1]
    w_two_t = weight_two.T
    dense_form = n_row * n_col <= slots
    smem = pl.BlockSpec(memory_space=pltpu.SMEM)
    vmem = pl.BlockSpec(memory_space=pltpu.VMEM)
    hbm = pl.BlockSpec(memory_space=pltpu.HBM)
    shape = jax.ShapeDtypeStruct

    def prepare(*after):
        return call(
            prepare_ordered_kernel,
            (shape((block, block), F32), shape((classes, block), F32)),
            (batch_mask[0], bias_two[None], *after),
            specs=[vmem] * 2 + [pl.BlockSpec(memory_space=pl.ANY)] * len(after),
            scratch=[pltpu.VMEM((block, -(-classes // 128) * 128), F32)],
        )

    chips_one = [feat, *fetch_chips(feat, "row", n_row)]

    if dense_form:
        anywhere = pl.BlockSpec(memory_space=pl.ANY)
        chunks = 8
        dense = call(
            functools.partial(build_kernel, n_row, n_col, chunks),
            shape((n_col * block, n_row * block), BF16),
            (
                tile_count,
                pltpu.with_memory_space_constraint(coords, pltpu.HBM),
                pltpu.with_memory_space_constraint(tile_set, pltpu.HBM),
            ),
            specs=[smem, hbm, hbm],
            scratch=[
                pltpu.SMEM((2, slots), jnp.int32),
                pltpu.VMEM((slots, block, block), BF16),
                pltpu.VMEM((n_row * n_col + 1, block // 2, block), F32),
                pltpu.VMEM((n_row * n_col + 1, block // 2, block), F32),
                pltpu.SemaphoreType.DMA((chunks,)),
                pltpu.SemaphoreType.DMA(()),
            ],
            cost=pl.CostEstimate(
                flops=slots * block * block,
                bytes_accessed=2 * slots * block * block,
                transcendentals=0,
            ),
        )
        mine_one = call(
            join_rows_kernel,
            shape((n_row // 2 * block, f_in), BF16),
            (*chips_one, dense),
            specs=[vmem] * len(chips_one) + [anywhere],
        )
        other_one = fetch_core(mine_one, "row", n_row)
        mask_cols, bias_cols = prepare(mine_one)
        half_one = call(half_one_kernel, shape((n_col * block, f_in), F32), (dense, mine_one))
        parts_one = call(
            layer_one_kernel,
            [shape((block, f_in), BF16)] * n_col,
            (dense, half_one, other_one),
        )
    else:
        mask_cols, bias_cols = prepare()
        summed = call(
            functools.partial(tiles_kernel, n_row, n_col, False),
            shape((n_col, block, f_in), BF16),
            (coords, tile_count, tile_set, both_cores(jnp.stack(chips_one), "row", n_row)),
            specs=[smem, smem, vmem, vmem],
            scratch=[pltpu.VMEM((n_col, block, f_in), F32)],
        )
        parts_one = [summed[k] for k in range(n_col)]

    arrived_one = send_each(parts_one, "col", n_col)
    pushed, proj = call(
        functools.partial(hidden_kernel, n_col),
        (shape((block, hid), BF16), shape((classes, block), BF16)),
        (parts_one[0], *arrived_one, feat, weight_one, bias_one[None], w_two_t, mask_cols, hist),
    )
    chips_two = [proj, *fetch_chips(proj, "row", n_row)]
    if dense_form:
        near_other = permuted(proj, "row", n_row, 2)
        others_two = [fetch_core(x, "row", n_row) for x in chips_two[:-1]] + [near_other]
    pushed = call(write_kernel, shape((block, hid), BF16), (pushed,))

    if dense_form:
        early, late = chips_two[:-1], [chips_two[-1], *others_two]
        half_two = call(
            half_two_kernel,
            shape((classes, n_col * block), F32),
            (dense, *early),
            scratch=[pltpu.VMEM((classes, len(early) * block), BF16)],
        )
        parts_two = call(
            functools.partial(layer_two_kernel, n_col),
            [shape((classes, block), BF16)] * n_col,
            (dense, half_two, *late),
            scratch=[pltpu.VMEM((classes, len(late) * block), BF16)],
        )
    else:
        summed = call(
            functools.partial(tiles_kernel, n_row, n_col, True),
            shape((n_col, classes, block), BF16),
            (coords, tile_count, tile_set, both_cores(jnp.stack(chips_two), "row", n_row)),
            specs=[smem, smem, vmem, vmem],
            scratch=[pltpu.VMEM((n_col, classes, block), F32)],
        )
        parts_two = [summed[k] for k in range(n_col)]

    arrived_two = send_each(parts_two, "col", n_col)
    pieces = 4
    scores = call(
        functools.partial(logits_kernel, n_col, pieces),
        shape((classes, 1, block), F32),
        (parts_two[0], *arrived_two, proj, bias_cols),
        scratch=[pltpu.VMEM((classes, 1, block), F32), pltpu.SemaphoreType.DMA((pieces,))],
        out_specs=pl.BlockSpec(memory_space=pl.ANY),
    )
    return pushed[None, None], scores.transpose(1, 2, 0)[None]


def solution(mesh):
    sizes = mesh.shape
    return jax.shard_map(
        functools.partial(on_device, sizes["row"], sizes["col"]),
        mesh=mesh,
        in_specs=(
            P("row", "col", None, None),
            P("row", "col", None, None, None),
            P("row", "col", None, None),
            P("row", "col"),
            P("row", "col", None),
            P("row", "col", None, None),
            P(),
            P(),
            P(),
            P(),
        ),
        out_specs=(P("row", "col", None, None), P("row", "col", None, None)),
        check_vma=False,
    )
```

```python
import functools

import jax
import jax.numpy as jnp
from jax import lax
from jax.experimental import pallas as pl
from jax.experimental.pallas import tpu as pltpu
from jax.sharding import PartitionSpec as P

BF16 = jnp.bfloat16
F32 = jnp.float32
VMEM_LIMIT = 48 * 1024 * 1024


def partner(index, slot):
    return index ^ slot


def order(size):
    return [0, *range(5, size, 2), 3]


def column_at(slot, size):
    first = order(size)
    return first.index(slot) if slot in first else size // 2 + first.index(slot ^ 1)


def column_of(slot, size):
    column = slot
    for i in range(size):
        column = jnp.where(slot == i, column_at(i, size), column)
    return column


def permuted(block, axis, size, slot):
    return lax.ppermute(block, axis, [(i, partner(i, slot)) for i in range(size)])


def fetch_chips(block, axis, size):
    return [permuted(block, axis, size, slot) for slot in order(size)[1:]]


def fetch_core(blocks, axis, size):
    return permuted(blocks, axis, size, 1)


def both_cores(blocks, axis, size):
    return jnp.concatenate([blocks, fetch_core(blocks, axis, size)])


def send_each(blocks, axis, size):
    return [permuted(blocks[slot], axis, size, slot) for slot in reversed(range(1, size))]


def call(kernel, out_shape, operands, specs=None, scratch=(), cost=None, out_specs=None):
    vmem = pl.BlockSpec(memory_space=pltpu.VMEM)
    return pl.pallas_call(
        kernel,
        out_shape=out_shape,
        in_specs=specs or [vmem] * len(operands),
        out_specs=out_specs or jax.tree.map(lambda _: vmem, out_shape),
        scratch_shapes=list(scratch),
        cost_estimate=cost,
        compiler_params=pltpu.CompilerParams(vmem_limit_bytes=VMEM_LIMIT),
    )(*operands)


def dot_nt(left, right):
    return lax.dot_general(left, right, (((1,), (1,)), ((), ())), preferred_element_type=F32)


def places_kernel(
    n_row, n_col, count, coords_hbm, feat_hbm, places, feat_out, coords, coords_sem, feat_sem
):
    copy = pltpu.make_async_copy(coords_hbm, coords, coords_sem)
    feat_copy = pltpu.make_async_copy(feat_hbm, feat_out, feat_sem)
    copy.start()
    feat_copy.start()
    copy.wait()
    row, col = lax.axis_index("row"), lax.axis_index("col")
    k = partner(coords[0:1, :], col)
    j = column_of(partner(coords[1:2, :], row), n_row)
    slot = lax.broadcasted_iota(jnp.int32, k.shape, 1)
    places[...] = jnp.where(slot < count[0, 0], k * n_row + j, n_row * n_col)
    feat_copy.wait()


def build_kernel(n_row, n_col, chunks, places_any, tiles_hbm, *refs):
    dense_ref, places, tiles, first, second, sems, places_sem = refs[-7:]
    slots, block = tiles.shape[0], tiles.shape[1]
    per, part = slots // chunks, block // 2
    copies = [
        pltpu.make_async_copy(
            tiles_hbm.at[pl.ds(i * per, per)], tiles.at[pl.ds(i * per, per)], sems.at[i]
        )
        for i in range(chunks)
    ]
    places_copy = pltpu.make_async_copy(places_any, places, places_sem)
    places_copy.start()
    for copy in copies:
        copy.start()
    first[...] = jnp.zeros_like(first)
    second[...] = jnp.zeros_like(second)
    places_copy.wait()

    for i in range(chunks):
        copies[i].wait()

        @pl.loop(0, per, unroll=8)
        def _(step):
            t = i * per + step
            at = places[0, t]
            first[at] += tiles[t, :part].astype(F32)
            second[at] += tiles[t, part:].astype(F32)

    for k in range(n_col):
        for j in range(n_row):
            at = k * n_row + j
            columns = slice(j * block, (j + 1) * block)
            dense_ref[k * block : k * block + part, columns] = first[at].astype(BF16)
            dense_ref[k * block + part : (k + 1) * block, columns] = second[at].astype(BF16)


def prepare_ordered_kernel(mask, bias, *refs):
    mask_out, bias_out, wide = refs[-3:]
    block, classes = mask_out.shape[0], bias.shape[1]
    wide[...] = jnp.zeros_like(wide)
    mask_out[...] = jnp.broadcast_to(mask[...].astype(F32), (block, block)).T
    wide[:, :classes] = jnp.broadcast_to(bias[...], (block, classes))
    bias_out[...] = wide[...].T[:classes]


def join_rows_kernel(*refs):
    out = refs[-1]
    block = refs[0].shape[0]
    for i in range(out.shape[0] // block):
        out[i * block : (i + 1) * block, :] = refs[i][...]


def stack_pairs(pairs, columns, scratch):
    block = scratch.shape[0] // (2 * len(pairs))
    for ref, places in zip(pairs, columns):
        for i, place in enumerate(places):
            scratch[place * block : (place + 1) * block, :] = ref[i * block : (i + 1) * block, :]


def layer_one_kernel(columns, dense_ref, *refs):
    n_pairs = len(columns)
    pairs, outputs, gathered = refs[:n_pairs], refs[n_pairs:-1], refs[-1]
    block = dense_ref.shape[0] // len(outputs)
    stack_pairs(pairs, columns, gathered)
    for k, out in enumerate(outputs):
        out[...] = jnp.dot(
            dense_ref[k * block : (k + 1) * block, :], gathered[...], preferred_element_type=F32
        ).astype(BF16)


def hidden_kernel(sends, *refs):
    parts = refs[:sends]
    feat, w_one, b_one, w_two, mask, history, pushed_ref, proj_ref = refs[sends:]
    total = feat[...].astype(F32)
    for part in parts:
        total += part[...].astype(F32)
    pre = jnp.dot(total.astype(BF16), w_one[...], preferred_element_type=F32) + b_one[...]
    hidden = jnp.maximum(pre, 0.0)
    chosen = jnp.concatenate([mask[...]] * (hidden.shape[1] // mask.shape[1]), axis=1) == 1.0
    pushed = jnp.where(chosen, hidden, history[...].astype(F32)).astype(BF16)
    pushed_ref[...] = pushed
    proj_ref[...] = dot_nt(w_two[...], pushed).astype(BF16)


def write_kernel(value, out):
    out[...] = value[...]


def lanes(refs, scratch):
    block = refs[0].shape[1]
    for i, ref in enumerate(refs):
        scratch[:, i * block : (i + 1) * block] = ref[...]
    return scratch[...]


def half_two_kernel(dense_ref, *refs):
    blocks, (out, scratch) = refs[:-2], refs[-2:]
    out[...] = dot_nt(lanes(blocks, scratch), dense_ref[:, : scratch.shape[1]])


def layer_two_kernel(n_col, dense_ref, first_ref, *refs):
    blocks, outputs, scratch = refs[: -n_col - 1], refs[-n_col - 1 : -1], refs[-1]
    block, at = blocks[0].shape[1], dense_ref.shape[1] - scratch.shape[1]
    rest = lanes(blocks, scratch)
    for k, out in enumerate(outputs):
        rows = pl.ds(k * block, block)
        out[...] = (first_ref[:, rows] + dot_nt(rest, dense_ref[rows, at:])).astype(BF16)


def logits_kernel(n_col, pieces, *refs):
    parts = refs[:n_col]
    proj, bias, out_hbm, staged, sems = refs[n_col:]
    step = -(-staged.shape[0] // pieces // 16) * 16
    copies = []
    for i in range(pieces):
        rows = slice(i * step, (i + 1) * step if i < pieces - 1 else staged.shape[0])
        total = proj[rows, :].astype(F32) + bias[rows, :]
        for part in parts:
            total += part[rows, :].astype(F32)
        staged[rows, 0, :] = total
        copies.append(pltpu.make_async_copy(staged.at[rows], out_hbm.at[rows], sems.at[i]))
        copies[-1].start()
    for copy in copies:
        copy.wait()


def tiles_kernel(
    n_row, n_col, transposed, coords_ref, count_ref, tiles_ref, stacked_ref, out_ref, total
):
    row, col = lax.axis_index("row"), lax.axis_index("col")
    total[...] = jnp.zeros_like(total)

    @pl.loop(0, count_ref[0, 0])
    def _(t):
        k = partner(coords_ref[0, t], col)
        j = column_of(partner(coords_ref[1, t], row), n_row)
        if transposed:
            total[k] += dot_nt(stacked_ref[j], tiles_ref[t])
        else:
            total[k] += jnp.dot(tiles_ref[t], stacked_ref[j], preferred_element_type=F32)

    out_ref[...] = total[...].astype(BF16)


def on_device(
    n_row, n_col,
    features, tiles, tile_coords, tile_count, batch_mask, history,
    weight_one, bias_one, weight_two, bias_two,
):
    feat, tile_set, hist = features[0, 0], tiles[0, 0], history[0, 0]
    coords = tile_coords[0, 0].T
    slots, block = tile_set.shape[0], tile_set.shape[1]
    f_in, hid, classes = feat.shape[1], weight_one.shape[1], weight_two.shape[1]
    w_two_t = weight_two.T
    dense_form = n_row * n_col <= slots
    smem = pl.BlockSpec(memory_space=pltpu.SMEM)
    vmem = pl.BlockSpec(memory_space=pltpu.VMEM)
    hbm = pl.BlockSpec(memory_space=pltpu.HBM)
    shape = jax.ShapeDtypeStruct

    def prepare(*after):
        return call(
            prepare_ordered_kernel,
            (shape((block, block), F32), shape((classes, block), F32)),
            (batch_mask[0], bias_two[None], *after),
            specs=[vmem] * 2 + [pl.BlockSpec(memory_space=pl.ANY)] * len(after),
            scratch=[pltpu.VMEM((block, -(-classes // 128) * 128), F32)],
        )

    anywhere = pl.BlockSpec(memory_space=pl.ANY)
    if dense_form:
        other_feat = fetch_core(feat, "row", n_row)
        places, feat_near = call(
            functools.partial(places_kernel, n_row, n_col),
            (shape((1, slots), jnp.int32), shape((block, f_in), BF16)),
            (
                tile_count,
                pltpu.with_memory_space_constraint(coords, pltpu.HBM),
                pltpu.with_memory_space_constraint(feat, pltpu.HBM),
            ),
            specs=[smem, hbm, hbm],
            scratch=[
                pltpu.VMEM((2, slots), jnp.int32),
                pltpu.SemaphoreType.DMA(()),
                pltpu.SemaphoreType.DMA(()),
            ],
        )
        pair = call(
            join_rows_kernel,
            shape((2 * block, f_in), BF16),
            (feat_near, other_feat, places),
            specs=[vmem, vmem, anywhere],
        )
        pairs_one = [pair, *fetch_chips(pair, "row", n_row)]
        columns = [(column_at(slot, n_row), column_at(slot ^ 1, n_row)) for slot in order(n_row)]
        chunks = 8
        dense = call(
            functools.partial(build_kernel, n_row, n_col, chunks),
            shape((n_col * block, n_row * block), BF16),
            (places, pltpu.with_memory_space_constraint(tile_set, pltpu.HBM), pair),
            specs=[anywhere, hbm, anywhere],
            scratch=[
                pltpu.SMEM((1, slots), jnp.int32),
                pltpu.VMEM((slots, block, block), BF16),
                pltpu.VMEM((n_row * n_col + 1, block // 2, block), F32),
                pltpu.VMEM((n_row * n_col + 1, block // 2, block), F32),
                pltpu.SemaphoreType.DMA((chunks,)),
                pltpu.SemaphoreType.DMA(()),
            ],
            cost=pl.CostEstimate(
                flops=slots * block * block,
                bytes_accessed=2 * slots * block * block,
                transcendentals=0,
            ),
        )
        mask_cols, bias_cols = prepare(dense)
        parts_one = call(
            functools.partial(layer_one_kernel, columns),
            [shape((block, f_in), BF16)] * n_col,
            (dense, *pairs_one),
            scratch=[pltpu.VMEM((n_row * block, f_in), BF16)],
        )
    else:
        chips_one = [feat, *fetch_chips(feat, "row", n_row)]
        mask_cols, bias_cols = prepare()
        summed = call(
            functools.partial(tiles_kernel, n_row, n_col, False),
            shape((n_col, block, f_in), BF16),
            (coords, tile_count, tile_set, both_cores(jnp.stack(chips_one), "row", n_row)),
            specs=[smem, smem, vmem, vmem],
            scratch=[pltpu.VMEM((n_col, block, f_in), F32)],
        )
        parts_one = [summed[k] for k in range(n_col)]

    arrived_one = send_each(parts_one, "col", n_col)
    pushed, proj = call(
        functools.partial(hidden_kernel, n_col),
        (shape((block, hid), BF16), shape((classes, block), BF16)),
        (parts_one[0], *arrived_one, feat, weight_one, bias_one[None], w_two_t, mask_cols, hist),
    )
    chips_two = [proj, *fetch_chips(proj, "row", n_row)]
    if dense_form:
        near_other = permuted(proj, "row", n_row, 2)
        others_two = [fetch_core(x, "row", n_row) for x in chips_two[:-1]] + [near_other]
    pushed = call(write_kernel, shape((block, hid), BF16), (pushed,))

    if dense_form:
        early, late = chips_two[:-1], [chips_two[-1], *others_two]
        half_two = call(
            half_two_kernel,
            shape((classes, n_col * block), F32),
            (dense, *early),
            scratch=[pltpu.VMEM((classes, len(early) * block), BF16)],
        )
        parts_two = call(
            functools.partial(layer_two_kernel, n_col),
            [shape((classes, block), BF16)] * n_col,
            (dense, half_two, *late),
            scratch=[pltpu.VMEM((classes, len(late) * block), BF16)],
        )
    else:
        summed = call(
            functools.partial(tiles_kernel, n_row, n_col, True),
            shape((n_col, classes, block), BF16),
            (coords, tile_count, tile_set, both_cores(jnp.stack(chips_two), "row", n_row)),
            specs=[smem, smem, vmem, vmem],
            scratch=[pltpu.VMEM((n_col, classes, block), F32)],
        )
        parts_two = [summed[k] for k in range(n_col)]

    arrived_two = send_each(parts_two, "col", n_col)
    pieces = 4
    scores = call(
        functools.partial(logits_kernel, n_col, pieces),
        shape((classes, 1, block), F32),
        (parts_two[0], *arrived_two, proj, bias_cols),
        scratch=[pltpu.VMEM((classes, 1, block), F32), pltpu.SemaphoreType.DMA((pieces,))],
        out_specs=pl.BlockSpec(memory_space=pl.ANY),
    )
    return pushed[None, None], scores.transpose(1, 2, 0)[None]


def solution(mesh):
    sizes = mesh.shape
    return jax.shard_map(
        functools.partial(on_device, sizes["row"], sizes["col"]),
        mesh=mesh,
        in_specs=(
            P("row", "col", None, None),
            P("row", "col", None, None, None),
            P("row", "col", None, None),
            P("row", "col"),
            P("row", "col", None),
            P("row", "col", None, None),
            P(),
            P(),
            P(),
            P(),
        ),
        out_specs=(P("row", "col", None, None), P("row", "col", None, None)),
        check_vma=False,
    )
```

```python
import functools

import jax
import jax.numpy as jnp
from jax import lax
from jax.experimental import pallas as pl
from jax.experimental.pallas import tpu as pltpu
from jax.sharding import PartitionSpec as P

BF16 = jnp.bfloat16
F32 = jnp.float32
VMEM_LIMIT = 48 * 1024 * 1024


def partner(index, slot):
    return index ^ slot


def order(size):
    return [0, *range(5, size, 2), 3]


def column_order(size):
    return order(size) + [slot ^ 1 for slot in order(size)]


def permuted(block, axis, size, slot):
    return lax.ppermute(block, axis, [(i, partner(i, slot)) for i in range(size)])


def fetch_chips(block, axis, size):
    return [permuted(block, axis, size, slot) for slot in order(size)[1:]]


def fetch_core(blocks, axis, size):
    return permuted(blocks, axis, size, 1)


def both_cores(blocks, axis, size):
    found = jnp.concatenate([blocks, fetch_core(blocks, axis, size)])
    return found[jnp.argsort(jnp.array(column_order(size)))]


def send_each(blocks, axis, size):
    return [permuted(blocks[slot], axis, size, slot) for slot in reversed(range(1, size))]


def call(kernel, out_shape, operands, specs=None, scratch=(), cost=None, out_specs=None):
    vmem = pl.BlockSpec(memory_space=pltpu.VMEM)
    return pl.pallas_call(
        kernel,
        out_shape=out_shape,
        in_specs=specs or [vmem] * len(operands),
        out_specs=out_specs or jax.tree.map(lambda _: vmem, out_shape),
        scratch_shapes=list(scratch),
        cost_estimate=cost,
        compiler_params=pltpu.CompilerParams(vmem_limit_bytes=VMEM_LIMIT),
    )(*operands)


def dot_nt(left, right):
    return lax.dot_general(left, right, (((1,), (1,)), ((), ())), preferred_element_type=F32)


def build_kernel(
    n_row, n_col, chunks, count, coords_hbm, tiles_hbm, dense_ref, coords, tiles, first, second, sems, coords_sem
):
    slots, block = tiles.shape[0], tiles.shape[1]
    per, part = slots // chunks, block // 2
    copies = [
        pltpu.make_async_copy(
            tiles_hbm.at[pl.ds(i * per, per)], tiles.at[pl.ds(i * per, per)], sems.at[i]
        )
        for i in range(chunks)
    ]
    coords_copy = pltpu.make_async_copy(coords_hbm, coords, coords_sem)
    coords_copy.start()
    live = count[0, 0]
    for i, copy in enumerate(copies):
        pl.when(i * per < live)(copy.start)
    row, col = lax.axis_index("row"), lax.axis_index("col")
    first[...] = jnp.zeros_like(first)
    second[...] = jnp.zeros_like(second)
    coords_copy.wait()

    def place(t):
        at = partner(coords[0, t], col) * n_row + partner(coords[1, t], row)
        return jnp.where(t < live, at, n_row * n_col)

    for i in range(chunks):

        @pl.when(i * per < live)
        def _():
            copies[i].wait()

            @pl.loop(0, per, unroll=8)
            def _(step):
                t = i * per + step
                at = place(t)
                first[at] += tiles[t, :part].astype(F32)
                second[at] += tiles[t, part:].astype(F32)

    for k in range(n_col):
        for j, slot in enumerate(column_order(n_row)):
            at = k * n_row + slot
            columns = slice(j * block, (j + 1) * block)
            dense_ref[k * block : k * block + part, columns] = first[at].astype(BF16)
            dense_ref[k * block + part : (k + 1) * block, columns] = second[at].astype(BF16)


def prepare_ordered_kernel(mask, bias, *refs):
    mask_out, bias_out, wide = refs[-3:]
    block, classes = mask_out.shape[0], bias.shape[1]
    wide[...] = jnp.zeros_like(wide)
    mask_out[...] = jnp.broadcast_to(mask[...].astype(F32), (block, block)).T
    wide[:, :classes] = jnp.broadcast_to(bias[...], (block, classes))
    bias_out[...] = wide[...].T[:classes]


def join_rows_kernel(*refs):
    out = refs[-1]
    block = refs[0].shape[0]
    for i in range(out.shape[0] // block):
        out[i * block : (i + 1) * block, :] = refs[i][...]


def half_one_kernel(dense_ref, mine_ref, out):
    half = mine_ref.shape[0]
    out[...] = jnp.dot(dense_ref[:, :half], mine_ref[...], preferred_element_type=F32)


def layer_one_kernel(dense_ref, first_ref, other_ref, *outputs):
    half, block = other_ref.shape[0], dense_ref.shape[0] // len(outputs)
    for k, out in enumerate(outputs):
        rows = pl.ds(k * block, block)
        total = jnp.dot(dense_ref[rows, half:], other_ref[...], preferred_element_type=F32)
        out[...] = (first_ref[rows, :] + total).astype(BF16)


def hidden_kernel(sends, *refs):
    parts = refs[:sends]
    feat, w_one, b_one, w_two, mask, history, pushed_ref, proj_ref = refs[sends:]
    total = feat[...].astype(F32)
    for part in parts:
        total += part[...].astype(F32)
    pre = jnp.dot(total.astype(BF16), w_one[...], preferred_element_type=F32) + b_one[...]
    hidden = jnp.maximum(pre, 0.0)
    chosen = jnp.concatenate([mask[...]] * (hidden.shape[1] // mask.shape[1]), axis=1) == 1.0
    pushed = jnp.where(chosen, hidden, history[...].astype(F32)).astype(BF16)
    pushed_ref[...] = pushed
    proj_ref[...] = dot_nt(w_two[...], pushed).astype(BF16)


def write_kernel(value, out):
    out[...] = value[...]


def lanes(refs, scratch):
    block = refs[0].shape[1]
    for i, ref in enumerate(refs):
        scratch[:, i * block : (i + 1) * block] = ref[...]
    return scratch[...]


def half_two_kernel(dense_ref, *refs):
    blocks, (out, scratch) = refs[:-2], refs[-2:]
    out[...] = dot_nt(lanes(blocks, scratch), dense_ref[:, : scratch.shape[1]])


def layer_two_kernel(n_col, dense_ref, first_ref, *refs):
    blocks, outputs, scratch = refs[: -n_col - 1], refs[-n_col - 1 : -1], refs[-1]
    block, at = blocks[0].shape[1], dense_ref.shape[1] - scratch.shape[1]
    rest = lanes(blocks, scratch)
    for k, out in enumerate(outputs):
        rows = pl.ds(k * block, block)
        out[...] = (first_ref[:, rows] + dot_nt(rest, dense_ref[rows, at:])).astype(BF16)


def logits_kernel(n_col, pieces, *refs):
    parts = refs[:n_col]
    proj, bias, out_hbm, staged, sems = refs[n_col:]
    step = -(-staged.shape[0] // pieces // 16) * 16
    copies = []
    for i in range(pieces):
        rows = slice(i * step, (i + 1) * step if i < pieces - 1 else staged.shape[0])
        total = proj[rows, :].astype(F32) + bias[rows, :]
        for part in parts:
            total += part[rows, :].astype(F32)
        staged[rows, 0, :] = total
        copies.append(pltpu.make_async_copy(staged.at[rows], out_hbm.at[rows], sems.at[i]))
        copies[-1].start()
    for copy in copies:
        copy.wait()


def tiles_kernel(
    n_row, n_col, transposed, coords_ref, count_ref, tiles_ref, stacked_ref, out_ref, total
):
    row, col = lax.axis_index("row"), lax.axis_index("col")
    total[...] = jnp.zeros_like(total)

    @pl.loop(0, count_ref[0, 0])
    def _(t):
        k = partner(coords_ref[0, t], col)
        j = partner(coords_ref[1, t], row)
        if transposed:
            total[k] += dot_nt(stacked_ref[j], tiles_ref[t])
        else:
            total[k] += jnp.dot(tiles_ref[t], stacked_ref[j], preferred_element_type=F32)

    out_ref[...] = total[...].astype(BF16)


def on_device(
    n_row, n_col,
    features, tiles, tile_coords, tile_count, batch_mask, history,
    weight_one, bias_one, weight_two, bias_two,
):
    feat, tile_set, hist = features[0, 0], tiles[0, 0], history[0, 0]
    coords = tile_coords[0, 0].T
    slots, block = tile_set.shape[0], tile_set.shape[1]
    f_in, hid, classes = feat.shape[1], weight_one.shape[1], weight_two.shape[1]
    w_two_t = weight_two.T
    dense_form = n_row * n_col <= slots
    smem = pl.BlockSpec(memory_space=pltpu.SMEM)
    vmem = pl.BlockSpec(memory_space=pltpu.VMEM)
    hbm = pl.BlockSpec(memory_space=pltpu.HBM)
    shape = jax.ShapeDtypeStruct

    def prepare(*after):
        return call(
            prepare_ordered_kernel,
            (shape((block, block), F32), shape((classes, block), F32)),
            (batch_mask[0], bias_two[None], *after),
            specs=[vmem] * 2 + [pl.BlockSpec(memory_space=pl.ANY)] * len(after),
            scratch=[pltpu.VMEM((block, -(-classes // 128) * 128), F32)],
        )

    chips_one = [feat, *fetch_chips(feat, "row", n_row)]

    if dense_form:
        anywhere = pl.BlockSpec(memory_space=pl.ANY)
        chunks = 8
        dense = call(
            functools.partial(build_kernel, n_row, n_col, chunks),
            shape((n_col * block, n_row * block), BF16),
            (
                tile_count,
                pltpu.with_memory_space_constraint(coords, pltpu.HBM),
                pltpu.with_memory_space_constraint(tile_set, pltpu.HBM),
            ),
            specs=[smem, hbm, hbm],
            scratch=[
                pltpu.SMEM((2, slots), jnp.int32),
                pltpu.VMEM((slots, block, block), BF16),
                pltpu.VMEM((n_row * n_col + 1, block // 2, block), F32),
                pltpu.VMEM((n_row * n_col + 1, block // 2, block), F32),
                pltpu.SemaphoreType.DMA((chunks,)),
                pltpu.SemaphoreType.DMA(()),
            ],
            cost=pl.CostEstimate(
                flops=slots * block * block,
                bytes_accessed=2 * slots * block * block,
                transcendentals=0,
            ),
        )
        mine_one = call(
            join_rows_kernel,
            shape((n_row // 2 * block, f_in), BF16),
            (*chips_one, dense),
            specs=[vmem] * len(chips_one) + [anywhere],
        )
        other_one = fetch_core(mine_one, "row", n_row)
        mask_cols, bias_cols = prepare(mine_one)
        half_one = call(half_one_kernel, shape((n_col * block, f_in), F32), (dense, mine_one))
        parts_one = call(
            layer_one_kernel,
            [shape((block, f_in), BF16)] * n_col,
            (dense, half_one, other_one),
        )
    else:
        mask_cols, bias_cols = prepare()
        summed = call(
            functools.partial(tiles_kernel, n_row, n_col, False),
            shape((n_col, block, f_in), BF16),
            (coords, tile_count, tile_set, both_cores(jnp.stack(chips_one), "row", n_row)),
            specs=[smem, smem, vmem, vmem],
            scratch=[pltpu.VMEM((n_col, block, f_in), F32)],
        )
        parts_one = [summed[k] for k in range(n_col)]

    arrived_one = send_each(parts_one, "col", n_col)
    pushed, proj = call(
        functools.partial(hidden_kernel, n_col),
        (shape((block, hid), BF16), shape((classes, block), BF16)),
        (parts_one[0], *arrived_one, feat, weight_one, bias_one[None], w_two_t, mask_cols, hist),
    )
    chips_two = [proj, *fetch_chips(proj, "row", n_row)]
    if dense_form:
        near_other = permuted(proj, "row", n_row, 2)
        others_two = [fetch_core(x, "row", n_row) for x in chips_two[:-1]] + [near_other]
    pushed = call(write_kernel, shape((block, hid), BF16), (pushed,))

    if dense_form:
        early, late = chips_two[:-1], [chips_two[-1], *others_two]
        half_two = call(
            half_two_kernel,
            shape((classes, n_col * block), F32),
            (dense, *early),
            scratch=[pltpu.VMEM((classes, len(early) * block), BF16)],
        )
        parts_two = call(
            functools.partial(layer_two_kernel, n_col),
            [shape((classes, block), BF16)] * n_col,
            (dense, half_two, *late),
            scratch=[pltpu.VMEM((classes, len(late) * block), BF16)],
        )
    else:
        summed = call(
            functools.partial(tiles_kernel, n_row, n_col, True),
            shape((n_col, classes, block), BF16),
            (coords, tile_count, tile_set, both_cores(jnp.stack(chips_two), "row", n_row)),
            specs=[smem, smem, vmem, vmem],
            scratch=[pltpu.VMEM((n_col, classes, block), F32)],
        )
        parts_two = [summed[k] for k in range(n_col)]

    arrived_two = send_each(parts_two, "col", n_col)
    pieces = 4
    scores = call(
        functools.partial(logits_kernel, n_col, pieces),
        shape((classes, 1, block), F32),
        (parts_two[0], *arrived_two, proj, bias_cols),
        scratch=[pltpu.VMEM((classes, 1, block), F32), pltpu.SemaphoreType.DMA((pieces,))],
        out_specs=pl.BlockSpec(memory_space=pl.ANY),
    )
    return pushed[None, None], scores.transpose(1, 2, 0)[None]


def solution(mesh):
    sizes = mesh.shape
    return jax.shard_map(
        functools.partial(on_device, sizes["row"], sizes["col"]),
        mesh=mesh,
        in_specs=(
            P("row", "col", None, None),
            P("row", "col", None, None, None),
            P("row", "col", None, None),
            P("row", "col"),
            P("row", "col", None),
            P("row", "col", None, None),
            P(),
            P(),
            P(),
            P(),
        ),
        out_specs=(P("row", "col", None, None), P("row", "col", None, None)),
        check_vma=False,
    )
```

```python
import functools

import jax
import jax.numpy as jnp
from jax import lax
from jax.experimental import pallas as pl
from jax.experimental.pallas import tpu as pltpu
from jax.sharding import PartitionSpec as P

BF16 = jnp.bfloat16
F32 = jnp.float32
VMEM_LIMIT = 48 * 1024 * 1024


def partner(index, slot):
    return index ^ slot


def order(size):
    return [0, *range(5, size, 2), 3]


def column_order(size):
    return order(size) + [slot ^ 1 for slot in order(size)]


def permuted(block, axis, size, slot):
    return lax.ppermute(block, axis, [(i, partner(i, slot)) for i in range(size)])


def fetch_chips(block, axis, size):
    return [permuted(block, axis, size, slot) for slot in order(size)[1:]]


def fetch_core(blocks, axis, size):
    return permuted(blocks, axis, size, 1)


def both_cores(blocks, axis, size):
    found = jnp.concatenate([blocks, fetch_core(blocks, axis, size)])
    return found[jnp.argsort(jnp.array(column_order(size)))]


def send_each(blocks, axis, size):
    return [permuted(blocks[slot], axis, size, slot) for slot in reversed(range(1, size))]


def call(kernel, out_shape, operands, specs=None, scratch=(), cost=None, out_specs=None):
    vmem = pl.BlockSpec(memory_space=pltpu.VMEM)
    return pl.pallas_call(
        kernel,
        out_shape=out_shape,
        in_specs=specs or [vmem] * len(operands),
        out_specs=out_specs or jax.tree.map(lambda _: vmem, out_shape),
        scratch_shapes=list(scratch),
        cost_estimate=cost,
        compiler_params=pltpu.CompilerParams(vmem_limit_bytes=VMEM_LIMIT),
    )(*operands)


def dot_nt(left, right):
    return lax.dot_general(left, right, (((1,), (1,)), ((), ())), preferred_element_type=F32)


def build_kernel(
    n_row, n_col, chunks, count, coords_hbm, tiles_hbm, dense_ref, coords, tiles, first, second, sems, coords_sem
):
    slots, block = tiles.shape[0], tiles.shape[1]
    per, part = slots // chunks, block // 2
    copies = [
        pltpu.make_async_copy(
            tiles_hbm.at[pl.ds(i * per, per)], tiles.at[pl.ds(i * per, per)], sems.at[i]
        )
        for i in range(chunks)
    ]
    coords_copy = pltpu.make_async_copy(coords_hbm, coords, coords_sem)
    coords_copy.start()
    live = count[0, 0]
    for i, copy in enumerate(copies):
        pl.when(i * per < live)(copy.start)
    row, col = lax.axis_index("row"), lax.axis_index("col")
    first[...] = jnp.zeros_like(first)
    second[...] = jnp.zeros_like(second)
    coords_copy.wait()

    def place(t):
        at = partner(coords[0, t], col) * n_row + partner(coords[1, t], row)
        return jnp.where(t < live, at, n_row * n_col)

    for i in range(chunks):

        @pl.when(i * per < live)
        def _():
            copies[i].wait()

            @pl.loop(0, per, unroll=8)
            def _(step):
                t = i * per + step
                at = place(t)
                first[at] += tiles[t, :part].astype(F32)
                second[at] += tiles[t, part:].astype(F32)

    for k in range(n_col):
        for j, slot in enumerate(column_order(n_row)):
            at = k * n_row + slot
            columns = slice(j * block, (j + 1) * block)
            dense_ref[k * block : k * block + part, columns] = first[at].astype(BF16)
            dense_ref[k * block + part : (k + 1) * block, columns] = second[at].astype(BF16)


def prepare_ordered_kernel(mask, bias, *refs):
    mask_out, bias_out, wide = refs[-3:]
    block, classes = mask_out.shape[0], bias.shape[1]
    wide[...] = jnp.zeros_like(wide)
    mask_out[...] = jnp.broadcast_to(mask[...].astype(F32), (block, block)).T
    wide[:, :classes] = jnp.broadcast_to(bias[...], (block, classes))
    bias_out[...] = wide[...].T[:classes]


def join_rows_kernel(places, *refs):
    out = refs[-1]
    block = refs[0].shape[0]
    for ref, place in zip(refs, places):
        out[place * block : (place + 1) * block, :] = ref[...]


def half_one_kernel(dense_ref, mine_ref, out):
    half = mine_ref.shape[0]
    out[...] = jnp.dot(dense_ref[:, :half], mine_ref[...], preferred_element_type=F32)


def layer_one_kernel(dense_ref, first_ref, other_ref, *outputs):
    half, block = other_ref.shape[0], dense_ref.shape[0] // len(outputs)
    for k, out in enumerate(outputs):
        rows = pl.ds(k * block, block)
        total = jnp.dot(dense_ref[rows, half:], other_ref[...], preferred_element_type=F32)
        out[...] = (first_ref[rows, :] + total).astype(BF16)


def hidden_kernel(sends, *refs):
    parts = refs[:sends]
    feat, w_one, b_one, w_two, mask, history, pushed_ref, proj_ref = refs[sends:]
    total = feat[...].astype(F32)
    for part in parts:
        total += part[...].astype(F32)
    pre = jnp.dot(total.astype(BF16), w_one[...], preferred_element_type=F32) + b_one[...]
    hidden = jnp.maximum(pre, 0.0)
    chosen = jnp.concatenate([mask[...]] * (hidden.shape[1] // mask.shape[1]), axis=1) == 1.0
    pushed = jnp.where(chosen, hidden, history[...].astype(F32)).astype(BF16)
    pushed_ref[...] = pushed
    proj_ref[...] = dot_nt(w_two[...], pushed).astype(BF16)


def write_kernel(value, out):
    out[...] = value[...]


def lanes(refs, scratch):
    block = refs[0].shape[1]
    for i, ref in enumerate(refs):
        scratch[:, i * block : (i + 1) * block] = ref[...]
    return scratch[...]


def half_two_kernel(dense_ref, *refs):
    blocks, (out, scratch) = refs[:-2], refs[-2:]
    out[...] = dot_nt(lanes(blocks, scratch), dense_ref[:, : scratch.shape[1]])


def layer_two_kernel(n_col, dense_ref, first_ref, *refs):
    blocks, outputs, scratch = refs[: -n_col - 1], refs[-n_col - 1 : -1], refs[-1]
    block, at = blocks[0].shape[1], dense_ref.shape[1] - scratch.shape[1]
    rest = lanes(blocks, scratch)
    for k, out in enumerate(outputs):
        rows = pl.ds(k * block, block)
        out[...] = (first_ref[:, rows] + dot_nt(rest, dense_ref[rows, at:])).astype(BF16)


def logits_kernel(n_col, pieces, *refs):
    parts = refs[:n_col]
    proj, bias, out_hbm, staged, sems = refs[n_col:]
    step = -(-staged.shape[0] // pieces // 16) * 16
    copies = []
    for i in range(pieces):
        rows = slice(i * step, (i + 1) * step if i < pieces - 1 else staged.shape[0])
        total = proj[rows, :].astype(F32) + bias[rows, :]
        for part in parts:
            total += part[rows, :].astype(F32)
        staged[rows, 0, :] = total
        copies.append(pltpu.make_async_copy(staged.at[rows], out_hbm.at[rows], sems.at[i]))
        copies[-1].start()
    for copy in copies:
        copy.wait()


def tiles_kernel(
    n_row, n_col, transposed, coords_ref, count_ref, tiles_ref, stacked_ref, out_ref, total
):
    row, col = lax.axis_index("row"), lax.axis_index("col")
    total[...] = jnp.zeros_like(total)

    @pl.loop(0, count_ref[0, 0])
    def _(t):
        k = partner(coords_ref[0, t], col)
        j = partner(coords_ref[1, t], row)
        if transposed:
            total[k] += dot_nt(stacked_ref[j], tiles_ref[t])
        else:
            total[k] += jnp.dot(tiles_ref[t], stacked_ref[j], preferred_element_type=F32)

    out_ref[...] = total[...].astype(BF16)


def on_device(
    n_row, n_col,
    features, tiles, tile_coords, tile_count, batch_mask, history,
    weight_one, bias_one, weight_two, bias_two,
):
    feat, tile_set, hist = features[0, 0], tiles[0, 0], history[0, 0]
    coords = tile_coords[0, 0].T
    slots, block = tile_set.shape[0], tile_set.shape[1]
    f_in, hid, classes = feat.shape[1], weight_one.shape[1], weight_two.shape[1]
    w_two_t = weight_two.T
    dense_form = n_row * n_col <= slots
    smem = pl.BlockSpec(memory_space=pltpu.SMEM)
    vmem = pl.BlockSpec(memory_space=pltpu.VMEM)
    hbm = pl.BlockSpec(memory_space=pltpu.HBM)
    shape = jax.ShapeDtypeStruct

    def prepare(*after):
        return call(
            prepare_ordered_kernel,
            (shape((block, block), F32), shape((classes, block), F32)),
            (batch_mask[0], bias_two[None], *after),
            specs=[vmem] * 2 + [pl.BlockSpec(memory_space=pl.ANY)] * len(after),
            scratch=[pltpu.VMEM((block, -(-classes // 128) * 128), F32)],
        )

    chips_one = [feat, *fetch_chips(feat, "row", n_row)]

    if dense_form:
        anywhere = pl.BlockSpec(memory_space=pl.ANY)
        chunks = 8
        dense = call(
            functools.partial(build_kernel, n_row, n_col, chunks),
            shape((n_col * block, n_row * block), BF16),
            (
                tile_count,
                pltpu.with_memory_space_constraint(coords, pltpu.HBM),
                pltpu.with_memory_space_constraint(tile_set, pltpu.HBM),
            ),
            specs=[smem, hbm, hbm],
            scratch=[
                pltpu.SMEM((2, slots), jnp.int32),
                pltpu.VMEM((slots, block, block), BF16),
                pltpu.VMEM((n_row * n_col + 1, block // 2, block), F32),
                pltpu.VMEM((n_row * n_col + 1, block // 2, block), F32),
                pltpu.SemaphoreType.DMA((chunks,)),
                pltpu.SemaphoreType.DMA(()),
            ],
            cost=pl.CostEstimate(
                flops=slots * block * block,
                bytes_accessed=2 * slots * block * block,
                transcendentals=0,
            ),
        )
        by_distance = sorted(range(n_row // 2), key=lambda i: order(n_row)[i])
        mine_one = call(
            functools.partial(join_rows_kernel, by_distance),
            shape((n_row // 2 * block, f_in), BF16),
            (*[chips_one[i] for i in by_distance], dense),
            specs=[vmem] * len(chips_one) + [anywhere],
        )
        other_one = fetch_core(mine_one, "row", n_row)
        mask_cols, bias_cols = prepare(mine_one)
        half_one = call(half_one_kernel, shape((n_col * block, f_in), F32), (dense, mine_one))
        parts_one = call(
            layer_one_kernel,
            [shape((block, f_in), BF16)] * n_col,
            (dense, half_one, other_one),
        )
    else:
        mask_cols, bias_cols = prepare()
        summed = call(
            functools.partial(tiles_kernel, n_row, n_col, False),
            shape((n_col, block, f_in), BF16),
            (coords, tile_count, tile_set, both_cores(jnp.stack(chips_one), "row", n_row)),
            specs=[smem, smem, vmem, vmem],
            scratch=[pltpu.VMEM((n_col, block, f_in), F32)],
        )
        parts_one = [summed[k] for k in range(n_col)]

    arrived_one = send_each(parts_one, "col", n_col)
    pushed, proj = call(
        functools.partial(hidden_kernel, n_col),
        (shape((block, hid), BF16), shape((classes, block), BF16)),
        (parts_one[0], *arrived_one, feat, weight_one, bias_one[None], w_two_t, mask_cols, hist),
    )
    chips_two = [proj, *fetch_chips(proj, "row", n_row)]
    if dense_form:
        near_other = permuted(proj, "row", n_row, 2)
        others_two = [fetch_core(x, "row", n_row) for x in chips_two[:-1]] + [near_other]
    pushed = call(write_kernel, shape((block, hid), BF16), (pushed,))

    if dense_form:
        early, late = chips_two[:-1], [chips_two[-1], *others_two]
        half_two = call(
            half_two_kernel,
            shape((classes, n_col * block), F32),
            (dense, *early),
            scratch=[pltpu.VMEM((classes, len(early) * block), BF16)],
        )
        parts_two = call(
            functools.partial(layer_two_kernel, n_col),
            [shape((classes, block), BF16)] * n_col,
            (dense, half_two, *late),
            scratch=[pltpu.VMEM((classes, len(late) * block), BF16)],
        )
    else:
        summed = call(
            functools.partial(tiles_kernel, n_row, n_col, True),
            shape((n_col, classes, block), BF16),
            (coords, tile_count, tile_set, both_cores(jnp.stack(chips_two), "row", n_row)),
            specs=[smem, smem, vmem, vmem],
            scratch=[pltpu.VMEM((n_col, classes, block), F32)],
        )
        parts_two = [summed[k] for k in range(n_col)]

    arrived_two = send_each(parts_two, "col", n_col)
    pieces = 4
    scores = call(
        functools.partial(logits_kernel, n_col, pieces),
        shape((classes, 1, block), F32),
        (parts_two[0], *arrived_two, proj, bias_cols),
        scratch=[pltpu.VMEM((classes, 1, block), F32), pltpu.SemaphoreType.DMA((pieces,))],
        out_specs=pl.BlockSpec(memory_space=pl.ANY),
    )
    return pushed[None, None], scores.transpose(1, 2, 0)[None]


def solution(mesh):
    sizes = mesh.shape
    return jax.shard_map(
        functools.partial(on_device, sizes["row"], sizes["col"]),
        mesh=mesh,
        in_specs=(
            P("row", "col", None, None),
            P("row", "col", None, None, None),
            P("row", "col", None, None),
            P("row", "col"),
            P("row", "col", None),
            P("row", "col", None, None),
            P(),
            P(),
            P(),
            P(),
        ),
        out_specs=(P("row", "col", None, None), P("row", "col", None, None)),
        check_vma=False,
    )
```

```python
import functools

import jax
import jax.numpy as jnp
from jax import lax
from jax.experimental import pallas as pl
from jax.experimental.pallas import tpu as pltpu
from jax.sharding import PartitionSpec as P

BF16 = jnp.bfloat16
F32 = jnp.float32
VMEM_LIMIT = 48 * 1024 * 1024


def partner(index, slot):
    return index ^ slot


def order(size):
    return [0, *range(5, size, 2), 3]


def column_order(size):
    return order(size) + [slot ^ 1 for slot in order(size)]


def permuted(block, axis, size, slot):
    return lax.ppermute(block, axis, [(i, partner(i, slot)) for i in range(size)])


def fetch_chips(block, axis, size):
    return [permuted(block, axis, size, slot) for slot in order(size)[1:]]


def fetch_core(blocks, axis, size):
    return permuted(blocks, axis, size, 1)


def both_cores(blocks, axis, size):
    found = jnp.concatenate([blocks, fetch_core(blocks, axis, size)])
    return found[jnp.argsort(jnp.array(column_order(size)))]


def send_across(blocks, n_row, n_col):
    arrived = []
    for slot in reversed(range(n_col)):
        pairs = [
            (row * n_col + col, partner(row, 1) * n_col + partner(col, slot))
            for row in range(n_row)
            for col in range(n_col)
        ]
        arrived.append(lax.ppermute(blocks[slot], ("row", "col"), pairs))
    return arrived


def send_each(blocks, axis, size):
    return [permuted(blocks[slot], axis, size, slot) for slot in reversed(range(1, size))]


def call(kernel, out_shape, operands, specs=None, scratch=(), cost=None, out_specs=None):
    vmem = pl.BlockSpec(memory_space=pltpu.VMEM)
    return pl.pallas_call(
        kernel,
        out_shape=out_shape,
        in_specs=specs or [vmem] * len(operands),
        out_specs=out_specs or jax.tree.map(lambda _: vmem, out_shape),
        scratch_shapes=list(scratch),
        cost_estimate=cost,
        compiler_params=pltpu.CompilerParams(vmem_limit_bytes=VMEM_LIMIT),
    )(*operands)


def dot_nt(left, right):
    return lax.dot_general(left, right, (((1,), (1,)), ((), ())), preferred_element_type=F32)


def build_kernel(
    n_row, n_col, chunks, count, coords_hbm, tiles_hbm, dense_ref, coords, tiles, first, second, sems, coords_sem
):
    slots, block = tiles.shape[0], tiles.shape[1]
    per, part = slots // chunks, block // 2
    copies = [
        pltpu.make_async_copy(
            tiles_hbm.at[pl.ds(i * per, per)], tiles.at[pl.ds(i * per, per)], sems.at[i]
        )
        for i in range(chunks)
    ]
    coords_copy = pltpu.make_async_copy(coords_hbm, coords, coords_sem)
    coords_copy.start()
    live = count[0, 0]
    for i, copy in enumerate(copies):
        pl.when(i * per < live)(copy.start)
    row, col = lax.axis_index("row"), lax.axis_index("col")
    first[...] = jnp.zeros_like(first)
    second[...] = jnp.zeros_like(second)
    coords_copy.wait()

    def place(t):
        at = partner(coords[0, t], col) * n_row + partner(coords[1, t], row)
        return jnp.where(t < live, at, n_row * n_col)

    for i in range(chunks):

        @pl.when(i * per < live)
        def _():
            copies[i].wait()

            @pl.loop(0, per, unroll=8)
            def _(step):
                t = i * per + step
                at = place(t)
                first[at] += tiles[t, :part].astype(F32)
                second[at] += tiles[t, part:].astype(F32)

    for k in range(n_col):
        for j, slot in enumerate(column_order(n_row)):
            at = k * n_row + slot
            columns = slice(j * block, (j + 1) * block)
            dense_ref[k * block : k * block + part, columns] = first[at].astype(BF16)
            dense_ref[k * block + part : (k + 1) * block, columns] = second[at].astype(BF16)


def prepare_kernel(mask, bias, history, *refs):
    kept_out, bias_out, wide = refs[-3:]
    block, classes = history.shape[0], bias.shape[1]
    mask_cols = jnp.broadcast_to(mask[...].astype(F32), (block, block)).T
    chosen = jnp.concatenate([mask_cols] * (history.shape[1] // block), axis=1) == 1.0
    kept_out[...] = jnp.where(chosen, -1.0, history[...].astype(F32)).astype(BF16)
    wide[...] = jnp.zeros_like(wide)
    wide[:, :classes] = jnp.broadcast_to(bias[...], (block, classes))
    bias_out[...] = wide[...].T[:classes]


def join_rows_kernel(places, *refs):
    out = refs[-1]
    block = refs[0].shape[0]
    for ref, place in zip(refs, places):
        out[place * block : (place + 1) * block, :] = ref[...]


def half_one_kernel(dense_ref, mine_ref, out):
    half = mine_ref.shape[0]
    out[...] = jnp.dot(dense_ref[:, :half], mine_ref[...], preferred_element_type=F32)


def layer_one_kernel(dense_ref, first_ref, other_ref, *outputs):
    half, block = other_ref.shape[0], dense_ref.shape[0] // len(outputs)
    for k, out in enumerate(outputs):
        rows = pl.ds(k * block, block)
        total = jnp.dot(dense_ref[rows, half:], other_ref[...], preferred_element_type=F32)
        out[...] = (first_ref[rows, :] + total).astype(BF16)


def hidden_kernel(n_col, *refs):
    parts = refs[:n_col]
    feats, w_one, b_one, w_two, kept, pushed_ref, proj_ref = refs[n_col:]
    total = feats[: kept.shape[0], :].astype(F32)
    for part in parts:
        total += part[...].astype(F32)
    pre = jnp.dot(total.astype(BF16), w_one[...], preferred_element_type=F32) + b_one[...]
    hidden = jnp.maximum(pre, 0.0)
    old = kept[...].astype(F32)
    pushed = jnp.where(old < 0.0, hidden, old).astype(BF16)
    pushed_ref[...] = pushed
    proj_ref[...] = dot_nt(w_two[...], pushed).astype(BF16)


def write_kernel(value, out):
    out[...] = value[...]


def lanes(refs, scratch):
    block = refs[0].shape[1]
    for i, ref in enumerate(refs):
        scratch[:, i * block : (i + 1) * block] = ref[...]
    return scratch[...]


def half_two_kernel(dense_ref, *refs):
    blocks, (out, scratch) = refs[:-2], refs[-2:]
    half = dense_ref.shape[1] // 2
    out[...] = dot_nt(lanes(blocks, scratch), dense_ref[:, half : half + scratch.shape[1]])


def layer_two_kernel(n_col, dense_ref, first_ref, near_ref, *refs):
    blocks, outputs, scratch = refs[: -n_col - 1], refs[-n_col - 1 : -1], refs[-1]
    block, half = near_ref.shape[1], scratch.shape[1]
    rest = lanes(blocks, scratch)
    for k, out in enumerate(outputs):
        rows = pl.ds(k * block, block)
        total = first_ref[:, rows] + dot_nt(rest, dense_ref[rows, :half])
        total += dot_nt(near_ref[...], dense_ref[rows, dense_ref.shape[1] - block :])
        out[...] = total.astype(BF16)


def logits_kernel(n_col, pieces, *refs):
    parts = refs[:n_col]
    proj, bias, out_hbm, staged, sems = refs[n_col:]
    step = -(-staged.shape[0] // pieces // 16) * 16
    copies = []
    for i in range(pieces):
        rows = slice(i * step, (i + 1) * step if i < pieces - 1 else staged.shape[0])
        total = proj[rows, :].astype(F32) + bias[rows, :]
        for part in parts:
            total += part[rows, :].astype(F32)
        staged[rows, 0, :] = total
        copies.append(pltpu.make_async_copy(staged.at[rows], out_hbm.at[rows], sems.at[i]))
        copies[-1].start()
    for copy in copies:
        copy.wait()


def tiles_kernel(
    n_row, n_col, transposed, coords_ref, count_ref, tiles_ref, stacked_ref, out_ref, total
):
    row, col = lax.axis_index("row"), lax.axis_index("col")
    total[...] = jnp.zeros_like(total)

    @pl.loop(0, count_ref[0, 0])
    def _(t):
        k = partner(coords_ref[0, t], col)
        j = partner(coords_ref[1, t], row)
        if transposed:
            total[k] += dot_nt(stacked_ref[j], tiles_ref[t])
        else:
            total[k] += jnp.dot(tiles_ref[t], stacked_ref[j], preferred_element_type=F32)

    out_ref[...] = total[...].astype(BF16)


def on_device(
    n_row, n_col,
    features, tiles, tile_coords, tile_count, batch_mask, history,
    weight_one, bias_one, weight_two, bias_two,
):
    feat, tile_set, hist = features[0, 0], tiles[0, 0], history[0, 0]
    coords = tile_coords[0, 0].T
    slots, block = tile_set.shape[0], tile_set.shape[1]
    f_in, hid, classes = feat.shape[1], weight_one.shape[1], weight_two.shape[1]
    w_two_t = weight_two.T
    dense_form = n_row * n_col <= slots
    smem = pl.BlockSpec(memory_space=pltpu.SMEM)
    vmem = pl.BlockSpec(memory_space=pltpu.VMEM)
    hbm = pl.BlockSpec(memory_space=pltpu.HBM)
    shape = jax.ShapeDtypeStruct

    def prepare(*after):
        return call(
            prepare_kernel,
            (shape((block, hid), BF16), shape((classes, block), F32)),
            (batch_mask[0], bias_two[None], hist, *after),
            specs=[vmem] * 3 + [pl.BlockSpec(memory_space=pl.ANY)] * len(after),
            scratch=[pltpu.VMEM((block, -(-classes // 128) * 128), F32)],
        )

    chips_one = [feat, *fetch_chips(feat, "row", n_row)]

    if dense_form:
        anywhere = pl.BlockSpec(memory_space=pl.ANY)
        chunks = 8
        dense = call(
            functools.partial(build_kernel, n_row, n_col, chunks),
            shape((n_col * block, n_row * block), BF16),
            (
                tile_count,
                pltpu.with_memory_space_constraint(coords, pltpu.HBM),
                pltpu.with_memory_space_constraint(tile_set, pltpu.HBM),
            ),
            specs=[smem, hbm, hbm],
            scratch=[
                pltpu.SMEM((2, slots), jnp.int32),
                pltpu.VMEM((slots, block, block), BF16),
                pltpu.VMEM((n_row * n_col + 1, block // 2, block), F32),
                pltpu.VMEM((n_row * n_col + 1, block // 2, block), F32),
                pltpu.SemaphoreType.DMA((chunks,)),
                pltpu.SemaphoreType.DMA(()),
            ],
            cost=pl.CostEstimate(
                flops=slots * block * block,
                bytes_accessed=2 * slots * block * block,
                transcendentals=0,
            ),
        )
        by_distance = sorted(range(n_row // 2), key=lambda i: order(n_row)[i])
        mine_one = call(
            functools.partial(join_rows_kernel, by_distance),
            shape((n_row // 2 * block, f_in), BF16),
            (*[chips_one[i] for i in by_distance], dense),
            specs=[vmem] * len(chips_one) + [anywhere],
        )
        other_one = fetch_core(mine_one, "row", n_row)
        kept, bias_cols = prepare(mine_one)
        half_one = call(half_one_kernel, shape((n_col * block, f_in), F32), (dense, mine_one))
        parts_one = call(
            layer_one_kernel,
            [shape((block, f_in), BF16)] * n_col,
            (dense, half_one, other_one),
        )
    else:
        kept, bias_cols = prepare()
        summed = call(
            functools.partial(tiles_kernel, n_row, n_col, False),
            shape((n_col, block, f_in), BF16),
            (coords, tile_count, tile_set, both_cores(jnp.stack(chips_one), "row", n_row)),
            specs=[smem, smem, vmem, vmem],
            scratch=[pltpu.VMEM((n_col, block, f_in), F32)],
        )
        parts_one = [summed[k] for k in range(n_col)]
        other_one = fetch_core(feat, "row", n_row)

    arrived_one = send_across(parts_one, n_row, n_col)
    kept = fetch_core(kept, "row", n_row)
    pushed, proj = call(
        functools.partial(hidden_kernel, n_col),
        (shape((block, hid), BF16), shape((classes, block), BF16)),
        (*arrived_one, other_one, weight_one, bias_one[None], w_two_t, kept),
    )
    chips_two = [proj, *fetch_chips(proj, "row", n_row)]
    if dense_form:
        near_other = permuted(proj, "row", n_row, 2)
        others_two = [fetch_core(x, "row", n_row) for x in chips_two[:-1]] + [near_other]
        own_proj = others_two[0]
    else:
        own_proj = fetch_core(proj, "row", n_row)
    pushed = fetch_core(pushed, "row", n_row)
    pushed = call(write_kernel, shape((block, hid), BF16), (pushed,))

    if dense_form:
        early, near, late = chips_two[:-1], chips_two[-1], others_two
        half_two = call(
            half_two_kernel,
            shape((classes, n_col * block), F32),
            (dense, *early),
            scratch=[pltpu.VMEM((classes, len(early) * block), BF16)],
        )
        parts_two = call(
            functools.partial(layer_two_kernel, n_col),
            [shape((classes, block), BF16)] * n_col,
            (dense, half_two, near, *late),
            scratch=[pltpu.VMEM((classes, len(late) * block), BF16)],
        )
    else:
        other_slots = jnp.arange(n_row) ^ 1
        summed = call(
            functools.partial(tiles_kernel, n_row, n_col, True),
            shape((n_col, classes, block), BF16),
            (coords, tile_count, tile_set, both_cores(jnp.stack(chips_two), "row", n_row)[other_slots]),
            specs=[smem, smem, vmem, vmem],
            scratch=[pltpu.VMEM((n_col, classes, block), F32)],
        )
        parts_two = [summed[k] for k in range(n_col)]

    arrived_two = send_each(parts_two, "col", n_col)
    pieces = 4
    scores = call(
        functools.partial(logits_kernel, n_col, pieces),
        shape((classes, 1, block), F32),
        (parts_two[0], *arrived_two, own_proj, bias_cols),
        scratch=[pltpu.VMEM((classes, 1, block), F32), pltpu.SemaphoreType.DMA((pieces,))],
        out_specs=pl.BlockSpec(memory_space=pl.ANY),
    )
    return pushed[None, None], scores.transpose(1, 2, 0)[None]


def solution(mesh):
    sizes = mesh.shape
    return jax.shard_map(
        functools.partial(on_device, sizes["row"], sizes["col"]),
        mesh=mesh,
        in_specs=(
            P("row", "col", None, None),
            P("row", "col", None, None, None),
            P("row", "col", None, None),
            P("row", "col"),
            P("row", "col", None),
            P("row", "col", None, None),
            P(),
            P(),
            P(),
            P(),
        ),
        out_specs=(P("row", "col", None, None), P("row", "col", None, None)),
        check_vma=False,
    )
```

```python
import functools

import jax
import jax.numpy as jnp
from jax import lax
from jax.experimental import pallas as pl
from jax.experimental.pallas import tpu as pltpu
from jax.sharding import PartitionSpec as P

BF16 = jnp.bfloat16
F32 = jnp.float32
VMEM_LIMIT = 48 * 1024 * 1024


def partner(index, slot):
    return index ^ slot


def order(size):
    return [0, *range(5, size, 2), 3]


def column_order(size):
    return order(size) + [slot ^ 1 for slot in order(size)]


def permuted(block, axis, size, slot):
    return lax.ppermute(block, axis, [(i, partner(i, slot)) for i in range(size)])


def fetch_chips(block, axis, size):
    return [permuted(block, axis, size, slot) for slot in order(size)[1:]]


def fetch_core(blocks, axis, size):
    return permuted(blocks, axis, size, 1)


def both_cores(blocks, axis, size):
    found = jnp.concatenate([blocks, fetch_core(blocks, axis, size)])
    return found[jnp.argsort(jnp.array(column_order(size)))]


def send_across(blocks, n_row, n_col):
    arrived = []
    for slot in reversed(range(n_col)):
        pairs = [
            (row * n_col + col, partner(row, 1) * n_col + partner(col, slot))
            for row in range(n_row)
            for col in range(n_col)
        ]
        arrived.append(lax.ppermute(blocks[slot], ("row", "col"), pairs))
    return arrived


def send_each(blocks, axis, size):
    return [permuted(blocks[slot], axis, size, slot) for slot in reversed(range(1, size))]


def call(kernel, out_shape, operands, specs=None, scratch=(), cost=None, out_specs=None):
    vmem = pl.BlockSpec(memory_space=pltpu.VMEM)
    return pl.pallas_call(
        kernel,
        out_shape=out_shape,
        in_specs=specs or [vmem] * len(operands),
        out_specs=out_specs or jax.tree.map(lambda _: vmem, out_shape),
        scratch_shapes=list(scratch),
        cost_estimate=cost,
        compiler_params=pltpu.CompilerParams(vmem_limit_bytes=VMEM_LIMIT),
    )(*operands)


def dot_nt(left, right):
    return lax.dot_general(left, right, (((1,), (1,)), ((), ())), preferred_element_type=F32)


def build_kernel(
    n_row, n_col, chunks, count, coords_hbm, tiles_hbm, dense_ref, coords, tiles, first, second, sems, coords_sem
):
    slots, block = tiles.shape[0], tiles.shape[1]
    per, part = slots // chunks, block // 2
    copies = [
        pltpu.make_async_copy(
            tiles_hbm.at[pl.ds(i * per, per)], tiles.at[pl.ds(i * per, per)], sems.at[i]
        )
        for i in range(chunks)
    ]
    coords_copy = pltpu.make_async_copy(coords_hbm, coords, coords_sem)
    coords_copy.start()
    live = count[0, 0]
    for i, copy in enumerate(copies):
        pl.when(i * per < live)(copy.start)
    row, col = lax.axis_index("row"), lax.axis_index("col")
    first[...] = jnp.zeros_like(first)
    second[...] = jnp.zeros_like(second)
    coords_copy.wait()

    def place(t):
        at = partner(coords[0, t], col) * n_row + partner(coords[1, t], row)
        return jnp.where(t < live, at, n_row * n_col)

    for i in range(chunks):

        @pl.when(i * per < live)
        def _():
            copies[i].wait()

            @pl.loop(0, per, unroll=8)
            def _(step):
                t = i * per + step
                at = place(t)
                first[at] += tiles[t, :part].astype(F32)
                second[at] += tiles[t, part:].astype(F32)

    for k in range(n_col):
        for j, slot in enumerate(column_order(n_row)):
            at = k * n_row + slot
            columns = slice(j * block, (j + 1) * block)
            dense_ref[k * block : k * block + part, columns] = first[at].astype(BF16)
            dense_ref[k * block + part : (k + 1) * block, columns] = second[at].astype(BF16)


def prepare_kernel(mask, bias, history, *refs):
    kept_out, bias_out, wide = refs[-3:]
    block, classes = history.shape[0], bias.shape[1]
    mask_cols = jnp.broadcast_to(mask[...].astype(F32), (block, block)).T
    chosen = jnp.concatenate([mask_cols] * (history.shape[1] // block), axis=1) == 1.0
    kept_out[...] = jnp.where(chosen, -1.0, history[...].astype(F32)).astype(BF16)
    wide[...] = jnp.zeros_like(wide)
    wide[:, :classes] = jnp.broadcast_to(bias[...], (block, classes))
    bias_out[...] = wide[...].T[:classes]


def join_rows_kernel(places, *refs):
    out = refs[-1]
    block = refs[0].shape[0]
    for ref, place in zip(refs, places):
        out[place * block : (place + 1) * block, :] = ref[...]


def half_one_kernel(dense_ref, mine_ref, out):
    half = mine_ref.shape[0]
    out[...] = jnp.dot(dense_ref[:, :half], mine_ref[...], preferred_element_type=F32)


def layer_one_kernel(dense_ref, first_ref, other_ref, *outputs):
    half, block = other_ref.shape[0], dense_ref.shape[0] // len(outputs)
    for k, out in enumerate(outputs):
        rows = pl.ds(k * block, block)
        total = jnp.dot(dense_ref[rows, half:], other_ref[...], preferred_element_type=F32)
        out[...] = (first_ref[rows, :] + total).astype(BF16)


def hidden_kernel(n_col, *refs):
    parts = refs[:n_col]
    feats, w_one, b_one, w_two, kept, pushed_ref, proj_ref = refs[n_col:]
    total = feats[: kept.shape[0], :].astype(F32)
    for part in parts:
        total += part[...].astype(F32)
    pre = jnp.dot(total.astype(BF16), w_one[...], preferred_element_type=F32) + b_one[...]
    hidden = jnp.maximum(pre, 0.0)
    old = kept[...].astype(F32)
    pushed = jnp.where(old < 0.0, hidden, old).astype(BF16)
    pushed_ref[...] = pushed
    proj_ref[...] = dot_nt(w_two[...], pushed).astype(BF16)


def write_kernel(value, out):
    out[...] = value[...]


def late_kernel(value, after, out):
    del after
    out[...] = value[...]


def lanes(refs, scratch):
    block = refs[0].shape[1]
    for i, ref in enumerate(refs):
        scratch[:, i * block : (i + 1) * block] = ref[...]
    return scratch[...]


def half_two_kernel(dense_ref, *refs):
    blocks, (out, scratch) = refs[:-2], refs[-2:]
    half = dense_ref.shape[1] // 2
    out[...] = dot_nt(lanes(blocks, scratch), dense_ref[:, half : half + scratch.shape[1]])


def layer_two_kernel(n_col, dense_ref, first_ref, own_ref, near_ref, *refs):
    blocks, outputs, scratch = refs[: -n_col - 1], refs[-n_col - 1 : -1], refs[-1]
    block, half = near_ref.shape[1], scratch.shape[1]
    rest = lanes([own_ref, *blocks], scratch)
    for k, out in enumerate(outputs):
        rows = pl.ds(k * block, block)
        total = first_ref[:, rows] + dot_nt(rest, dense_ref[rows, :half])
        total += dot_nt(near_ref[...], dense_ref[rows, dense_ref.shape[1] - block :])
        out[...] = total.astype(BF16)


def logits_kernel(n_col, pieces, *refs):
    parts = refs[:n_col]
    proj, bias, out_hbm, staged, sems = refs[n_col:]
    step = -(-staged.shape[0] // pieces // 16) * 16
    copies = []
    for i in range(pieces):
        rows = slice(i * step, (i + 1) * step if i < pieces - 1 else staged.shape[0])
        total = proj[rows, :].astype(F32) + bias[rows, :]
        for part in parts:
            total += part[rows, :].astype(F32)
        staged[rows, 0, :] = total
        copies.append(pltpu.make_async_copy(staged.at[rows], out_hbm.at[rows], sems.at[i]))
        copies[-1].start()
    for copy in copies:
        copy.wait()


def tiles_kernel(
    n_row, n_col, transposed, coords_ref, count_ref, tiles_ref, stacked_ref, out_ref, total
):
    row, col = lax.axis_index("row"), lax.axis_index("col")
    total[...] = jnp.zeros_like(total)

    @pl.loop(0, count_ref[0, 0])
    def _(t):
        k = partner(coords_ref[0, t], col)
        j = partner(coords_ref[1, t], row)
        if transposed:
            total[k] += dot_nt(stacked_ref[j], tiles_ref[t])
        else:
            total[k] += jnp.dot(tiles_ref[t], stacked_ref[j], preferred_element_type=F32)

    out_ref[...] = total[...].astype(BF16)


def on_device(
    n_row, n_col,
    features, tiles, tile_coords, tile_count, batch_mask, history,
    weight_one, bias_one, weight_two, bias_two,
):
    feat, tile_set, hist = features[0, 0], tiles[0, 0], history[0, 0]
    coords = tile_coords[0, 0].T
    slots, block = tile_set.shape[0], tile_set.shape[1]
    f_in, hid, classes = feat.shape[1], weight_one.shape[1], weight_two.shape[1]
    w_two_t = weight_two.T
    dense_form = n_row * n_col <= slots
    smem = pl.BlockSpec(memory_space=pltpu.SMEM)
    vmem = pl.BlockSpec(memory_space=pltpu.VMEM)
    hbm = pl.BlockSpec(memory_space=pltpu.HBM)
    shape = jax.ShapeDtypeStruct

    def prepare(*after):
        return call(
            prepare_kernel,
            (shape((block, hid), BF16), shape((classes, block), F32)),
            (batch_mask[0], bias_two[None], hist, *after),
            specs=[vmem] * 3 + [pl.BlockSpec(memory_space=pl.ANY)] * len(after),
            scratch=[pltpu.VMEM((block, -(-classes // 128) * 128), F32)],
        )

    chips_one = [feat, *fetch_chips(feat, "row", n_row)]

    if dense_form:
        anywhere = pl.BlockSpec(memory_space=pl.ANY)
        chunks = 8
        dense = call(
            functools.partial(build_kernel, n_row, n_col, chunks),
            shape((n_col * block, n_row * block), BF16),
            (
                tile_count,
                pltpu.with_memory_space_constraint(coords, pltpu.HBM),
                pltpu.with_memory_space_constraint(tile_set, pltpu.HBM),
            ),
            specs=[smem, hbm, hbm],
            scratch=[
                pltpu.SMEM((2, slots), jnp.int32),
                pltpu.VMEM((slots, block, block), BF16),
                pltpu.VMEM((n_row * n_col + 1, block // 2, block), F32),
                pltpu.VMEM((n_row * n_col + 1, block // 2, block), F32),
                pltpu.SemaphoreType.DMA((chunks,)),
                pltpu.SemaphoreType.DMA(()),
            ],
            cost=pl.CostEstimate(
                flops=slots * block * block,
                bytes_accessed=2 * slots * block * block,
                transcendentals=0,
            ),
        )
        by_distance = sorted(range(n_row // 2), key=lambda i: order(n_row)[i])
        mine_one = call(
            functools.partial(join_rows_kernel, by_distance),
            shape((n_row // 2 * block, f_in), BF16),
            (*[chips_one[i] for i in by_distance], dense),
            specs=[vmem] * len(chips_one) + [anywhere],
        )
        other_one = fetch_core(mine_one, "row", n_row)
        kept, bias_cols = prepare(mine_one)
        half_one = call(half_one_kernel, shape((n_col * block, f_in), F32), (dense, mine_one))
        parts_one = call(
            layer_one_kernel,
            [shape((block, f_in), BF16)] * n_col,
            (dense, half_one, other_one),
        )
    else:
        kept, bias_cols = prepare()
        summed = call(
            functools.partial(tiles_kernel, n_row, n_col, False),
            shape((n_col, block, f_in), BF16),
            (coords, tile_count, tile_set, both_cores(jnp.stack(chips_one), "row", n_row)),
            specs=[smem, smem, vmem, vmem],
            scratch=[pltpu.VMEM((n_col, block, f_in), F32)],
        )
        parts_one = [summed[k] for k in range(n_col)]
        other_one = fetch_core(feat, "row", n_row)

    arrived_one = send_across(parts_one, n_row, n_col)
    kept = fetch_core(kept, "row", n_row)
    pushed, proj = call(
        functools.partial(hidden_kernel, n_col),
        (shape((block, hid), BF16), shape((classes, block), BF16)),
        (*arrived_one, other_one, weight_one, bias_one[None], w_two_t, kept),
    )
    chips_two = [proj, *fetch_chips(proj, "row", n_row)]
    if dense_form:
        near_other = permuted(proj, "row", n_row, 2)
        others_two = [fetch_core(x, "row", n_row) for x in chips_two[:-1]] + [near_other]
        own_proj = others_two[0]
    else:
        own_proj = fetch_core(proj, "row", n_row)

    if dense_form:
        early, near, late = chips_two[:-1], chips_two[-1], others_two
        half_two = call(
            half_two_kernel,
            shape((classes, n_col * block), F32),
            (dense, *early),
            scratch=[pltpu.VMEM((classes, len(early) * block), BF16)],
        )
        pushed = call(
            late_kernel, shape((block, hid), BF16), (pushed, half_two), specs=[vmem, anywhere]
        )
        parts_two = call(
            functools.partial(layer_two_kernel, n_col),
            [shape((classes, block), BF16)] * n_col,
            (dense, half_two, late[0], near, *late[1:]),
            scratch=[pltpu.VMEM((classes, len(late) * block), BF16)],
        )
    else:
        other_slots = jnp.arange(n_row) ^ 1
        summed = call(
            functools.partial(tiles_kernel, n_row, n_col, True),
            shape((n_col, classes, block), BF16),
            (coords, tile_count, tile_set, both_cores(jnp.stack(chips_two), "row", n_row)[other_slots]),
            specs=[smem, smem, vmem, vmem],
            scratch=[pltpu.VMEM((n_col, classes, block), F32)],
        )
        parts_two = [summed[k] for k in range(n_col)]

    arrived_two = send_each(parts_two, "col", n_col)
    pushed = call(write_kernel, shape((block, hid), BF16), (fetch_core(pushed, "row", n_row),))
    pieces = 4
    scores = call(
        functools.partial(logits_kernel, n_col, pieces),
        shape((classes, 1, block), F32),
        (parts_two[0], *arrived_two, own_proj, bias_cols),
        scratch=[pltpu.VMEM((classes, 1, block), F32), pltpu.SemaphoreType.DMA((pieces,))],
        out_specs=pl.BlockSpec(memory_space=pl.ANY),
    )
    return pushed[None, None], scores.transpose(1, 2, 0)[None]


def solution(mesh):
    sizes = mesh.shape
    return jax.shard_map(
        functools.partial(on_device, sizes["row"], sizes["col"]),
        mesh=mesh,
        in_specs=(
            P("row", "col", None, None),
            P("row", "col", None, None, None),
            P("row", "col", None, None),
            P("row", "col"),
            P("row", "col", None),
            P("row", "col", None, None),
            P(),
            P(),
            P(),
            P(),
        ),
        out_specs=(P("row", "col", None, None), P("row", "col", None, None)),
        check_vma=False,
    )
```

```python
import functools

import jax
import jax.numpy as jnp
from jax import lax
from jax.experimental import pallas as pl
from jax.experimental.pallas import tpu as pltpu
from jax.sharding import PartitionSpec as P

BF16 = jnp.bfloat16
F32 = jnp.float32
VMEM_LIMIT = 48 * 1024 * 1024


def partner(index, slot):
    return index ^ slot


def turned(slot):
    return slot ^ (((slot >> 1) ^ (slot >> 2)) & 1) * 6


def seen(slot, index):
    return slot ^ (index & 1) * (turned(slot) ^ slot)


def order(size):
    return [0, *reversed(range(3, size, 2))]


def column_order(size):
    return order(size) + [turned(slot) ^ 1 for slot in order(size)]


def permuted(block, axis, size, slot):
    return lax.ppermute(block, axis, [(i, partner(i, slot)) for i in range(size)])


def fetched(block, axis, size, slot):
    return lax.ppermute(block, axis, [(partner(i, seen(slot, i)), i) for i in range(size)])


def fetch_chips(block, axis, size):
    return [fetched(block, axis, size, slot) for slot in order(size)[1:]]


def fetch_core(blocks, axis, size):
    return permuted(blocks, axis, size, 1)


def both_cores(blocks, axis, size):
    found = jnp.concatenate([blocks, fetch_core(blocks, axis, size)])
    return found[jnp.argsort(jnp.array(column_order(size)))]


def send_across(blocks, n_row, n_col):
    arrived = []
    for slot in reversed(range(n_col)):
        pairs = [
            (row * n_col + col, partner(row, 1) * n_col + partner(col, slot))
            for row in range(n_row)
            for col in range(n_col)
        ]
        arrived.append(lax.ppermute(blocks[slot], ("row", "col"), pairs))
    return arrived


def send_each(blocks, axis, size):
    return [permuted(blocks[slot], axis, size, slot) for slot in reversed(range(1, size))]


def call(kernel, out_shape, operands, specs=None, scratch=(), cost=None, out_specs=None):
    vmem = pl.BlockSpec(memory_space=pltpu.VMEM)
    return pl.pallas_call(
        kernel,
        out_shape=out_shape,
        in_specs=specs or [vmem] * len(operands),
        out_specs=out_specs or jax.tree.map(lambda _: vmem, out_shape),
        scratch_shapes=list(scratch),
        cost_estimate=cost,
        compiler_params=pltpu.CompilerParams(vmem_limit_bytes=VMEM_LIMIT),
    )(*operands)


def dot_nt(left, right):
    return lax.dot_general(left, right, (((1,), (1,)), ((), ())), preferred_element_type=F32)


def build_kernel(
    n_row, n_col, chunks, count, coords_hbm, tiles_hbm, dense_ref, coords, tiles, first, second, sems, coords_sem
):
    slots, block = tiles.shape[0], tiles.shape[1]
    per, part = slots // chunks, block // 2
    copies = [
        pltpu.make_async_copy(
            tiles_hbm.at[pl.ds(i * per, per)], tiles.at[pl.ds(i * per, per)], sems.at[i]
        )
        for i in range(chunks)
    ]
    coords_copy = pltpu.make_async_copy(coords_hbm, coords, coords_sem)
    coords_copy.start()
    live = count[0, 0]
    for i, copy in enumerate(copies):
        pl.when(i * per < live)(copy.start)
    row, col = lax.axis_index("row"), lax.axis_index("col")
    first[...] = jnp.zeros_like(first)
    second[...] = jnp.zeros_like(second)
    coords_copy.wait()

    def place(t):
        at = partner(coords[0, t], col) * n_row + seen(partner(coords[1, t], row), row)
        return jnp.where(t < live, at, n_row * n_col)

    for i in range(chunks):

        @pl.when(i * per < live)
        def _():
            copies[i].wait()

            @pl.loop(0, per, unroll=8)
            def _(step):
                t = i * per + step
                at = place(t)
                first[at] += tiles[t, :part].astype(F32)
                second[at] += tiles[t, part:].astype(F32)

    for k in range(n_col):
        for j, slot in enumerate(column_order(n_row)):
            at = k * n_row + slot
            columns = slice(j * block, (j + 1) * block)
            dense_ref[k * block : k * block + part, columns] = first[at].astype(BF16)
            dense_ref[k * block + part : (k + 1) * block, columns] = second[at].astype(BF16)


def prepare_kernel(mask, bias, history, *refs):
    kept_out, bias_out, wide = refs[-3:]
    block, classes = history.shape[0], bias.shape[1]
    mask_cols = jnp.broadcast_to(mask[...].astype(F32), (block, block)).T
    chosen = jnp.concatenate([mask_cols] * (history.shape[1] // block), axis=1) == 1.0
    kept_out[...] = jnp.where(chosen, -1.0, history[...].astype(F32)).astype(BF16)
    wide[...] = jnp.zeros_like(wide)
    wide[:, :classes] = jnp.broadcast_to(bias[...], (block, classes))
    bias_out[...] = wide[...].T[:classes]


def join_rows_kernel(places, *refs):
    out = refs[-1]
    block = refs[0].shape[0]
    for ref, place in zip(refs, places):
        out[place * block : (place + 1) * block, :] = ref[...]


def half_one_kernel(dense_ref, mine_ref, out):
    half = mine_ref.shape[0]
    out[...] = jnp.dot(dense_ref[:, :half], mine_ref[...], preferred_element_type=F32)


def layer_one_kernel(dense_ref, first_ref, other_ref, *outputs):
    half, block = other_ref.shape[0], dense_ref.shape[0] // len(outputs)
    for k, out in enumerate(outputs):
        rows = pl.ds(k * block, block)
        total = jnp.dot(dense_ref[rows, half:], other_ref[...], preferred_element_type=F32)
        out[...] = (first_ref[rows, :] + total).astype(BF16)


def hidden_kernel(n_col, *refs):
    parts = refs[:n_col]
    feats, w_one, b_one, w_two, kept, pushed_ref, proj_ref = refs[n_col:]
    total = feats[: kept.shape[0], :].astype(F32)
    for part in parts:
        total += part[...].astype(F32)
    pre = jnp.dot(total.astype(BF16), w_one[...], preferred_element_type=F32) + b_one[...]
    hidden = jnp.maximum(pre, 0.0)
    old = kept[...].astype(F32)
    pushed = jnp.where(old < 0.0, hidden, old).astype(BF16)
    pushed_ref[...] = pushed
    proj_ref[...] = dot_nt(w_two[...], pushed).astype(BF16)


def write_kernel(value, out):
    out[...] = value[...]


def late_kernel(value, after, out):
    del after
    out[...] = value[...]


def lanes(refs, scratch, places=None):
    block = refs[0].shape[1]
    for i, ref in zip(places or range(len(refs)), refs):
        scratch[:, i * block : (i + 1) * block] = ref[...]
    return scratch[...]


def half_two_kernel(places, dense_ref, *refs):
    blocks, (out, scratch) = refs[:-2], refs[-2:]
    half = dense_ref.shape[1] // 2
    out[...] = dot_nt(
        lanes(blocks, scratch, places), dense_ref[:, half : half + scratch.shape[1]]
    )


def layer_two_kernel(n_col, dense_ref, first_ref, own_ref, near_ref, *refs):
    blocks, outputs, scratch = refs[: -n_col - 1], refs[-n_col - 1 : -1], refs[-1]
    block, half = near_ref.shape[1], scratch.shape[1]
    rest = lanes([own_ref, *blocks], scratch)
    for k, out in enumerate(outputs):
        rows = pl.ds(k * block, block)
        total = first_ref[:, rows] + dot_nt(rest, dense_ref[rows, :half])
        total += dot_nt(near_ref[...], dense_ref[rows, dense_ref.shape[1] - block :])
        out[...] = total.astype(BF16)


def logits_kernel(n_col, pieces, *refs):
    parts = refs[:n_col]
    proj, bias, out_hbm, staged, sems = refs[n_col:]
    step = -(-staged.shape[0] // pieces // 16) * 16
    copies = []
    for i in range(pieces):
        rows = slice(i * step, (i + 1) * step if i < pieces - 1 else staged.shape[0])
        total = proj[rows, :].astype(F32) + bias[rows, :]
        for part in parts:
            total += part[rows, :].astype(F32)
        staged[rows, 0, :] = total
        copies.append(pltpu.make_async_copy(staged.at[rows], out_hbm.at[rows], sems.at[i]))
        copies[-1].start()
    for copy in copies:
        copy.wait()


def tiles_kernel(
    n_row, n_col, transposed, coords_ref, count_ref, tiles_ref, stacked_ref, out_ref, total
):
    row, col = lax.axis_index("row"), lax.axis_index("col")
    total[...] = jnp.zeros_like(total)

    @pl.loop(0, count_ref[0, 0])
    def _(t):
        k = partner(coords_ref[0, t], col)
        j = seen(partner(coords_ref[1, t], row), row)
        if transposed:
            total[k] += dot_nt(stacked_ref[j], tiles_ref[t])
        else:
            total[k] += jnp.dot(tiles_ref[t], stacked_ref[j], preferred_element_type=F32)

    out_ref[...] = total[...].astype(BF16)


def on_device(
    n_row, n_col,
    features, tiles, tile_coords, tile_count, batch_mask, history,
    weight_one, bias_one, weight_two, bias_two,
):
    feat, tile_set, hist = features[0, 0], tiles[0, 0], history[0, 0]
    coords = tile_coords[0, 0].T
    slots, block = tile_set.shape[0], tile_set.shape[1]
    f_in, hid, classes = feat.shape[1], weight_one.shape[1], weight_two.shape[1]
    w_two_t = weight_two.T
    dense_form = n_row * n_col <= slots
    smem = pl.BlockSpec(memory_space=pltpu.SMEM)
    vmem = pl.BlockSpec(memory_space=pltpu.VMEM)
    hbm = pl.BlockSpec(memory_space=pltpu.HBM)
    shape = jax.ShapeDtypeStruct

    def prepare(*after):
        return call(
            prepare_kernel,
            (shape((block, hid), BF16), shape((classes, block), F32)),
            (batch_mask[0], bias_two[None], hist, *after),
            specs=[vmem] * 3 + [pl.BlockSpec(memory_space=pl.ANY)] * len(after),
            scratch=[pltpu.VMEM((block, -(-classes // 128) * 128), F32)],
        )

    chips_one = [feat, *fetch_chips(feat, "row", n_row)]

    if dense_form:
        anywhere = pl.BlockSpec(memory_space=pl.ANY)
        chunks = 8
        dense = call(
            functools.partial(build_kernel, n_row, n_col, chunks),
            shape((n_col * block, n_row * block), BF16),
            (
                tile_count,
                pltpu.with_memory_space_constraint(coords, pltpu.HBM),
                pltpu.with_memory_space_constraint(tile_set, pltpu.HBM),
            ),
            specs=[smem, hbm, hbm],
            scratch=[
                pltpu.SMEM((2, slots), jnp.int32),
                pltpu.VMEM((slots, block, block), BF16),
                pltpu.VMEM((n_row * n_col + 1, block // 2, block), F32),
                pltpu.VMEM((n_row * n_col + 1, block // 2, block), F32),
                pltpu.SemaphoreType.DMA((chunks,)),
                pltpu.SemaphoreType.DMA(()),
            ],
            cost=pl.CostEstimate(
                flops=slots * block * block,
                bytes_accessed=2 * slots * block * block,
                transcendentals=0,
            ),
        )
        names = order(n_row)
        places_one = [0, *sorted(range(1, n_row // 2), key=lambda i: (names[i] != 5, names[i]))]
        mine_one = call(
            functools.partial(join_rows_kernel, places_one),
            shape((n_row // 2 * block, f_in), BF16),
            (*[chips_one[i] for i in places_one], dense),
            specs=[vmem] * len(chips_one) + [anywhere],
        )
        other_one = fetch_core(mine_one, "row", n_row)
        kept, bias_cols = prepare(mine_one)
        half_one = call(half_one_kernel, shape((n_col * block, f_in), F32), (dense, mine_one))
        parts_one = call(
            layer_one_kernel,
            [shape((block, f_in), BF16)] * n_col,
            (dense, half_one, other_one),
        )
    else:
        kept, bias_cols = prepare()
        summed = call(
            functools.partial(tiles_kernel, n_row, n_col, False),
            shape((n_col, block, f_in), BF16),
            (coords, tile_count, tile_set, both_cores(jnp.stack(chips_one), "row", n_row)),
            specs=[smem, smem, vmem, vmem],
            scratch=[pltpu.VMEM((n_col, block, f_in), F32)],
        )
        parts_one = [summed[k] for k in range(n_col)]
        other_one = fetch_core(feat, "row", n_row)

    arrived_one = send_across(parts_one, n_row, n_col)
    kept = fetch_core(kept, "row", n_row)
    pushed, proj = call(
        functools.partial(hidden_kernel, n_col),
        (shape((block, hid), BF16), shape((classes, block), BF16)),
        (*arrived_one, other_one, weight_one, bias_one[None], w_two_t, kept),
    )
    chips_two = [proj, *fetch_chips(proj, "row", n_row)]
    if dense_form:
        near = chips_two[order(n_row).index(5)]
        early = [x for x in chips_two if x is not near]
        near_other = fetched(proj, "row", n_row, 2)
        others_two = [fetch_core(x, "row", n_row) for x in early] + [near_other]
        own_proj = others_two[0]
    else:
        own_proj = fetch_core(proj, "row", n_row)

    if dense_form:
        late = others_two
        places_two = [0, *reversed(range(1, len(early)))]
        half_two = call(
            functools.partial(half_two_kernel, places_two),
            shape((classes, n_col * block), F32),
            (dense, *[early[i] for i in places_two]),
            scratch=[pltpu.VMEM((classes, len(early) * block), BF16)],
        )
        pushed = call(
            late_kernel, shape((block, hid), BF16), (pushed, half_two), specs=[vmem, anywhere]
        )
        parts_two = call(
            functools.partial(layer_two_kernel, n_col),
            [shape((classes, block), BF16)] * n_col,
            (dense, half_two, late[0], near, *late[1:]),
            scratch=[pltpu.VMEM((classes, len(late) * block), BF16)],
        )
    else:
        other_slots = jnp.arange(n_row) ^ 1
        summed = call(
            functools.partial(tiles_kernel, n_row, n_col, True),
            shape((n_col, classes, block), BF16),
            (coords, tile_count, tile_set, both_cores(jnp.stack(chips_two), "row", n_row)[other_slots]),
            specs=[smem, smem, vmem, vmem],
            scratch=[pltpu.VMEM((n_col, classes, block), F32)],
        )
        parts_two = [summed[k] for k in range(n_col)]

    arrived_two = send_each(parts_two, "col", n_col)
    pushed = call(write_kernel, shape((block, hid), BF16), (fetch_core(pushed, "row", n_row),))
    pieces = 4
    scores = call(
        functools.partial(logits_kernel, n_col, pieces),
        shape((classes, 1, block), F32),
        (parts_two[0], *arrived_two, own_proj, bias_cols),
        scratch=[pltpu.VMEM((classes, 1, block), F32), pltpu.SemaphoreType.DMA((pieces,))],
        out_specs=pl.BlockSpec(memory_space=pl.ANY),
    )
    return pushed[None, None], scores.transpose(1, 2, 0)[None]


def solution(mesh):
    sizes = mesh.shape
    return jax.shard_map(
        functools.partial(on_device, sizes["row"], sizes["col"]),
        mesh=mesh,
        in_specs=(
            P("row", "col", None, None),
            P("row", "col", None, None, None),
            P("row", "col", None, None),
            P("row", "col"),
            P("row", "col", None),
            P("row", "col", None, None),
            P(),
            P(),
            P(),
            P(),
        ),
        out_specs=(P("row", "col", None, None), P("row", "col", None, None)),
        check_vma=False,
    )
```

```python
import functools

import jax
import jax.numpy as jnp
from jax import lax
from jax.experimental import pallas as pl
from jax.experimental.pallas import tpu as pltpu
from jax.sharding import PartitionSpec as P

BF16 = jnp.bfloat16
F32 = jnp.float32
VMEM_LIMIT = 48 * 1024 * 1024


def partner(index, slot):
    return index ^ slot


def turned(slot):
    return slot ^ (((slot >> 1) ^ (slot >> 2)) & 1) * 6


def seen(slot, index):
    return slot ^ (index & 1) * (turned(slot) ^ slot)


def order(size):
    return [0, *reversed(range(3, size, 2))]


def column_order(size):
    return order(size) + [turned(slot) ^ 1 for slot in order(size)]


def permuted(block, axis, size, slot):
    return lax.ppermute(block, axis, [(i, partner(i, slot)) for i in range(size)])


def fetched(block, axis, size, slot):
    return lax.ppermute(block, axis, [(partner(i, seen(slot, i)), i) for i in range(size)])


def fetch_chips(block, axis, size):
    return [fetched(block, axis, size, slot) for slot in order(size)[1:]]


def fetch_core(blocks, axis, size):
    return permuted(blocks, axis, size, 1)


def both_cores(blocks, axis, size):
    found = jnp.concatenate([blocks, fetch_core(blocks, axis, size)])
    return found[jnp.argsort(jnp.array(column_order(size)))]


def send_across(blocks, n_row, n_col):
    arrived = []
    for slot in reversed(range(n_col)):
        pairs = [
            (row * n_col + col, partner(row, 1) * n_col + partner(col, slot))
            for row in range(n_row)
            for col in range(n_col)
        ]
        arrived.append(lax.ppermute(blocks[slot], ("row", "col"), pairs))
    return arrived


def send_each(blocks, axis, size):
    return [permuted(blocks[slot], axis, size, slot) for slot in reversed(range(1, size))]


def call(kernel, out_shape, operands, specs=None, scratch=(), cost=None, out_specs=None):
    vmem = pl.BlockSpec(memory_space=pltpu.VMEM)
    return pl.pallas_call(
        kernel,
        out_shape=out_shape,
        in_specs=specs or [vmem] * len(operands),
        out_specs=out_specs or jax.tree.map(lambda _: vmem, out_shape),
        scratch_shapes=list(scratch),
        cost_estimate=cost,
        compiler_params=pltpu.CompilerParams(vmem_limit_bytes=VMEM_LIMIT),
    )(*operands)


def dot_nt(left, right):
    return lax.dot_general(left, right, (((1,), (1,)), ((), ())), preferred_element_type=F32)


def build_kernel(
    n_row, n_col, chunks, count, coords_hbm, tiles_hbm, dense_ref, coords, tiles, first, second, sems, coords_sem
):
    slots, block = tiles.shape[0], tiles.shape[1]
    per, part = slots // chunks, block // 2
    copies = [
        pltpu.make_async_copy(
            tiles_hbm.at[pl.ds(i * per, per)], tiles.at[pl.ds(i * per, per)], sems.at[i]
        )
        for i in range(chunks)
    ]
    coords_copy = pltpu.make_async_copy(coords_hbm, coords, coords_sem)
    coords_copy.start()
    live = count[0, 0]
    for i, copy in enumerate(copies):
        pl.when(i * per < live)(copy.start)
    row, col = lax.axis_index("row"), lax.axis_index("col")
    first[...] = jnp.zeros_like(first)
    second[...] = jnp.zeros_like(second)
    coords_copy.wait()

    def place(t):
        at = partner(coords[0, t], col) * n_row + seen(partner(coords[1, t], row), row)
        return jnp.where(t < live, at, n_row * n_col)

    for i in range(chunks):

        @pl.when(i * per < live)
        def _():
            copies[i].wait()

            @pl.loop(0, per, unroll=8)
            def _(step):
                t = i * per + step
                at = place(t)
                first[at] += tiles[t, :part].astype(F32)
                second[at] += tiles[t, part:].astype(F32)

    for k in range(n_col):
        for j, slot in enumerate(column_order(n_row)):
            at = k * n_row + slot
            columns = slice(j * block, (j + 1) * block)
            dense_ref[k * block : k * block + part, columns] = first[at].astype(BF16)
            dense_ref[k * block + part : (k + 1) * block, columns] = second[at].astype(BF16)


def prepare_kernel(mask, bias, history, *refs):
    kept_out, bias_out, wide = refs[-3:]
    block, classes = history.shape[0], bias.shape[1]
    mask_cols = jnp.broadcast_to(mask[...].astype(F32), (block, block)).T
    chosen = jnp.concatenate([mask_cols] * (history.shape[1] // block), axis=1) == 1.0
    kept_out[...] = jnp.where(chosen, -1.0, history[...].astype(F32)).astype(BF16)
    wide[...] = jnp.zeros_like(wide)
    wide[:, :classes] = jnp.broadcast_to(bias[...], (block, classes))
    bias_out[...] = wide[...].T[:classes]


def join_rows_kernel(places, *refs):
    out = refs[-1]
    block = refs[0].shape[0]
    for ref, place in zip(refs, places):
        out[place * block : (place + 1) * block, :] = ref[...]


def half_one_kernel(dense_ref, mine_ref, out):
    half = mine_ref.shape[0]
    out[...] = jnp.dot(dense_ref[:, :half], mine_ref[...], preferred_element_type=F32)


def layer_one_kernel(dense_ref, first_ref, other_ref, *outputs):
    half, block = other_ref.shape[0], dense_ref.shape[0] // len(outputs)
    total = first_ref[...] + jnp.dot(
        dense_ref[:, half:], other_ref[...], preferred_element_type=F32
    )
    for k, out in enumerate(outputs):
        out[...] = total[k * block : (k + 1) * block, :].astype(BF16)


def hidden_kernel(n_col, *refs):
    parts = refs[:n_col]
    feats, w_one, b_one, w_two, kept, pushed_ref, proj_ref = refs[n_col:]
    total = feats[: kept.shape[0], :].astype(F32)
    for part in parts:
        total += part[...].astype(F32)
    pre = jnp.dot(total.astype(BF16), w_one[...], preferred_element_type=F32) + b_one[...]
    hidden = jnp.maximum(pre, 0.0)
    old = kept[...].astype(F32)
    pushed = jnp.where(old < 0.0, hidden, old).astype(BF16)
    pushed_ref[...] = pushed
    proj_ref[...] = dot_nt(w_two[...], pushed).astype(BF16)


def write_kernel(value, out):
    out[...] = value[...]


def late_kernel(value, after, out):
    del after
    out[...] = value[...]


def lanes(refs, scratch, places=None):
    block = refs[0].shape[1]
    for i, ref in zip(places or range(len(refs)), refs):
        scratch[:, i * block : (i + 1) * block] = ref[...]
    return scratch[...]


def half_two_kernel(places, dense_ref, *refs):
    blocks, (out, scratch) = refs[:-2], refs[-2:]
    half = dense_ref.shape[1] // 2
    out[...] = dot_nt(
        lanes(blocks, scratch, places), dense_ref[:, half : half + scratch.shape[1]]
    )


def layer_two_kernel(n_col, dense_ref, first_ref, own_ref, near_ref, *refs):
    blocks, outputs, scratch = refs[: -n_col - 1], refs[-n_col - 1 : -1], refs[-1]
    block, half = near_ref.shape[1], scratch.shape[1]
    rest = lanes([own_ref, *blocks], scratch)
    total = first_ref[...] + dot_nt(rest, dense_ref[:, :half])
    total += dot_nt(near_ref[...], dense_ref[:, dense_ref.shape[1] - block :])
    for k, out in enumerate(outputs):
        out[...] = total[:, k * block : (k + 1) * block].astype(BF16)


def logits_kernel(n_col, pieces, *refs):
    parts = refs[:n_col]
    proj, bias, out_hbm, staged, sems = refs[n_col:]
    step = -(-staged.shape[0] // pieces // 16) * 16
    copies = []
    for i in range(pieces):
        rows = slice(i * step, (i + 1) * step if i < pieces - 1 else staged.shape[0])
        total = proj[rows, :].astype(F32) + bias[rows, :]
        for part in parts:
            total += part[rows, :].astype(F32)
        staged[rows, 0, :] = total
        copies.append(pltpu.make_async_copy(staged.at[rows], out_hbm.at[rows], sems.at[i]))
        copies[-1].start()
    for copy in copies:
        copy.wait()


def tiles_kernel(
    n_row, n_col, transposed, coords_ref, count_ref, tiles_ref, stacked_ref, out_ref, total
):
    row, col = lax.axis_index("row"), lax.axis_index("col")
    total[...] = jnp.zeros_like(total)

    @pl.loop(0, count_ref[0, 0])
    def _(t):
        k = partner(coords_ref[0, t], col)
        j = seen(partner(coords_ref[1, t], row), row)
        if transposed:
            total[k] += dot_nt(stacked_ref[j], tiles_ref[t])
        else:
            total[k] += jnp.dot(tiles_ref[t], stacked_ref[j], preferred_element_type=F32)

    out_ref[...] = total[...].astype(BF16)


def on_device(
    n_row, n_col,
    features, tiles, tile_coords, tile_count, batch_mask, history,
    weight_one, bias_one, weight_two, bias_two,
):
    feat, tile_set, hist = features[0, 0], tiles[0, 0], history[0, 0]
    coords = tile_coords[0, 0].T
    slots, block = tile_set.shape[0], tile_set.shape[1]
    f_in, hid, classes = feat.shape[1], weight_one.shape[1], weight_two.shape[1]
    w_two_t = weight_two.T
    dense_form = n_row * n_col <= slots
    smem = pl.BlockSpec(memory_space=pltpu.SMEM)
    vmem = pl.BlockSpec(memory_space=pltpu.VMEM)
    hbm = pl.BlockSpec(memory_space=pltpu.HBM)
    shape = jax.ShapeDtypeStruct

    def prepare(*after):
        return call(
            prepare_kernel,
            (shape((block, hid), BF16), shape((classes, block), F32)),
            (batch_mask[0], bias_two[None], hist, *after),
            specs=[vmem] * 3 + [pl.BlockSpec(memory_space=pl.ANY)] * len(after),
            scratch=[pltpu.VMEM((block, -(-classes // 128) * 128), F32)],
        )

    chips_one = [feat, *fetch_chips(feat, "row", n_row)]

    if dense_form:
        anywhere = pl.BlockSpec(memory_space=pl.ANY)
        chunks = 8
        dense = call(
            functools.partial(build_kernel, n_row, n_col, chunks),
            shape((n_col * block, n_row * block), BF16),
            (
                tile_count,
                pltpu.with_memory_space_constraint(coords, pltpu.HBM),
                pltpu.with_memory_space_constraint(tile_set, pltpu.HBM),
            ),
            specs=[smem, hbm, hbm],
            scratch=[
                pltpu.SMEM((2, slots), jnp.int32),
                pltpu.VMEM((slots, block, block), BF16),
                pltpu.VMEM((n_row * n_col + 1, block // 2, block), F32),
                pltpu.VMEM((n_row * n_col + 1, block // 2, block), F32),
                pltpu.SemaphoreType.DMA((chunks,)),
                pltpu.SemaphoreType.DMA(()),
            ],
            cost=pl.CostEstimate(
                flops=slots * block * block,
                bytes_accessed=2 * slots * block * block,
                transcendentals=0,
            ),
        )
        names = order(n_row)
        places_one = [0, *sorted(range(1, n_row // 2), key=lambda i: (names[i] != 5, names[i]))]
        mine_one = call(
            functools.partial(join_rows_kernel, places_one),
            shape((n_row // 2 * block, f_in), BF16),
            (*[chips_one[i] for i in places_one], dense),
            specs=[vmem] * len(chips_one) + [anywhere],
        )
        other_one = fetch_core(mine_one, "row", n_row)
        kept, bias_cols = prepare(mine_one)
        half_one = call(half_one_kernel, shape((n_col * block, f_in), F32), (dense, mine_one))
        parts_one = call(
            layer_one_kernel,
            [shape((block, f_in), BF16)] * n_col,
            (dense, half_one, other_one),
        )
    else:
        kept, bias_cols = prepare()
        summed = call(
            functools.partial(tiles_kernel, n_row, n_col, False),
            shape((n_col, block, f_in), BF16),
            (coords, tile_count, tile_set, both_cores(jnp.stack(chips_one), "row", n_row)),
            specs=[smem, smem, vmem, vmem],
            scratch=[pltpu.VMEM((n_col, block, f_in), F32)],
        )
        parts_one = [summed[k] for k in range(n_col)]
        other_one = fetch_core(feat, "row", n_row)

    arrived_one = send_across(parts_one, n_row, n_col)
    kept = fetch_core(kept, "row", n_row)
    pushed, proj = call(
        functools.partial(hidden_kernel, n_col),
        (shape((block, hid), BF16), shape((classes, block), BF16)),
        (*arrived_one, other_one, weight_one, bias_one[None], w_two_t, kept),
    )
    chips_two = [proj, *fetch_chips(proj, "row", n_row)]
    if dense_form:
        near = chips_two[order(n_row).index(5)]
        early = [x for x in chips_two if x is not near]
        near_other = fetched(proj, "row", n_row, 2)
        others_two = [fetch_core(x, "row", n_row) for x in early] + [near_other]
        own_proj = others_two[0]
    else:
        own_proj = fetch_core(proj, "row", n_row)

    if dense_form:
        late = others_two
        places_two = [0, *reversed(range(1, len(early)))]
        half_two = call(
            functools.partial(half_two_kernel, places_two),
            shape((classes, n_col * block), F32),
            (dense, *[early[i] for i in places_two]),
            scratch=[pltpu.VMEM((classes, len(early) * block), BF16)],
        )
        pushed = call(
            late_kernel, shape((block, hid), BF16), (pushed, half_two), specs=[vmem, anywhere]
        )
        parts_two = call(
            functools.partial(layer_two_kernel, n_col),
            [shape((classes, block), BF16)] * n_col,
            (dense, half_two, late[0], near, *late[1:]),
            scratch=[pltpu.VMEM((classes, len(late) * block), BF16)],
        )
    else:
        other_slots = jnp.arange(n_row) ^ 1
        summed = call(
            functools.partial(tiles_kernel, n_row, n_col, True),
            shape((n_col, classes, block), BF16),
            (coords, tile_count, tile_set, both_cores(jnp.stack(chips_two), "row", n_row)[other_slots]),
            specs=[smem, smem, vmem, vmem],
            scratch=[pltpu.VMEM((n_col, classes, block), F32)],
        )
        parts_two = [summed[k] for k in range(n_col)]

    arrived_two = send_each(parts_two, "col", n_col)
    pushed = call(write_kernel, shape((block, hid), BF16), (fetch_core(pushed, "row", n_row),))
    pieces = 4
    scores = call(
        functools.partial(logits_kernel, n_col, pieces),
        shape((classes, 1, block), F32),
        (parts_two[0], *arrived_two, own_proj, bias_cols),
        scratch=[pltpu.VMEM((classes, 1, block), F32), pltpu.SemaphoreType.DMA((pieces,))],
        out_specs=pl.BlockSpec(memory_space=pl.ANY),
    )
    return pushed[None, None], scores.transpose(1, 2, 0)[None]


def solution(mesh):
    sizes = mesh.shape
    return jax.shard_map(
        functools.partial(on_device, sizes["row"], sizes["col"]),
        mesh=mesh,
        in_specs=(
            P("row", "col", None, None),
            P("row", "col", None, None, None),
            P("row", "col", None, None),
            P("row", "col"),
            P("row", "col", None),
            P("row", "col", None, None),
            P(),
            P(),
            P(),
            P(),
        ),
        out_specs=(P("row", "col", None, None), P("row", "col", None, None)),
        check_vma=False,
    )
```

```python
import functools

import jax
import jax.numpy as jnp
from jax import lax
from jax.experimental import pallas as pl
from jax.experimental.pallas import tpu as pltpu
from jax.sharding import PartitionSpec as P

BF16 = jnp.bfloat16
F32 = jnp.float32
VMEM_LIMIT = 48 * 1024 * 1024


def partner(index, slot):
    return index ^ slot


def turned(slot):
    return slot ^ (((slot >> 1) ^ (slot >> 2)) & 1) * 6


def seen(slot, index):
    return slot ^ (index & 1) * (turned(slot) ^ slot)


def order(size):
    return [0, *reversed(range(3, size, 2))]


def column_order(size):
    return order(size) + [turned(slot) ^ 1 for slot in order(size)]


def permuted(block, axis, size, slot):
    return lax.ppermute(block, axis, [(i, partner(i, slot)) for i in range(size)])


def fetched(block, axis, size, slot):
    return lax.ppermute(block, axis, [(partner(i, seen(slot, i)), i) for i in range(size)])


def fetch_chips(block, axis, size):
    return [fetched(block, axis, size, slot) for slot in order(size)[1:]]


def fetch_core(blocks, axis, size):
    return permuted(blocks, axis, size, 1)


def both_cores(blocks, axis, size):
    found = jnp.concatenate([blocks, fetch_core(blocks, axis, size)])
    return found[jnp.argsort(jnp.array(column_order(size)))]


def send_across(blocks, n_row, n_col):
    arrived = []
    for slot in reversed(range(n_col)):
        pairs = [
            (row * n_col + col, partner(row, 1) * n_col + partner(col, slot))
            for row in range(n_row)
            for col in range(n_col)
        ]
        arrived.append(lax.ppermute(blocks[slot], ("row", "col"), pairs))
    return arrived


def send_each(blocks, axis, size):
    return [permuted(blocks[slot], axis, size, slot) for slot in reversed(range(1, size))]


def call(kernel, out_shape, operands, specs=None, scratch=(), cost=None, out_specs=None):
    vmem = pl.BlockSpec(memory_space=pltpu.VMEM)
    return pl.pallas_call(
        kernel,
        out_shape=out_shape,
        in_specs=specs or [vmem] * len(operands),
        out_specs=out_specs or jax.tree.map(lambda _: vmem, out_shape),
        scratch_shapes=list(scratch),
        cost_estimate=cost,
        compiler_params=pltpu.CompilerParams(vmem_limit_bytes=VMEM_LIMIT),
    )(*operands)


def dot_nt(left, right):
    return lax.dot_general(left, right, (((1,), (1,)), ((), ())), preferred_element_type=F32)


def build_kernel(
    n_row, n_col, chunks, count, coords_hbm, tiles_hbm, dense_ref, coords, tiles, first, second, sems, coords_sem
):
    slots, block = tiles.shape[0], tiles.shape[1]
    per, part = slots // chunks, block // 2
    copies = [
        pltpu.make_async_copy(
            tiles_hbm.at[pl.ds(i * per, per)], tiles.at[pl.ds(i * per, per)], sems.at[i]
        )
        for i in range(chunks)
    ]
    coords_copy = pltpu.make_async_copy(coords_hbm, coords, coords_sem)
    coords_copy.start()
    live = count[0, 0]
    for i, copy in enumerate(copies):
        pl.when(i * per < live)(copy.start)
    row, col = lax.axis_index("row"), lax.axis_index("col")
    first[...] = jnp.zeros_like(first)
    second[...] = jnp.zeros_like(second)
    coords_copy.wait()

    def place(t):
        at = partner(coords[0, t], col) * n_row + seen(partner(coords[1, t], row), row)
        return jnp.where(t < live, at, n_row * n_col)

    for i in range(chunks):

        @pl.when(i * per < live)
        def _():
            copies[i].wait()

            @pl.loop(0, per, unroll=8)
            def _(step):
                t = i * per + step
                at = place(t)
                first[at] += tiles[t, :part].astype(F32)
                second[at] += tiles[t, part:].astype(F32)

    for k in range(n_col):
        for j, slot in enumerate(column_order(n_row)):
            at = k * n_row + slot
            columns = slice(j * block, (j + 1) * block)
            dense_ref[k * block : k * block + part, columns] = first[at].astype(BF16)
            dense_ref[k * block + part : (k + 1) * block, columns] = second[at].astype(BF16)


def prepare_kernel(mask, bias, history, *refs):
    kept_out, bias_out, wide = refs[-3:]
    block, classes = history.shape[0], bias.shape[1]
    mask_cols = jnp.broadcast_to(mask[...].astype(F32), (block, block)).T
    chosen = jnp.concatenate([mask_cols] * (history.shape[1] // block), axis=1) == 1.0
    kept_out[...] = jnp.where(chosen, -1.0, history[...].astype(F32)).astype(BF16)
    wide[...] = jnp.zeros_like(wide)
    wide[:, :classes] = jnp.broadcast_to(bias[...], (block, classes))
    bias_out[...] = wide[...].T[:classes]


def rows(refs, scratch, places):
    block = refs[0].shape[0]
    for i, ref in zip(places, refs):
        scratch[i * block : (i + 1) * block, :] = ref[...]
    return scratch[...]


def half_one_kernel(places, dense_ref, *refs):
    blocks, (out, scratch) = refs[:-2], refs[-2:]
    out[...] = jnp.dot(
        dense_ref[:, : scratch.shape[0]], rows(blocks, scratch, places), preferred_element_type=F32
    )


def layer_one_kernel(n_col, places, dense_ref, first_ref, *refs):
    blocks, outputs, scratch = refs[: -n_col - 1], refs[-n_col - 1 : -1], refs[-1]
    half, block = scratch.shape[0], dense_ref.shape[0] // n_col
    total = first_ref[...] + jnp.dot(
        dense_ref[:, half:], rows(blocks, scratch, places), preferred_element_type=F32
    )
    for k, out in enumerate(outputs):
        out[...] = total[k * block : (k + 1) * block, :].astype(BF16)


def hidden_kernel(n_col, *refs):
    parts = refs[:n_col]
    feats, w_one, b_one, w_two, kept, pushed_ref, proj_ref = refs[n_col:]
    total = feats[: kept.shape[0], :].astype(F32)
    for part in parts:
        total += part[...].astype(F32)
    pre = jnp.dot(total.astype(BF16), w_one[...], preferred_element_type=F32) + b_one[...]
    hidden = jnp.maximum(pre, 0.0)
    old = kept[...].astype(F32)
    pushed = jnp.where(old < 0.0, hidden, old).astype(BF16)
    pushed_ref[...] = pushed
    proj_ref[...] = dot_nt(w_two[...], pushed).astype(BF16)


def write_kernel(value, out):
    out[...] = value[...]


def late_kernel(value, after, out):
    del after
    out[...] = value[...]


def lanes(refs, scratch, places=None):
    block = refs[0].shape[1]
    for i, ref in zip(places or range(len(refs)), refs):
        scratch[:, i * block : (i + 1) * block] = ref[...]
    return scratch[...]


def half_two_kernel(places, dense_ref, *refs):
    blocks, (out, scratch) = refs[:-2], refs[-2:]
    half = dense_ref.shape[1] // 2
    out[...] = dot_nt(
        lanes(blocks, scratch, places), dense_ref[:, half : half + scratch.shape[1]]
    )


def layer_two_kernel(n_col, dense_ref, first_ref, own_ref, near_ref, *refs):
    blocks, outputs, scratch = refs[: -n_col - 1], refs[-n_col - 1 : -1], refs[-1]
    block, half = near_ref.shape[1], scratch.shape[1]
    rest = lanes([own_ref, *blocks], scratch)
    total = first_ref[...] + dot_nt(rest, dense_ref[:, :half])
    total += dot_nt(near_ref[...], dense_ref[:, dense_ref.shape[1] - block :])
    for k, out in enumerate(outputs):
        out[...] = total[:, k * block : (k + 1) * block].astype(BF16)


def logits_kernel(n_col, pieces, *refs):
    parts = refs[:n_col]
    proj, bias, out_hbm, staged, sems = refs[n_col:]
    step = -(-staged.shape[0] // pieces // 16) * 16
    copies = []
    for i in range(pieces):
        rows = slice(i * step, (i + 1) * step if i < pieces - 1 else staged.shape[0])
        total = proj[rows, :].astype(F32) + bias[rows, :]
        for part in parts:
            total += part[rows, :].astype(F32)
        staged[rows, 0, :] = total
        copies.append(pltpu.make_async_copy(staged.at[rows], out_hbm.at[rows], sems.at[i]))
        copies[-1].start()
    for copy in copies:
        copy.wait()


def tiles_kernel(
    n_row, n_col, transposed, coords_ref, count_ref, tiles_ref, stacked_ref, out_ref, total
):
    row, col = lax.axis_index("row"), lax.axis_index("col")
    total[...] = jnp.zeros_like(total)

    @pl.loop(0, count_ref[0, 0])
    def _(t):
        k = partner(coords_ref[0, t], col)
        j = seen(partner(coords_ref[1, t], row), row)
        if transposed:
            total[k] += dot_nt(stacked_ref[j], tiles_ref[t])
        else:
            total[k] += jnp.dot(tiles_ref[t], stacked_ref[j], preferred_element_type=F32)

    out_ref[...] = total[...].astype(BF16)


def on_device(
    n_row, n_col,
    features, tiles, tile_coords, tile_count, batch_mask, history,
    weight_one, bias_one, weight_two, bias_two,
):
    feat, tile_set, hist = features[0, 0], tiles[0, 0], history[0, 0]
    coords = tile_coords[0, 0].T
    slots, block = tile_set.shape[0], tile_set.shape[1]
    f_in, hid, classes = feat.shape[1], weight_one.shape[1], weight_two.shape[1]
    w_two_t = weight_two.T
    dense_form = n_row * n_col <= slots
    smem = pl.BlockSpec(memory_space=pltpu.SMEM)
    vmem = pl.BlockSpec(memory_space=pltpu.VMEM)
    hbm = pl.BlockSpec(memory_space=pltpu.HBM)
    shape = jax.ShapeDtypeStruct

    def prepare(*after):
        return call(
            prepare_kernel,
            (shape((block, hid), BF16), shape((classes, block), F32)),
            (batch_mask[0], bias_two[None], hist, *after),
            specs=[vmem] * 3 + [pl.BlockSpec(memory_space=pl.ANY)] * len(after),
            scratch=[pltpu.VMEM((block, -(-classes // 128) * 128), F32)],
        )

    chips_one = [feat, *fetch_chips(feat, "row", n_row)]

    if dense_form:
        anywhere = pl.BlockSpec(memory_space=pl.ANY)
        chunks = 8
        dense = call(
            functools.partial(build_kernel, n_row, n_col, chunks),
            shape((n_col * block, n_row * block), BF16),
            (
                tile_count,
                pltpu.with_memory_space_constraint(coords, pltpu.HBM),
                pltpu.with_memory_space_constraint(tile_set, pltpu.HBM),
            ),
            specs=[smem, hbm, hbm],
            scratch=[
                pltpu.SMEM((2, slots), jnp.int32),
                pltpu.VMEM((slots, block, block), BF16),
                pltpu.VMEM((n_row * n_col + 1, block // 2, block), F32),
                pltpu.VMEM((n_row * n_col + 1, block // 2, block), F32),
                pltpu.SemaphoreType.DMA((chunks,)),
                pltpu.SemaphoreType.DMA(()),
            ],
            cost=pl.CostEstimate(
                flops=slots * block * block,
                bytes_accessed=2 * slots * block * block,
                transcendentals=0,
            ),
        )
        names = order(n_row)
        places_one = [0, *sorted(range(1, n_row // 2), key=lambda i: (names[i] != 5, names[i]))]
        mine_one = [chips_one[i] for i in places_one]
        others_one = [fetch_core(x, "row", n_row) for x in mine_one]
        other_one = others_one[0]
        stacked = pltpu.VMEM((n_row // 2 * block, f_in), BF16)
        half_one = call(
            functools.partial(half_one_kernel, places_one),
            shape((n_col * block, f_in), F32),
            (dense, *mine_one),
            scratch=[stacked],
        )
        kept, bias_cols = prepare(half_one)
        parts_one = call(
            functools.partial(layer_one_kernel, n_col, places_one),
            [shape((block, f_in), BF16)] * n_col,
            (dense, half_one, *others_one),
            scratch=[stacked],
        )
    else:
        kept, bias_cols = prepare()
        summed = call(
            functools.partial(tiles_kernel, n_row, n_col, False),
            shape((n_col, block, f_in), BF16),
            (coords, tile_count, tile_set, both_cores(jnp.stack(chips_one), "row", n_row)),
            specs=[smem, smem, vmem, vmem],
            scratch=[pltpu.VMEM((n_col, block, f_in), F32)],
        )
        parts_one = [summed[k] for k in range(n_col)]
        other_one = fetch_core(feat, "row", n_row)

    arrived_one = send_across(parts_one, n_row, n_col)
    kept = fetch_core(kept, "row", n_row)
    pushed, proj = call(
        functools.partial(hidden_kernel, n_col),
        (shape((block, hid), BF16), shape((classes, block), BF16)),
        (*arrived_one, other_one, weight_one, bias_one[None], w_two_t, kept),
    )
    chips_two = [proj, *fetch_chips(proj, "row", n_row)]
    if dense_form:
        near = chips_two[order(n_row).index(5)]
        early = [x for x in chips_two if x is not near]
        near_other = fetched(proj, "row", n_row, 2)
        others_two = [fetch_core(x, "row", n_row) for x in early] + [near_other]
        own_proj = others_two[0]
    else:
        own_proj = fetch_core(proj, "row", n_row)

    if dense_form:
        late = others_two
        places_two = [0, *reversed(range(1, len(early)))]
        half_two = call(
            functools.partial(half_two_kernel, places_two),
            shape((classes, n_col * block), F32),
            (dense, *[early[i] for i in places_two]),
            scratch=[pltpu.VMEM((classes, len(early) * block), BF16)],
        )
        pushed = call(
            late_kernel, shape((block, hid), BF16), (pushed, half_two), specs=[vmem, anywhere]
        )
        parts_two = call(
            functools.partial(layer_two_kernel, n_col),
            [shape((classes, block), BF16)] * n_col,
            (dense, half_two, late[0], near, *late[1:]),
            scratch=[pltpu.VMEM((classes, len(late) * block), BF16)],
        )
    else:
        other_slots = jnp.arange(n_row) ^ 1
        summed = call(
            functools.partial(tiles_kernel, n_row, n_col, True),
            shape((n_col, classes, block), BF16),
            (coords, tile_count, tile_set, both_cores(jnp.stack(chips_two), "row", n_row)[other_slots]),
            specs=[smem, smem, vmem, vmem],
            scratch=[pltpu.VMEM((n_col, classes, block), F32)],
        )
        parts_two = [summed[k] for k in range(n_col)]

    arrived_two = send_each(parts_two, "col", n_col)
    pushed = call(write_kernel, shape((block, hid), BF16), (fetch_core(pushed, "row", n_row),))
    pieces = 4
    scores = call(
        functools.partial(logits_kernel, n_col, pieces),
        shape((classes, 1, block), F32),
        (parts_two[0], *arrived_two, own_proj, bias_cols),
        scratch=[pltpu.VMEM((classes, 1, block), F32), pltpu.SemaphoreType.DMA((pieces,))],
        out_specs=pl.BlockSpec(memory_space=pl.ANY),
    )
    return pushed[None, None], scores.transpose(1, 2, 0)[None]


def solution(mesh):
    sizes = mesh.shape
    return jax.shard_map(
        functools.partial(on_device, sizes["row"], sizes["col"]),
        mesh=mesh,
        in_specs=(
            P("row", "col", None, None),
            P("row", "col", None, None, None),
            P("row", "col", None, None),
            P("row", "col"),
            P("row", "col", None),
            P("row", "col", None, None),
            P(),
            P(),
            P(),
            P(),
        ),
        out_specs=(P("row", "col", None, None), P("row", "col", None, None)),
        check_vma=False,
    )
```

```python
import functools

import jax
import jax.numpy as jnp
from jax import lax
from jax.experimental import pallas as pl
from jax.experimental.pallas import tpu as pltpu
from jax.sharding import PartitionSpec as P

BF16 = jnp.bfloat16
F32 = jnp.float32
VMEM_LIMIT = 48 * 1024 * 1024


def partner(index, slot):
    return index ^ slot


def turned(slot):
    return slot ^ (((slot >> 1) ^ (slot >> 2)) & 1) * 6


def seen(slot, index):
    return slot ^ (index & 1) * (turned(slot) ^ slot)


def order(size):
    return [0, *reversed(range(3, size, 2))]


def column_order(size):
    return order(size) + [turned(slot) ^ 1 for slot in order(size)]


def permuted(block, axis, size, slot):
    return lax.ppermute(block, axis, [(i, partner(i, slot)) for i in range(size)])


def fetched(block, axis, size, slot):
    return lax.ppermute(block, axis, [(partner(i, seen(slot, i)), i) for i in range(size)])


def fetch_chips(block, axis, size):
    return [fetched(block, axis, size, slot) for slot in order(size)[1:]]


def fetch_core(blocks, axis, size):
    return permuted(blocks, axis, size, 1)


def both_cores(blocks, axis, size):
    found = jnp.concatenate([blocks, fetch_core(blocks, axis, size)])
    return found[jnp.argsort(jnp.array(column_order(size)))]


def send_across(blocks, n_row, n_col):
    arrived = []
    for slot in reversed(range(n_col)):
        pairs = [
            (row * n_col + col, partner(row, 1) * n_col + partner(col, slot))
            for row in range(n_row)
            for col in range(n_col)
        ]
        arrived.append(lax.ppermute(blocks[slot], ("row", "col"), pairs))
    return arrived


def send_each(blocks, axis, size):
    return [permuted(blocks[slot], axis, size, slot) for slot in reversed(range(1, size))]


def call(kernel, out_shape, operands, specs=None, scratch=(), cost=None, out_specs=None):
    vmem = pl.BlockSpec(memory_space=pltpu.VMEM)
    return pl.pallas_call(
        kernel,
        out_shape=out_shape,
        in_specs=specs or [vmem] * len(operands),
        out_specs=out_specs or jax.tree.map(lambda _: vmem, out_shape),
        scratch_shapes=list(scratch),
        cost_estimate=cost,
        compiler_params=pltpu.CompilerParams(vmem_limit_bytes=VMEM_LIMIT),
    )(*operands)


def dot_nt(left, right):
    return lax.dot_general(left, right, (((1,), (1,)), ((), ())), preferred_element_type=F32)


def build_kernel(
    n_row, n_col, chunks, count, coords_hbm, tiles_hbm, dense_ref, coords, tiles, first, second, sems, coords_sem
):
    slots, block = tiles.shape[0], tiles.shape[1]
    per, part = slots // chunks, block // 2
    copies = [
        pltpu.make_async_copy(
            tiles_hbm.at[pl.ds(i * per, per)], tiles.at[pl.ds(i * per, per)], sems.at[i]
        )
        for i in range(chunks)
    ]
    coords_copy = pltpu.make_async_copy(coords_hbm, coords, coords_sem)
    coords_copy.start()
    live = count[0, 0]
    for i, copy in enumerate(copies):
        pl.when(i * per < live)(copy.start)
    row, col = lax.axis_index("row"), lax.axis_index("col")
    first[...] = jnp.zeros_like(first)
    second[...] = jnp.zeros_like(second)
    coords_copy.wait()

    def place(t):
        at = partner(coords[0, t], col) * n_row + seen(partner(coords[1, t], row), row)
        return jnp.where(t < live, at, n_row * n_col)

    for i in range(chunks):

        @pl.when(i * per < live)
        def _():
            copies[i].wait()

            @pl.loop(0, per, unroll=8)
            def _(step):
                t = i * per + step
                at = place(t)
                first[at] += tiles[t, :part].astype(F32)
                second[at] += tiles[t, part:].astype(F32)

    for k in range(n_col):
        for j, slot in enumerate(column_order(n_row)):
            at = k * n_row + slot
            columns = slice(j * block, (j + 1) * block)
            dense_ref[k * block : k * block + part, columns] = first[at].astype(BF16)
            dense_ref[k * block + part : (k + 1) * block, columns] = second[at].astype(BF16)


def prepare_kernel(mask, bias, history, *refs):
    kept_out, bias_out, wide = refs[-3:]
    block, classes = history.shape[0], bias.shape[1]
    mask_cols = jnp.broadcast_to(mask[...].astype(F32), (block, block)).T
    chosen = jnp.concatenate([mask_cols] * (history.shape[1] // block), axis=1) == 1.0
    kept_out[...] = jnp.where(chosen, -1.0, history[...].astype(F32)).astype(BF16)
    wide[...] = jnp.zeros_like(wide)
    wide[:, :classes] = jnp.broadcast_to(bias[...], (block, classes))
    bias_out[...] = wide[...].T[:classes]


def join_rows_kernel(places, *refs):
    out = refs[-1]
    block = refs[0].shape[0]
    for ref, place in zip(refs, places):
        out[place * block : (place + 1) * block, :] = ref[...]


def half_one_kernel(dense_ref, mine_ref, out):
    half = mine_ref.shape[0]
    out[...] = jnp.dot(dense_ref[:, :half], mine_ref[...], preferred_element_type=F32)


def layer_one_kernel(slots, dense_ref, first_ref, other_ref, *refs):
    outputs = refs[-len(slots) :]
    half, block = other_ref.shape[0], outputs[0].shape[0]
    at = slice(slots[0] * block, (slots[-1] + 1) * block)
    total = first_ref[at, :] + jnp.dot(
        dense_ref[at, half:], other_ref[...], preferred_element_type=F32
    )
    for i, out in enumerate(outputs):
        out[...] = total[i * block : (i + 1) * block, :].astype(BF16)


def begin_kernel(base, *refs):
    total = base[: refs[-1].shape[0], :].astype(F32)
    for ref in refs[:-1]:
        total += ref[...].astype(F32)
    refs[-1][...] = total


def hidden_kernel(begun, *refs):
    parts = refs[:-6]
    w_one, b_one, w_two, kept, pushed_ref, proj_ref = refs[-6:]
    total = begun[...]
    for part in parts:
        total += part[...].astype(F32)
    pre = jnp.dot(total.astype(BF16), w_one[...], preferred_element_type=F32) + b_one[...]
    hidden = jnp.maximum(pre, 0.0)
    old = kept[...].astype(F32)
    pushed = jnp.where(old < 0.0, hidden, old).astype(BF16)
    pushed_ref[...] = pushed
    proj_ref[...] = dot_nt(w_two[...], pushed).astype(BF16)


def write_kernel(value, out):
    out[...] = value[...]


def late_kernel(value, after, out):
    del after
    out[...] = value[...]


def lanes(refs, scratch, places=None):
    block = refs[0].shape[1]
    for i, ref in zip(places or range(len(refs)), refs):
        scratch[:, i * block : (i + 1) * block] = ref[...]
    return scratch[...]


def half_two_kernel(places, dense_ref, *refs):
    blocks, (out, scratch) = refs[:-2], refs[-2:]
    half = dense_ref.shape[1] // 2
    out[...] = dot_nt(
        lanes(blocks, scratch, places), dense_ref[:, half : half + scratch.shape[1]]
    )


def layer_two_kernel(slots, dense_ref, first_ref, near_ref, rest_ref, *refs):
    outputs = refs[-len(slots) :]
    block, half = near_ref.shape[1], rest_ref.shape[1]
    at = slice(slots[0] * block, (slots[-1] + 1) * block)
    total = first_ref[:, at] + dot_nt(rest_ref[...], dense_ref[at, :half])
    total += dot_nt(near_ref[...], dense_ref[at, dense_ref.shape[1] - block :])
    for i, out in enumerate(outputs):
        out[...] = total[:, i * block : (i + 1) * block].astype(BF16)


def farthest_two_kernel(slot, dense_ref, first_ref, own_ref, near_ref, *refs):
    blocks, (out, rest) = refs[:-2], refs[-2:]
    lanes([own_ref, *blocks], rest)
    layer_two_kernel([slot], dense_ref, first_ref, near_ref, rest, out)


def logits_kernel(pieces, begun, *refs):
    parts, (out_hbm, staged, sems) = refs[:-3], refs[-3:]
    step = -(-staged.shape[0] // pieces // 16) * 16
    copies = []
    for i in range(pieces):
        rows = slice(i * step, (i + 1) * step if i < pieces - 1 else staged.shape[0])
        total = begun[rows, :]
        for part in parts:
            total += part[rows, :].astype(F32)
        staged[rows, 0, :] = total
        copies.append(pltpu.make_async_copy(staged.at[rows], out_hbm.at[rows], sems.at[i]))
        copies[-1].start()
    for copy in copies:
        copy.wait()


def tiles_kernel(
    n_row, n_col, transposed, coords_ref, count_ref, tiles_ref, stacked_ref, out_ref, total
):
    row, col = lax.axis_index("row"), lax.axis_index("col")
    total[...] = jnp.zeros_like(total)

    @pl.loop(0, count_ref[0, 0])
    def _(t):
        k = partner(coords_ref[0, t], col)
        j = seen(partner(coords_ref[1, t], row), row)
        if transposed:
            total[k] += dot_nt(stacked_ref[j], tiles_ref[t])
        else:
            total[k] += jnp.dot(tiles_ref[t], stacked_ref[j], preferred_element_type=F32)

    out_ref[...] = total[...].astype(BF16)


def on_device(
    n_row, n_col,
    features, tiles, tile_coords, tile_count, batch_mask, history,
    weight_one, bias_one, weight_two, bias_two,
):
    feat, tile_set, hist = features[0, 0], tiles[0, 0], history[0, 0]
    coords = tile_coords[0, 0].T
    slots, block = tile_set.shape[0], tile_set.shape[1]
    f_in, hid, classes = feat.shape[1], weight_one.shape[1], weight_two.shape[1]
    w_two_t = weight_two.T
    dense_form = n_row * n_col <= slots
    smem = pl.BlockSpec(memory_space=pltpu.SMEM)
    vmem = pl.BlockSpec(memory_space=pltpu.VMEM)
    hbm = pl.BlockSpec(memory_space=pltpu.HBM)
    shape = jax.ShapeDtypeStruct

    def prepare(*after):
        return call(
            prepare_kernel,
            (shape((block, hid), BF16), shape((classes, block), F32)),
            (batch_mask[0], bias_two[None], hist, *after),
            specs=[vmem] * 3 + [pl.BlockSpec(memory_space=pl.ANY)] * len(after),
            scratch=[pltpu.VMEM((block, -(-classes // 128) * 128), F32)],
        )

    chips_one = [feat, *fetch_chips(feat, "row", n_row)]

    if dense_form:
        anywhere = pl.BlockSpec(memory_space=pl.ANY)
        chunks = 8
        dense = call(
            functools.partial(build_kernel, n_row, n_col, chunks),
            shape((n_col * block, n_row * block), BF16),
            (
                tile_count,
                pltpu.with_memory_space_constraint(coords, pltpu.HBM),
                pltpu.with_memory_space_constraint(tile_set, pltpu.HBM),
            ),
            specs=[smem, hbm, hbm],
            scratch=[
                pltpu.SMEM((2, slots), jnp.int32),
                pltpu.VMEM((slots, block, block), BF16),
                pltpu.VMEM((n_row * n_col + 1, block // 2, block), F32),
                pltpu.VMEM((n_row * n_col + 1, block // 2, block), F32),
                pltpu.SemaphoreType.DMA((chunks,)),
                pltpu.SemaphoreType.DMA(()),
            ],
            cost=pl.CostEstimate(
                flops=slots * block * block,
                bytes_accessed=2 * slots * block * block,
                transcendentals=0,
            ),
        )
        names = order(n_row)
        places_one = [0, *sorted(range(1, n_row // 2), key=lambda i: (names[i] != 5, names[i]))]
        mine_one = call(
            functools.partial(join_rows_kernel, places_one),
            shape((n_row // 2 * block, f_in), BF16),
            (*[chips_one[i] for i in places_one], dense),
            specs=[vmem] * len(chips_one) + [anywhere],
        )
        other_one = fetch_core(mine_one, "row", n_row)
        kept, bias_cols = prepare(mine_one)
        half_one = call(half_one_kernel, shape((n_col * block, f_in), F32), (dense, mine_one))
        far, others = n_col - 1, range(1, n_col - 1)
        far_one = call(
            functools.partial(layer_one_kernel, [far]),
            [shape((block, f_in), BF16)],
            (dense, half_one, other_one),
        )
        near_one = call(
            functools.partial(layer_one_kernel, range(far)),
            [shape((block, f_in), BF16)] * far,
            (dense, half_one, other_one, *far_one),
            specs=[vmem] * 3 + [anywhere],
        )
        parts_one = [*near_one, *far_one]
    else:
        kept, bias_cols = prepare()
        summed = call(
            functools.partial(tiles_kernel, n_row, n_col, False),
            shape((n_col, block, f_in), BF16),
            (coords, tile_count, tile_set, both_cores(jnp.stack(chips_one), "row", n_row)),
            specs=[smem, smem, vmem, vmem],
            scratch=[pltpu.VMEM((n_col, block, f_in), F32)],
        )
        parts_one = [summed[k] for k in range(n_col)]
        other_one = fetch_core(feat, "row", n_row)

    arrived_one = send_across(parts_one, n_row, n_col)
    kept = fetch_core(kept, "row", n_row)
    begun_one = call(
        begin_kernel, shape((block, f_in), F32), (other_one, arrived_one[0])
    )
    pushed, proj = call(
        hidden_kernel,
        (shape((block, hid), BF16), shape((classes, block), BF16)),
        (begun_one, *arrived_one[1:], weight_one, bias_one[None], w_two_t, kept),
    )
    chips_two = [proj, *fetch_chips(proj, "row", n_row)]
    if dense_form:
        near = chips_two[order(n_row).index(5)]
        early = [x for x in chips_two if x is not near]
        near_other = fetched(proj, "row", n_row, 2)
        others_two = [fetch_core(x, "row", n_row) for x in early] + [near_other]
        own_proj = others_two[0]
    else:
        own_proj = fetch_core(proj, "row", n_row)

    if dense_form:
        late = others_two
        places_two = [0, *reversed(range(1, len(early)))]
        half_two = call(
            functools.partial(half_two_kernel, places_two),
            shape((classes, n_col * block), F32),
            (dense, *[early[i] for i in places_two]),
            scratch=[pltpu.VMEM((classes, len(early) * block), BF16)],
        )
        pushed = call(
            late_kernel, shape((block, hid), BF16), (pushed, half_two), specs=[vmem, anywhere]
        )
        far_two, rest = call(
            functools.partial(farthest_two_kernel, far),
            [shape((classes, block), BF16), shape((classes, len(late) * block), BF16)],
            (dense, half_two, late[0], near, *late[1:]),
        )
        middle_two = call(
            functools.partial(layer_two_kernel, others),
            [shape((classes, block), BF16)] * len(others),
            (dense, half_two, near, rest),
        )
        own_two = call(
            functools.partial(layer_two_kernel, [0]),
            [shape((classes, block), BF16)],
            (dense, half_two, near, rest, middle_two[0]),
            specs=[vmem] * 4 + [anywhere],
        )
        parts_two = [*own_two, *middle_two, far_two]
    else:
        other_slots = jnp.arange(n_row) ^ 1
        summed = call(
            functools.partial(tiles_kernel, n_row, n_col, True),
            shape((n_col, classes, block), BF16),
            (coords, tile_count, tile_set, both_cores(jnp.stack(chips_two), "row", n_row)[other_slots]),
            specs=[smem, smem, vmem, vmem],
            scratch=[pltpu.VMEM((n_col, classes, block), F32)],
        )
        parts_two = [summed[k] for k in range(n_col)]

    arrived_two = send_each(parts_two, "col", n_col)
    pushed = call(write_kernel, shape((block, hid), BF16), (fetch_core(pushed, "row", n_row),))
    pieces = 4
    begun_two = call(
        begin_kernel,
        shape((classes, block), F32),
        (bias_cols, own_proj, parts_two[0], arrived_two[0]),
    )
    scores = call(
        functools.partial(logits_kernel, pieces),
        shape((classes, 1, block), F32),
        (begun_two, *arrived_two[1:]),
        scratch=[pltpu.VMEM((classes, 1, block), F32), pltpu.SemaphoreType.DMA((pieces,))],
        out_specs=pl.BlockSpec(memory_space=pl.ANY),
    )
    return pushed[None, None], scores.transpose(1, 2, 0)[None]


def solution(mesh):
    sizes = mesh.shape
    return jax.shard_map(
        functools.partial(on_device, sizes["row"], sizes["col"]),
        mesh=mesh,
        in_specs=(
            P("row", "col", None, None),
            P("row", "col", None, None, None),
            P("row", "col", None, None),
            P("row", "col"),
            P("row", "col", None),
            P("row", "col", None, None),
            P(),
            P(),
            P(),
            P(),
        ),
        out_specs=(P("row", "col", None, None), P("row", "col", None, None)),
        check_vma=False,
    )
```

```python
import functools

import jax
import jax.numpy as jnp
from jax import lax
from jax.experimental import pallas as pl
from jax.experimental.pallas import tpu as pltpu
from jax.sharding import PartitionSpec as P

BF16 = jnp.bfloat16
F32 = jnp.float32
VMEM_LIMIT = 48 * 1024 * 1024


def partner(index, slot):
    return index ^ slot


def turned(slot):
    return slot ^ (((slot >> 1) ^ (slot >> 2)) & 1) * 6


def seen(slot, index):
    return slot ^ (index & 1) * (turned(slot) ^ slot)


def order(size):
    return [0, *reversed(range(3, size, 2))]


def column_order(size):
    return order(size) + [turned(slot) ^ 1 for slot in order(size)]


def permuted(block, axis, size, slot):
    return lax.ppermute(block, axis, [(i, partner(i, slot)) for i in range(size)])


def fetched(block, axis, size, slot):
    return lax.ppermute(block, axis, [(partner(i, seen(slot, i)), i) for i in range(size)])


def fetch_chips(block, axis, size):
    return [fetched(block, axis, size, slot) for slot in order(size)[1:]]


def fetch_core(blocks, axis, size):
    return permuted(blocks, axis, size, 1)


def both_cores(blocks, axis, size):
    found = jnp.concatenate([blocks, fetch_core(blocks, axis, size)])
    return found[jnp.argsort(jnp.array(column_order(size)))]


def send_across(blocks, n_row, n_col):
    arrived = []
    for slot in reversed(range(n_col)):
        pairs = [
            (row * n_col + col, partner(row, 1) * n_col + partner(col, slot))
            for row in range(n_row)
            for col in range(n_col)
        ]
        arrived.append(lax.ppermute(blocks[slot], ("row", "col"), pairs))
    return arrived


def send_each(blocks, axis, size):
    slots = [size - 1, *range(1, size - 1)]
    return [permuted(blocks[slot], axis, size, slot) for slot in slots]


def call(kernel, out_shape, operands, specs=None, scratch=(), cost=None, out_specs=None):
    vmem = pl.BlockSpec(memory_space=pltpu.VMEM)
    return pl.pallas_call(
        kernel,
        out_shape=out_shape,
        in_specs=specs or [vmem] * len(operands),
        out_specs=out_specs or jax.tree.map(lambda _: vmem, out_shape),
        scratch_shapes=list(scratch),
        cost_estimate=cost,
        compiler_params=pltpu.CompilerParams(vmem_limit_bytes=VMEM_LIMIT),
    )(*operands)


def dot_nt(left, right):
    return lax.dot_general(left, right, (((1,), (1,)), ((), ())), preferred_element_type=F32)


def build_kernel(
    n_row, n_col, chunks, count, coords_hbm, tiles_hbm, dense_ref, coords, tiles, first, second, sems, coords_sem
):
    slots, block = tiles.shape[0], tiles.shape[1]
    per, part = slots // chunks, block // 2
    copies = [
        pltpu.make_async_copy(
            tiles_hbm.at[pl.ds(i * per, per)], tiles.at[pl.ds(i * per, per)], sems.at[i]
        )
        for i in range(chunks)
    ]
    coords_copy = pltpu.make_async_copy(coords_hbm, coords, coords_sem)
    coords_copy.start()
    live = count[0, 0]
    for i, copy in enumerate(copies):
        pl.when(i * per < live)(copy.start)
    row, col = lax.axis_index("row"), lax.axis_index("col")
    first[...] = jnp.zeros_like(first)
    second[...] = jnp.zeros_like(second)
    coords_copy.wait()

    def place(t):
        at = partner(coords[0, t], col) * n_row + seen(partner(coords[1, t], row), row)
        return jnp.where(t < live, at, n_row * n_col)

    for i in range(chunks):

        @pl.when(i * per < live)
        def _():
            copies[i].wait()

            @pl.loop(0, per, unroll=8)
            def _(step):
                t = i * per + step
                at = place(t)
                first[at] += tiles[t, :part].astype(F32)
                second[at] += tiles[t, part:].astype(F32)

    for k in range(n_col):
        for j, slot in enumerate(column_order(n_row)):
            at = k * n_row + slot
            columns = slice(j * block, (j + 1) * block)
            dense_ref[k * block : k * block + part, columns] = first[at].astype(BF16)
            dense_ref[k * block + part : (k + 1) * block, columns] = second[at].astype(BF16)


def prepare_kernel(mask, bias, history, *refs):
    kept_out, bias_out, wide = refs[-3:]
    block, classes = history.shape[0], bias.shape[1]
    mask_cols = jnp.broadcast_to(mask[...].astype(F32), (block, block)).T
    chosen = jnp.concatenate([mask_cols] * (history.shape[1] // block), axis=1) == 1.0
    kept_out[...] = jnp.where(chosen, -1.0, history[...].astype(F32)).astype(BF16)
    wide[...] = jnp.zeros_like(wide)
    wide[:, :classes] = jnp.broadcast_to(bias[...], (block, classes))
    bias_out[...] = wide[...].T[:classes]


def join_rows_kernel(places, *refs):
    out = refs[-1]
    block = refs[0].shape[0]
    for ref, place in zip(refs, places):
        out[place * block : (place + 1) * block, :] = ref[...]


def half_one_kernel(dense_ref, mine_ref, out):
    half = mine_ref.shape[0]
    out[...] = jnp.dot(dense_ref[:, :half], mine_ref[...], preferred_element_type=F32)


def layer_one_kernel(dense_ref, first_ref, other_ref, *outputs):
    half, block = other_ref.shape[0], dense_ref.shape[0] // len(outputs)
    total = first_ref[...] + jnp.dot(
        dense_ref[:, half:], other_ref[...], preferred_element_type=F32
    )
    for k, out in enumerate(outputs):
        out[...] = total[k * block : (k + 1) * block, :].astype(BF16)


def hidden_kernel(n_col, *refs):
    parts = refs[:n_col]
    feats, w_one, b_one, w_two, kept, pushed_ref, proj_ref = refs[n_col:]
    total = feats[: kept.shape[0], :].astype(F32)
    for part in parts:
        total += part[...].astype(F32)
    pre = jnp.dot(total.astype(BF16), w_one[...], preferred_element_type=F32) + b_one[...]
    hidden = jnp.maximum(pre, 0.0)
    old = kept[...].astype(F32)
    pushed = jnp.where(old < 0.0, hidden, old).astype(BF16)
    pushed_ref[...] = pushed
    proj_ref[...] = dot_nt(w_two[...], pushed).astype(BF16)


def write_kernel(value, out):
    out[...] = value[...]


def late_kernel(value, after, out):
    del after
    out[...] = value[...]


def lanes(refs, scratch, places=None):
    block = refs[0].shape[1]
    for i, ref in zip(places or range(len(refs)), refs):
        scratch[:, i * block : (i + 1) * block] = ref[...]
    return scratch[...]


def half_two_kernel(places, dense_ref, *refs):
    blocks, (out, scratch) = refs[:-2], refs[-2:]
    half = dense_ref.shape[1] // 2
    out[...] = dot_nt(
        lanes(blocks, scratch, places), dense_ref[:, half : half + scratch.shape[1]]
    )


def layer_two_kernel(n_col, dense_ref, first_ref, own_ref, near_ref, *refs):
    blocks, outputs, scratch = refs[: -n_col - 1], refs[-n_col - 1 : -1], refs[-1]
    block, half = near_ref.shape[1], scratch.shape[1]
    rest = lanes([own_ref, *blocks], scratch)
    total = first_ref[...] + dot_nt(rest, dense_ref[:, :half])
    total += dot_nt(near_ref[...], dense_ref[:, dense_ref.shape[1] - block :])
    for k, out in enumerate(outputs):
        out[...] = total[:, k * block : (k + 1) * block].astype(BF16)


def logits_kernel(n_col, pieces, *refs):
    parts = refs[:n_col]
    proj, bias, out_hbm, staged, sems = refs[n_col:]
    step = -(-staged.shape[0] // pieces // 16) * 16
    copies = []
    for i in range(pieces):
        rows = slice(i * step, (i + 1) * step if i < pieces - 1 else staged.shape[0])
        total = proj[rows, :].astype(F32) + bias[rows, :]
        for part in parts:
            total += part[rows, :].astype(F32)
        staged[rows, 0, :] = total
        copies.append(pltpu.make_async_copy(staged.at[rows], out_hbm.at[rows], sems.at[i]))
        copies[-1].start()
    for copy in copies:
        copy.wait()


def tiles_kernel(
    n_row, n_col, transposed, coords_ref, count_ref, tiles_ref, stacked_ref, out_ref, total
):
    row, col = lax.axis_index("row"), lax.axis_index("col")
    total[...] = jnp.zeros_like(total)

    @pl.loop(0, count_ref[0, 0])
    def _(t):
        k = partner(coords_ref[0, t], col)
        j = seen(partner(coords_ref[1, t], row), row)
        if transposed:
            total[k] += dot_nt(stacked_ref[j], tiles_ref[t])
        else:
            total[k] += jnp.dot(tiles_ref[t], stacked_ref[j], preferred_element_type=F32)

    out_ref[...] = total[...].astype(BF16)


def on_device(
    n_row, n_col,
    features, tiles, tile_coords, tile_count, batch_mask, history,
    weight_one, bias_one, weight_two, bias_two,
):
    feat, tile_set, hist = features[0, 0], tiles[0, 0], history[0, 0]
    coords = tile_coords[0, 0].T
    slots, block = tile_set.shape[0], tile_set.shape[1]
    f_in, hid, classes = feat.shape[1], weight_one.shape[1], weight_two.shape[1]
    w_two_t = weight_two.T
    dense_form = n_row * n_col <= slots
    smem = pl.BlockSpec(memory_space=pltpu.SMEM)
    vmem = pl.BlockSpec(memory_space=pltpu.VMEM)
    hbm = pl.BlockSpec(memory_space=pltpu.HBM)
    shape = jax.ShapeDtypeStruct

    def prepare(*after):
        return call(
            prepare_kernel,
            (shape((block, hid), BF16), shape((classes, block), F32)),
            (batch_mask[0], bias_two[None], hist, *after),
            specs=[vmem] * 3 + [pl.BlockSpec(memory_space=pl.ANY)] * len(after),
            scratch=[pltpu.VMEM((block, -(-classes // 128) * 128), F32)],
        )

    chips_one = [feat, *fetch_chips(feat, "row", n_row)]

    if dense_form:
        anywhere = pl.BlockSpec(memory_space=pl.ANY)
        chunks = 8
        dense = call(
            functools.partial(build_kernel, n_row, n_col, chunks),
            shape((n_col * block, n_row * block), BF16),
            (
                tile_count,
                pltpu.with_memory_space_constraint(coords, pltpu.HBM),
                pltpu.with_memory_space_constraint(tile_set, pltpu.HBM),
            ),
            specs=[smem, hbm, hbm],
            scratch=[
                pltpu.SMEM((2, slots), jnp.int32),
                pltpu.VMEM((slots, block, block), BF16),
                pltpu.VMEM((n_row * n_col + 1, block // 2, block), F32),
                pltpu.VMEM((n_row * n_col + 1, block // 2, block), F32),
                pltpu.SemaphoreType.DMA((chunks,)),
                pltpu.SemaphoreType.DMA(()),
            ],
            cost=pl.CostEstimate(
                flops=slots * block * block,
                bytes_accessed=2 * slots * block * block,
                transcendentals=0,
            ),
        )
        names = order(n_row)
        places_one = [0, *sorted(range(1, n_row // 2), key=lambda i: (names[i] != 5, names[i]))]
        mine_one = call(
            functools.partial(join_rows_kernel, places_one),
            shape((n_row // 2 * block, f_in), BF16),
            (*[chips_one[i] for i in places_one], dense),
            specs=[vmem] * len(chips_one) + [anywhere],
        )
        other_one = fetch_core(mine_one, "row", n_row)
        kept, bias_cols = prepare(mine_one)
        half_one = call(half_one_kernel, shape((n_col * block, f_in), F32), (dense, mine_one))
        parts_one = call(
            layer_one_kernel,
            [shape((block, f_in), BF16)] * n_col,
            (dense, half_one, other_one),
        )
    else:
        kept, bias_cols = prepare()
        summed = call(
            functools.partial(tiles_kernel, n_row, n_col, False),
            shape((n_col, block, f_in), BF16),
            (coords, tile_count, tile_set, both_cores(jnp.stack(chips_one), "row", n_row)),
            specs=[smem, smem, vmem, vmem],
            scratch=[pltpu.VMEM((n_col, block, f_in), F32)],
        )
        parts_one = [summed[k] for k in range(n_col)]
        other_one = fetch_core(feat, "row", n_row)

    arrived_one = send_across(parts_one, n_row, n_col)
    kept = fetch_core(kept, "row", n_row)
    pushed, proj = call(
        functools.partial(hidden_kernel, n_col),
        (shape((block, hid), BF16), shape((classes, block), BF16)),
        (*arrived_one, other_one, weight_one, bias_one[None], w_two_t, kept),
    )
    chips_two = [proj, *fetch_chips(proj, "row", n_row)]
    if dense_form:
        near = chips_two[order(n_row).index(5)]
        early = [x for x in chips_two if x is not near]
        near_other = fetched(proj, "row", n_row, 2)
        others_two = [fetch_core(x, "row", n_row) for x in early] + [near_other]
        own_proj = others_two[0]
    else:
        own_proj = fetch_core(proj, "row", n_row)

    if dense_form:
        late = others_two
        places_two = [0, *reversed(range(1, len(early)))]
        half_two = call(
            functools.partial(half_two_kernel, places_two),
            shape((classes, n_col * block), F32),
            (dense, *[early[i] for i in places_two]),
            scratch=[pltpu.VMEM((classes, len(early) * block), BF16)],
        )
        pushed = call(
            late_kernel, shape((block, hid), BF16), (pushed, half_two), specs=[vmem, anywhere]
        )
        parts_two = call(
            functools.partial(layer_two_kernel, n_col),
            [shape((classes, block), BF16)] * n_col,
            (dense, half_two, late[0], near, *late[1:]),
            scratch=[pltpu.VMEM((classes, len(late) * block), BF16)],
        )
    else:
        other_slots = jnp.arange(n_row) ^ 1
        summed = call(
            functools.partial(tiles_kernel, n_row, n_col, True),
            shape((n_col, classes, block), BF16),
            (coords, tile_count, tile_set, both_cores(jnp.stack(chips_two), "row", n_row)[other_slots]),
            specs=[smem, smem, vmem, vmem],
            scratch=[pltpu.VMEM((n_col, classes, block), F32)],
        )
        parts_two = [summed[k] for k in range(n_col)]

    arrived_two = send_each(parts_two, "col", n_col)
    pushed = call(write_kernel, shape((block, hid), BF16), (fetch_core(pushed, "row", n_row),))
    pieces = 4
    scores = call(
        functools.partial(logits_kernel, n_col, pieces),
        shape((classes, 1, block), F32),
        (parts_two[0], *arrived_two, own_proj, bias_cols),
        scratch=[pltpu.VMEM((classes, 1, block), F32), pltpu.SemaphoreType.DMA((pieces,))],
        out_specs=pl.BlockSpec(memory_space=pl.ANY),
    )
    return pushed[None, None], scores.transpose(1, 2, 0)[None]


def solution(mesh):
    sizes = mesh.shape
    return jax.shard_map(
        functools.partial(on_device, sizes["row"], sizes["col"]),
        mesh=mesh,
        in_specs=(
            P("row", "col", None, None),
            P("row", "col", None, None, None),
            P("row", "col", None, None),
            P("row", "col"),
            P("row", "col", None),
            P("row", "col", None, None),
            P(),
            P(),
            P(),
            P(),
        ),
        out_specs=(P("row", "col", None, None), P("row", "col", None, None)),
        check_vma=False,
    )
```

```python
import functools

import jax
import jax.numpy as jnp
from jax import lax
from jax.experimental import pallas as pl
from jax.experimental.pallas import tpu as pltpu
from jax.sharding import PartitionSpec as P

BF16 = jnp.bfloat16
F32 = jnp.float32
VMEM_LIMIT = 48 * 1024 * 1024


def partner(index, slot):
    return index ^ slot


def turned(slot):
    return slot ^ (((slot >> 1) ^ (slot >> 2)) & 1) * 6


def seen(slot, index):
    return slot ^ (index & 1) * (turned(slot) ^ slot)


def order(size):
    return [0, *reversed(range(3, size, 2))]


def column_order(size):
    return order(size) + [turned(slot) ^ 1 for slot in order(size)]


def permuted(block, axis, size, slot):
    return lax.ppermute(block, axis, [(i, partner(i, slot)) for i in range(size)])


def fetched(block, axis, size, slot):
    return lax.ppermute(block, axis, [(partner(i, seen(slot, i)), i) for i in range(size)])


def fetch_chips(block, axis, size):
    return [fetched(block, axis, size, slot) for slot in order(size)[1:]]


def fetch_core(blocks, axis, size):
    return permuted(blocks, axis, size, 1)


def both_cores(blocks, axis, size):
    found = jnp.concatenate([blocks, fetch_core(blocks, axis, size)])
    return found[jnp.argsort(jnp.array(column_order(size)))]


def send_across(blocks, n_row, n_col):
    arrived = []
    for slot in reversed(range(n_col)):
        pairs = [
            (row * n_col + col, partner(row, 1) * n_col + partner(col, slot))
            for row in range(n_row)
            for col in range(n_col)
        ]
        arrived.append(lax.ppermute(blocks[slot], ("row", "col"), pairs))
    return arrived


def send_plan(size):
    far = size - 1
    return list(zip([far, *reversed(range(1, far))], [far, *range(1, far)]))


def by_core(pair, pick):
    if pair[0] == pair[1]:
        return pick(pair[0])
    return jnp.where((lax.axis_index("row") & 1) == 0, pick(pair[0]), pick(pair[1]))


def send_each(blocks, n_row, n_col):
    arrived = []
    for block, slots in zip(blocks, send_plan(n_col)):
        pairs = [
            (row * n_col + col, row * n_col + partner(col, slots[row & 1]))
            for row in range(n_row)
            for col in range(n_col)
        ]
        arrived.append(lax.ppermute(block, ("row", "col"), pairs))
    return arrived


def call(kernel, out_shape, operands, specs=None, scratch=(), cost=None, out_specs=None):
    vmem = pl.BlockSpec(memory_space=pltpu.VMEM)
    return pl.pallas_call(
        kernel,
        out_shape=out_shape,
        in_specs=specs or [vmem] * len(operands),
        out_specs=out_specs or jax.tree.map(lambda _: vmem, out_shape),
        scratch_shapes=list(scratch),
        cost_estimate=cost,
        compiler_params=pltpu.CompilerParams(vmem_limit_bytes=VMEM_LIMIT),
    )(*operands)


def dot_nt(left, right):
    return lax.dot_general(left, right, (((1,), (1,)), ((), ())), preferred_element_type=F32)


def build_kernel(
    n_row, n_col, chunks, count, coords_hbm, tiles_hbm, dense_ref, coords, tiles, first, second, sems, coords_sem
):
    slots, block = tiles.shape[0], tiles.shape[1]
    per, part = slots // chunks, block // 2
    copies = [
        pltpu.make_async_copy(
            tiles_hbm.at[pl.ds(i * per, per)], tiles.at[pl.ds(i * per, per)], sems.at[i]
        )
        for i in range(chunks)
    ]
    coords_copy = pltpu.make_async_copy(coords_hbm, coords, coords_sem)
    coords_copy.start()
    live = count[0, 0]
    for i, copy in enumerate(copies):
        pl.when(i * per < live)(copy.start)
    row, col = lax.axis_index("row"), lax.axis_index("col")
    first[...] = jnp.zeros_like(first)
    second[...] = jnp.zeros_like(second)
    coords_copy.wait()

    def place(t):
        at = partner(coords[0, t], col) * n_row + seen(partner(coords[1, t], row), row)
        return jnp.where(t < live, at, n_row * n_col)

    for i in range(chunks):

        @pl.when(i * per < live)
        def _():
            copies[i].wait()

            @pl.loop(0, per, unroll=8)
            def _(step):
                t = i * per + step
                at = place(t)
                first[at] += tiles[t, :part].astype(F32)
                second[at] += tiles[t, part:].astype(F32)

    for k in range(n_col):
        for j, slot in enumerate(column_order(n_row)):
            at = k * n_row + slot
            columns = slice(j * block, (j + 1) * block)
            dense_ref[k * block : k * block + part, columns] = first[at].astype(BF16)
            dense_ref[k * block + part : (k + 1) * block, columns] = second[at].astype(BF16)


def prepare_kernel(mask, bias, history, *refs):
    kept_out, bias_out, wide = refs[-3:]
    block, classes = history.shape[0], bias.shape[1]
    mask_cols = jnp.broadcast_to(mask[...].astype(F32), (block, block)).T
    chosen = jnp.concatenate([mask_cols] * (history.shape[1] // block), axis=1) == 1.0
    kept_out[...] = jnp.where(chosen, -1.0, history[...].astype(F32)).astype(BF16)
    wide[...] = jnp.zeros_like(wide)
    wide[:, :classes] = jnp.broadcast_to(bias[...], (block, classes))
    bias_out[...] = wide[...].T[:classes]


def join_rows_kernel(places, *refs):
    out = refs[-1]
    block = refs[0].shape[0]
    for ref, place in zip(refs, places):
        out[place * block : (place + 1) * block, :] = ref[...]


def half_one_kernel(dense_ref, mine_ref, out):
    half = mine_ref.shape[0]
    out[...] = jnp.dot(dense_ref[:, :half], mine_ref[...], preferred_element_type=F32)


def layer_one_kernel(dense_ref, first_ref, other_ref, *outputs):
    half, block = other_ref.shape[0], dense_ref.shape[0] // len(outputs)
    total = first_ref[...] + jnp.dot(
        dense_ref[:, half:], other_ref[...], preferred_element_type=F32
    )
    for k, out in enumerate(outputs):
        out[...] = total[k * block : (k + 1) * block, :].astype(BF16)


def hidden_kernel(n_col, *refs):
    parts = refs[:n_col]
    feats, w_one, b_one, w_two, kept, pushed_ref, proj_ref = refs[n_col:]
    total = feats[: kept.shape[0], :].astype(F32)
    for part in parts:
        total += part[...].astype(F32)
    pre = jnp.dot(total.astype(BF16), w_one[...], preferred_element_type=F32) + b_one[...]
    hidden = jnp.maximum(pre, 0.0)
    old = kept[...].astype(F32)
    pushed = jnp.where(old < 0.0, hidden, old).astype(BF16)
    pushed_ref[...] = pushed
    proj_ref[...] = dot_nt(w_two[...], pushed).astype(BF16)


def write_kernel(value, out):
    out[...] = value[...]


def late_kernel(value, after, out):
    del after
    out[...] = value[...]


def lanes(refs, scratch, places=None):
    block = refs[0].shape[1]
    for i, ref in zip(places or range(len(refs)), refs):
        scratch[:, i * block : (i + 1) * block] = ref[...]
    return scratch[...]


def half_two_kernel(places, dense_ref, *refs):
    blocks, (out, scratch) = refs[:-2], refs[-2:]
    half = dense_ref.shape[1] // 2
    out[...] = dot_nt(
        lanes(blocks, scratch, places), dense_ref[:, half : half + scratch.shape[1]]
    )


def layer_two_kernel(n_col, dense_ref, first_ref, own_ref, near_ref, *refs):
    blocks, outputs, scratch = refs[: -n_col - 1], refs[-n_col - 1 : -1], refs[-1]
    block, half = near_ref.shape[1], scratch.shape[1]
    rest = lanes([own_ref, *blocks], scratch)
    total = first_ref[...] + dot_nt(rest, dense_ref[:, :half])
    total += dot_nt(near_ref[...], dense_ref[:, dense_ref.shape[1] - block :])
    for pair, out in zip([(0, 0), *send_plan(n_col)], outputs):
        out[...] = by_core(pair, lambda k: total[:, k * block : (k + 1) * block]).astype(BF16)


def logits_kernel(n_col, pieces, *refs):
    parts = refs[:n_col]
    proj, bias, out_hbm, staged, sems = refs[n_col:]
    step = -(-staged.shape[0] // pieces // 16) * 16
    copies = []
    for i in range(pieces):
        rows = slice(i * step, (i + 1) * step if i < pieces - 1 else staged.shape[0])
        total = proj[rows, :].astype(F32) + bias[rows, :]
        for part in parts:
            total += part[rows, :].astype(F32)
        staged[rows, 0, :] = total
        copies.append(pltpu.make_async_copy(staged.at[rows], out_hbm.at[rows], sems.at[i]))
        copies[-1].start()
    for copy in copies:
        copy.wait()


def tiles_kernel(
    n_row, n_col, transposed, coords_ref, count_ref, tiles_ref, stacked_ref, out_ref, total
):
    row, col = lax.axis_index("row"), lax.axis_index("col")
    total[...] = jnp.zeros_like(total)

    @pl.loop(0, count_ref[0, 0])
    def _(t):
        k = partner(coords_ref[0, t], col)
        j = seen(partner(coords_ref[1, t], row), row)
        if transposed:
            total[k] += dot_nt(stacked_ref[j], tiles_ref[t])
        else:
            total[k] += jnp.dot(tiles_ref[t], stacked_ref[j], preferred_element_type=F32)

    out_ref[...] = total[...].astype(BF16)


def on_device(
    n_row, n_col,
    features, tiles, tile_coords, tile_count, batch_mask, history,
    weight_one, bias_one, weight_two, bias_two,
):
    feat, tile_set, hist = features[0, 0], tiles[0, 0], history[0, 0]
    coords = tile_coords[0, 0].T
    slots, block = tile_set.shape[0], tile_set.shape[1]
    f_in, hid, classes = feat.shape[1], weight_one.shape[1], weight_two.shape[1]
    w_two_t = weight_two.T
    dense_form = n_row * n_col <= slots
    smem = pl.BlockSpec(memory_space=pltpu.SMEM)
    vmem = pl.BlockSpec(memory_space=pltpu.VMEM)
    hbm = pl.BlockSpec(memory_space=pltpu.HBM)
    shape = jax.ShapeDtypeStruct

    def prepare(*after):
        return call(
            prepare_kernel,
            (shape((block, hid), BF16), shape((classes, block), F32)),
            (batch_mask[0], bias_two[None], hist, *after),
            specs=[vmem] * 3 + [pl.BlockSpec(memory_space=pl.ANY)] * len(after),
            scratch=[pltpu.VMEM((block, -(-classes // 128) * 128), F32)],
        )

    chips_one = [feat, *fetch_chips(feat, "row", n_row)]

    if dense_form:
        anywhere = pl.BlockSpec(memory_space=pl.ANY)
        chunks = 8
        dense = call(
            functools.partial(build_kernel, n_row, n_col, chunks),
            shape((n_col * block, n_row * block), BF16),
            (
                tile_count,
                pltpu.with_memory_space_constraint(coords, pltpu.HBM),
                pltpu.with_memory_space_constraint(tile_set, pltpu.HBM),
            ),
            specs=[smem, hbm, hbm],
            scratch=[
                pltpu.SMEM((2, slots), jnp.int32),
                pltpu.VMEM((slots, block, block), BF16),
                pltpu.VMEM((n_row * n_col + 1, block // 2, block), F32),
                pltpu.VMEM((n_row * n_col + 1, block // 2, block), F32),
                pltpu.SemaphoreType.DMA((chunks,)),
                pltpu.SemaphoreType.DMA(()),
            ],
            cost=pl.CostEstimate(
                flops=slots * block * block,
                bytes_accessed=2 * slots * block * block,
                transcendentals=0,
            ),
        )
        names = order(n_row)
        places_one = [0, *sorted(range(1, n_row // 2), key=lambda i: (names[i] != 5, names[i]))]
        mine_one = call(
            functools.partial(join_rows_kernel, places_one),
            shape((n_row // 2 * block, f_in), BF16),
            (*[chips_one[i] for i in places_one], dense),
            specs=[vmem] * len(chips_one) + [anywhere],
        )
        other_one = fetch_core(mine_one, "row", n_row)
        kept, bias_cols = prepare(mine_one)
        half_one = call(half_one_kernel, shape((n_col * block, f_in), F32), (dense, mine_one))
        parts_one = call(
            layer_one_kernel,
            [shape((block, f_in), BF16)] * n_col,
            (dense, half_one, other_one),
        )
    else:
        kept, bias_cols = prepare()
        summed = call(
            functools.partial(tiles_kernel, n_row, n_col, False),
            shape((n_col, block, f_in), BF16),
            (coords, tile_count, tile_set, both_cores(jnp.stack(chips_one), "row", n_row)),
            specs=[smem, smem, vmem, vmem],
            scratch=[pltpu.VMEM((n_col, block, f_in), F32)],
        )
        parts_one = [summed[k] for k in range(n_col)]
        other_one = fetch_core(feat, "row", n_row)

    arrived_one = send_across(parts_one, n_row, n_col)
    kept = fetch_core(kept, "row", n_row)
    pushed, proj = call(
        functools.partial(hidden_kernel, n_col),
        (shape((block, hid), BF16), shape((classes, block), BF16)),
        (*arrived_one, other_one, weight_one, bias_one[None], w_two_t, kept),
    )
    chips_two = [proj, *fetch_chips(proj, "row", n_row)]
    if dense_form:
        near = chips_two[order(n_row).index(5)]
        early = [x for x in chips_two if x is not near]
        near_other = fetched(proj, "row", n_row, 2)
        others_two = [fetch_core(x, "row", n_row) for x in early] + [near_other]
        own_proj = others_two[0]
    else:
        own_proj = fetch_core(proj, "row", n_row)

    if dense_form:
        late = others_two
        places_two = [0, *reversed(range(1, len(early)))]
        half_two = call(
            functools.partial(half_two_kernel, places_two),
            shape((classes, n_col * block), F32),
            (dense, *[early[i] for i in places_two]),
            scratch=[pltpu.VMEM((classes, len(early) * block), BF16)],
        )
        pushed = call(
            late_kernel, shape((block, hid), BF16), (pushed, half_two), specs=[vmem, anywhere]
        )
        parts_two = call(
            functools.partial(layer_two_kernel, n_col),
            [shape((classes, block), BF16)] * n_col,
            (dense, half_two, late[0], near, *late[1:]),
            scratch=[pltpu.VMEM((classes, len(late) * block), BF16)],
        )
    else:
        other_slots = jnp.arange(n_row) ^ 1
        summed = call(
            functools.partial(tiles_kernel, n_row, n_col, True),
            shape((n_col, classes, block), BF16),
            (coords, tile_count, tile_set, both_cores(jnp.stack(chips_two), "row", n_row)[other_slots]),
            specs=[smem, smem, vmem, vmem],
            scratch=[pltpu.VMEM((n_col, classes, block), F32)],
        )
        parts_two = [summed[0], *[by_core(p, lambda k: summed[k]) for p in send_plan(n_col)]]

    arrived_two = send_each(parts_two[1:], n_row, n_col)
    pushed = call(write_kernel, shape((block, hid), BF16), (fetch_core(pushed, "row", n_row),))
    pieces = 4
    scores = call(
        functools.partial(logits_kernel, n_col, pieces),
        shape((classes, 1, block), F32),
        (parts_two[0], *arrived_two, own_proj, bias_cols),
        scratch=[pltpu.VMEM((classes, 1, block), F32), pltpu.SemaphoreType.DMA((pieces,))],
        out_specs=pl.BlockSpec(memory_space=pl.ANY),
    )
    return pushed[None, None], scores.transpose(1, 2, 0)[None]


def solution(mesh):
    sizes = mesh.shape
    return jax.shard_map(
        functools.partial(on_device, sizes["row"], sizes["col"]),
        mesh=mesh,
        in_specs=(
            P("row", "col", None, None),
            P("row", "col", None, None, None),
            P("row", "col", None, None),
            P("row", "col"),
            P("row", "col", None),
            P("row", "col", None, None),
            P(),
            P(),
            P(),
            P(),
        ),
        out_specs=(P("row", "col", None, None), P("row", "col", None, None)),
        check_vma=False,
    )
```

```python
import functools

import jax
import jax.numpy as jnp
from jax import lax
from jax.experimental import pallas as pl
from jax.experimental.pallas import tpu as pltpu
from jax.sharding import PartitionSpec as P

BF16 = jnp.bfloat16
F32 = jnp.float32
VMEM_LIMIT = 48 * 1024 * 1024


def partner(index, slot):
    return index ^ slot


def turned(slot):
    return slot ^ (((slot >> 1) ^ (slot >> 2)) & 1) * 6


def seen(slot, index):
    return slot ^ (index & 1) * (turned(slot) ^ slot)


def order(size):
    return [0, *reversed(range(3, size, 2))]


def column_order(size):
    return order(size) + [turned(slot) ^ 1 for slot in order(size)]


def permuted(block, axis, size, slot):
    return lax.ppermute(block, axis, [(i, partner(i, slot)) for i in range(size)])


def fetched(block, axis, size, slot):
    return lax.ppermute(block, axis, [(partner(i, seen(slot, i)), i) for i in range(size)])


def fetch_chips(block, axis, size):
    return [fetched(block, axis, size, slot) for slot in order(size)[1:]]


def fetch_core(blocks, axis, size):
    return permuted(blocks, axis, size, 1)


def both_cores(blocks, axis, size):
    found = jnp.concatenate([blocks, fetch_core(blocks, axis, size)])
    return found[jnp.argsort(jnp.array(column_order(size)))]


def send_across(blocks, n_row, n_col):
    arrived = []
    for slot in reversed(range(n_col)):
        pairs = [
            (row * n_col + col, partner(row, 1) * n_col + partner(col, slot))
            for row in range(n_row)
            for col in range(n_col)
        ]
        arrived.append(lax.ppermute(blocks[slot], ("row", "col"), pairs))
    return arrived


def send_each(blocks, axis, size):
    return [permuted(blocks[slot], axis, size, slot) for slot in reversed(range(1, size))]


def call(kernel, out_shape, operands, specs=None, scratch=(), cost=None, out_specs=None):
    vmem = pl.BlockSpec(memory_space=pltpu.VMEM)
    return pl.pallas_call(
        kernel,
        out_shape=out_shape,
        in_specs=specs or [vmem] * len(operands),
        out_specs=out_specs or jax.tree.map(lambda _: vmem, out_shape),
        scratch_shapes=list(scratch),
        cost_estimate=cost,
        compiler_params=pltpu.CompilerParams(vmem_limit_bytes=VMEM_LIMIT),
    )(*operands)


def dot_nt(left, right):
    return lax.dot_general(left, right, (((1,), (1,)), ((), ())), preferred_element_type=F32)


def build_kernel(
    n_row, n_col, chunks, count, coords_hbm, tiles_hbm, dense_ref, coords, tiles, first, second, sems, coords_sem
):
    slots, block = tiles.shape[0], tiles.shape[1]
    per, part = slots // chunks, block // 2
    copies = [
        pltpu.make_async_copy(
            tiles_hbm.at[pl.ds(i * per, per)], tiles.at[pl.ds(i * per, per)], sems.at[i]
        )
        for i in range(chunks)
    ]
    coords_copy = pltpu.make_async_copy(coords_hbm, coords, coords_sem)
    coords_copy.start()
    live = count[0, 0]
    for i, copy in enumerate(copies):
        pl.when(i * per < live)(copy.start)
    row, col = lax.axis_index("row"), lax.axis_index("col")
    first[...] = jnp.zeros_like(first)
    second[...] = jnp.zeros_like(second)
    coords_copy.wait()

    def place(t):
        at = partner(coords[0, t], col) * n_row + seen(partner(coords[1, t], row), row)
        return jnp.where(t < live, at, n_row * n_col)

    for i in range(chunks):

        @pl.when(i * per < live)
        def _():
            copies[i].wait()

            @pl.loop(0, per, unroll=8)
            def _(step):
                t = i * per + step
                at = place(t)
                first[at] += tiles[t, :part].astype(F32)
                second[at] += tiles[t, part:].astype(F32)

    for k in range(n_col):
        for j, slot in enumerate(column_order(n_row)):
            at = k * n_row + slot
            columns = slice(j * block, (j + 1) * block)
            dense_ref[k * block : k * block + part, columns] = first[at].astype(BF16)
            dense_ref[k * block + part : (k + 1) * block, columns] = second[at].astype(BF16)


def prepare_kernel(mask, bias, history, *refs):
    kept_out, bias_out, wide = refs[-3:]
    block, classes = history.shape[0], bias.shape[1]
    mask_cols = jnp.broadcast_to(mask[...].astype(F32), (block, block)).T
    chosen = jnp.concatenate([mask_cols] * (history.shape[1] // block), axis=1) == 1.0
    kept_out[...] = jnp.where(chosen, -1.0, history[...].astype(F32)).astype(BF16)
    wide[...] = jnp.zeros_like(wide)
    wide[:, :classes] = jnp.broadcast_to(bias[...], (block, classes))
    bias_out[...] = wide[...].T[:classes]


def join_rows_kernel(places, *refs):
    out = refs[-1]
    block = refs[0].shape[0]
    for ref, place in zip(refs, places):
        out[place * block : (place + 1) * block, :] = ref[...]


def half_one_kernel(dense_ref, mine_ref, out):
    half = mine_ref.shape[0]
    out[...] = jnp.dot(dense_ref[:, :half], mine_ref[...], preferred_element_type=F32)


def layer_one_kernel(dense_ref, first_ref, other_ref, *outputs):
    half, block = other_ref.shape[0], dense_ref.shape[0] // len(outputs)
    total = first_ref[...] + jnp.dot(
        dense_ref[:, half:], other_ref[...], preferred_element_type=F32
    )
    for k, out in enumerate(outputs):
        out[...] = total[k * block : (k + 1) * block, :].astype(BF16)


def hidden_kernel(n_col, *refs):
    parts = refs[:n_col]
    feats, w_one, b_one, w_two, kept, pushed_ref, proj_ref = refs[n_col:]
    total = feats[: kept.shape[0], :].astype(F32)
    for part in parts:
        total += part[...].astype(F32)
    pre = jnp.dot(total.astype(BF16), w_one[...], preferred_element_type=F32) + b_one[...]
    hidden = jnp.maximum(pre, 0.0)
    old = kept[...].astype(F32)
    pushed = jnp.where(old < 0.0, hidden, old).astype(BF16)
    pushed_ref[...] = pushed
    proj_ref[...] = dot_nt(w_two[...], pushed).astype(BF16)


def write_kernel(value, out):
    out[...] = value[...]


def late_kernel(value, after, out):
    del after
    out[...] = value[...]


def lanes(refs, scratch, places=None):
    block = refs[0].shape[1]
    for i, ref in zip(places or range(len(refs)), refs):
        scratch[:, i * block : (i + 1) * block] = ref[...]
    return scratch[...]


def half_two_kernel(places, dense_ref, *refs):
    blocks, (out, scratch) = refs[:-2], refs[-2:]
    half = dense_ref.shape[1] // 2
    out[...] = dot_nt(
        lanes(blocks, scratch, places), dense_ref[:, half : half + scratch.shape[1]]
    )


def layer_two_kernel(slots, dense_ref, first_ref, near_ref, rest_ref, *refs):
    outputs = refs[-len(slots) :]
    block, half = near_ref.shape[1], rest_ref.shape[1]
    at = slice(slots[0] * block, (slots[-1] + 1) * block)
    total = first_ref[:, at] + dot_nt(rest_ref[...], dense_ref[at, :half])
    total += dot_nt(near_ref[...], dense_ref[at, dense_ref.shape[1] - block :])
    for i, out in enumerate(outputs):
        out[...] = total[:, i * block : (i + 1) * block].astype(BF16)


def sent_two_kernel(slots, dense_ref, first_ref, own_ref, near_ref, *refs):
    rest = refs[-1]
    blocks, outputs = refs[: -len(slots) - 1], refs[-len(slots) - 1 : -1]
    lanes([own_ref, *blocks], rest)
    layer_two_kernel(slots, dense_ref, first_ref, near_ref, rest, *outputs)


def begin_kernel(*refs):
    total = refs[0][...].astype(F32)
    for ref in refs[1:-1]:
        total += ref[...].astype(F32)
    refs[-1][...] = total


def logits_kernel(pieces, begun, *refs):
    parts, (out_hbm, staged, sems) = refs[:-3], refs[-3:]
    step = -(-staged.shape[0] // pieces // 16) * 16
    copies = []
    for i in range(pieces):
        rows = slice(i * step, (i + 1) * step if i < pieces - 1 else staged.shape[0])
        total = begun[rows, :]
        for part in parts:
            total += part[rows, :].astype(F32)
        staged[rows, 0, :] = total
        copies.append(pltpu.make_async_copy(staged.at[rows], out_hbm.at[rows], sems.at[i]))
        copies[-1].start()
    for copy in copies:
        copy.wait()


def tiles_kernel(
    n_row, n_col, transposed, coords_ref, count_ref, tiles_ref, stacked_ref, out_ref, total
):
    row, col = lax.axis_index("row"), lax.axis_index("col")
    total[...] = jnp.zeros_like(total)

    @pl.loop(0, count_ref[0, 0])
    def _(t):
        k = partner(coords_ref[0, t], col)
        j = seen(partner(coords_ref[1, t], row), row)
        if transposed:
            total[k] += dot_nt(stacked_ref[j], tiles_ref[t])
        else:
            total[k] += jnp.dot(tiles_ref[t], stacked_ref[j], preferred_element_type=F32)

    out_ref[...] = total[...].astype(BF16)


def on_device(
    n_row, n_col,
    features, tiles, tile_coords, tile_count, batch_mask, history,
    weight_one, bias_one, weight_two, bias_two,
):
    feat, tile_set, hist = features[0, 0], tiles[0, 0], history[0, 0]
    coords = tile_coords[0, 0].T
    slots, block = tile_set.shape[0], tile_set.shape[1]
    f_in, hid, classes = feat.shape[1], weight_one.shape[1], weight_two.shape[1]
    w_two_t = weight_two.T
    dense_form = n_row * n_col <= slots
    smem = pl.BlockSpec(memory_space=pltpu.SMEM)
    vmem = pl.BlockSpec(memory_space=pltpu.VMEM)
    hbm = pl.BlockSpec(memory_space=pltpu.HBM)
    shape = jax.ShapeDtypeStruct

    def prepare(*after):
        return call(
            prepare_kernel,
            (shape((block, hid), BF16), shape((classes, block), F32)),
            (batch_mask[0], bias_two[None], hist, *after),
            specs=[vmem] * 3 + [pl.BlockSpec(memory_space=pl.ANY)] * len(after),
            scratch=[pltpu.VMEM((block, -(-classes // 128) * 128), F32)],
        )

    chips_one = [feat, *fetch_chips(feat, "row", n_row)]

    if dense_form:
        anywhere = pl.BlockSpec(memory_space=pl.ANY)
        chunks = 8
        dense = call(
            functools.partial(build_kernel, n_row, n_col, chunks),
            shape((n_col * block, n_row * block), BF16),
            (
                tile_count,
                pltpu.with_memory_space_constraint(coords, pltpu.HBM),
                pltpu.with_memory_space_constraint(tile_set, pltpu.HBM),
            ),
            specs=[smem, hbm, hbm],
            scratch=[
                pltpu.SMEM((2, slots), jnp.int32),
                pltpu.VMEM((slots, block, block), BF16),
                pltpu.VMEM((n_row * n_col + 1, block // 2, block), F32),
                pltpu.VMEM((n_row * n_col + 1, block // 2, block), F32),
                pltpu.SemaphoreType.DMA((chunks,)),
                pltpu.SemaphoreType.DMA(()),
            ],
            cost=pl.CostEstimate(
                flops=slots * block * block,
                bytes_accessed=2 * slots * block * block,
                transcendentals=0,
            ),
        )
        names = order(n_row)
        places_one = [0, *sorted(range(1, n_row // 2), key=lambda i: (names[i] != 5, names[i]))]
        mine_one = call(
            functools.partial(join_rows_kernel, places_one),
            shape((n_row // 2 * block, f_in), BF16),
            (*[chips_one[i] for i in places_one], dense),
            specs=[vmem] * len(chips_one) + [anywhere],
        )
        other_one = fetch_core(mine_one, "row", n_row)
        kept, bias_cols = prepare(mine_one)
        half_one = call(half_one_kernel, shape((n_col * block, f_in), F32), (dense, mine_one))
        parts_one = call(
            layer_one_kernel,
            [shape((block, f_in), BF16)] * n_col,
            (dense, half_one, other_one),
        )
    else:
        kept, bias_cols = prepare()
        summed = call(
            functools.partial(tiles_kernel, n_row, n_col, False),
            shape((n_col, block, f_in), BF16),
            (coords, tile_count, tile_set, both_cores(jnp.stack(chips_one), "row", n_row)),
            specs=[smem, smem, vmem, vmem],
            scratch=[pltpu.VMEM((n_col, block, f_in), F32)],
        )
        parts_one = [summed[k] for k in range(n_col)]
        other_one = fetch_core(feat, "row", n_row)

    arrived_one = send_across(parts_one, n_row, n_col)
    kept = fetch_core(kept, "row", n_row)
    pushed, proj = call(
        functools.partial(hidden_kernel, n_col),
        (shape((block, hid), BF16), shape((classes, block), BF16)),
        (*arrived_one, other_one, weight_one, bias_one[None], w_two_t, kept),
    )
    chips_two = [proj, *fetch_chips(proj, "row", n_row)]
    if dense_form:
        near = chips_two[order(n_row).index(5)]
        early = [x for x in chips_two if x is not near]
        near_other = fetched(proj, "row", n_row, 2)
        others_two = [fetch_core(x, "row", n_row) for x in early] + [near_other]
        own_proj = others_two[0]
    else:
        own_proj = fetch_core(proj, "row", n_row)

    if dense_form:
        late = others_two
        places_two = [0, *reversed(range(1, len(early)))]
        half_two = call(
            functools.partial(half_two_kernel, places_two),
            shape((classes, n_col * block), F32),
            (dense, *[early[i] for i in places_two]),
            scratch=[pltpu.VMEM((classes, len(early) * block), BF16)],
        )
        pushed = call(
            late_kernel, shape((block, hid), BF16), (pushed, half_two), specs=[vmem, anywhere]
        )
        sent = range(1, n_col)
        *sent_two, rest = call(
            functools.partial(sent_two_kernel, sent),
            [shape((classes, block), BF16)] * len(sent)
            + [shape((classes, len(late) * block), BF16)],
            (dense, half_two, late[0], near, *late[1:]),
        )
        own_two = call(
            functools.partial(layer_two_kernel, [0]),
            [shape((classes, block), BF16)],
            (dense, half_two, near, rest, sent_two[0]),
            specs=[vmem] * 4 + [anywhere],
        )
        parts_two = [*own_two, *sent_two]
    else:
        other_slots = jnp.arange(n_row) ^ 1
        summed = call(
            functools.partial(tiles_kernel, n_row, n_col, True),
            shape((n_col, classes, block), BF16),
            (coords, tile_count, tile_set, both_cores(jnp.stack(chips_two), "row", n_row)[other_slots]),
            specs=[smem, smem, vmem, vmem],
            scratch=[pltpu.VMEM((n_col, classes, block), F32)],
        )
        parts_two = [summed[k] for k in range(n_col)]

    arrived_two = send_each(parts_two, "col", n_col)
    pushed = call(write_kernel, shape((block, hid), BF16), (fetch_core(pushed, "row", n_row),))
    pieces = 4
    begun_two = call(
        begin_kernel,
        shape((classes, block), F32),
        (bias_cols, own_proj, parts_two[0], arrived_two[0]),
    )
    scores = call(
        functools.partial(logits_kernel, pieces),
        shape((classes, 1, block), F32),
        (begun_two, *arrived_two[1:]),
        scratch=[pltpu.VMEM((classes, 1, block), F32), pltpu.SemaphoreType.DMA((pieces,))],
        out_specs=pl.BlockSpec(memory_space=pl.ANY),
    )
    return pushed[None, None], scores.transpose(1, 2, 0)[None]


def solution(mesh):
    sizes = mesh.shape
    return jax.shard_map(
        functools.partial(on_device, sizes["row"], sizes["col"]),
        mesh=mesh,
        in_specs=(
            P("row", "col", None, None),
            P("row", "col", None, None, None),
            P("row", "col", None, None),
            P("row", "col"),
            P("row", "col", None),
            P("row", "col", None, None),
            P(),
            P(),
            P(),
            P(),
        ),
        out_specs=(P("row", "col", None, None), P("row", "col", None, None)),
        check_vma=False,
    )
```

```python
import functools

import jax
import jax.numpy as jnp
from jax import lax
from jax.experimental import pallas as pl
from jax.experimental.pallas import tpu as pltpu
from jax.sharding import PartitionSpec as P

BF16 = jnp.bfloat16
F32 = jnp.float32
VMEM_LIMIT = 48 * 1024 * 1024


def partner(index, slot):
    return index ^ slot


def turned(slot):
    return slot ^ (((slot >> 1) ^ (slot >> 2)) & 1) * 6


def seen(slot, index):
    return slot ^ (index & 1) * (turned(slot) ^ slot)


def order(size):
    return [0, *reversed(range(3, size, 2))]


def column_order(size):
    return order(size) + [turned(slot) ^ 1 for slot in order(size)]


def permuted(block, axis, size, slot):
    return lax.ppermute(block, axis, [(i, partner(i, slot)) for i in range(size)])


def fetched(block, axis, size, slot):
    return lax.ppermute(block, axis, [(partner(i, seen(slot, i)), i) for i in range(size)])


def fetch_chips(block, axis, size):
    return [fetched(block, axis, size, slot) for slot in order(size)[1:]]


def fetch_core(blocks, axis, size):
    return permuted(blocks, axis, size, 1)


def both_cores(blocks, axis, size):
    found = jnp.concatenate([blocks, fetch_core(blocks, axis, size)])
    return found[jnp.argsort(jnp.array(column_order(size)))]


def send_across(blocks, n_row, n_col):
    arrived = []
    for slot in reversed(range(n_col)):
        pairs = [
            (row * n_col + col, partner(row, 1) * n_col + partner(col, slot))
            for row in range(n_row)
            for col in range(n_col)
        ]
        arrived.append(lax.ppermute(blocks[slot], ("row", "col"), pairs))
    return arrived


def send_each(blocks, axis, size):
    slots = [size - 1, *range(1, size - 1)]
    return [permuted(blocks[slot], axis, size, slot) for slot in slots]


def call(kernel, out_shape, operands, specs=None, scratch=(), cost=None, out_specs=None):
    vmem = pl.BlockSpec(memory_space=pltpu.VMEM)
    return pl.pallas_call(
        kernel,
        out_shape=out_shape,
        in_specs=specs or [vmem] * len(operands),
        out_specs=out_specs or jax.tree.map(lambda _: vmem, out_shape),
        scratch_shapes=list(scratch),
        cost_estimate=cost,
        compiler_params=pltpu.CompilerParams(vmem_limit_bytes=VMEM_LIMIT),
    )(*operands)


def dot_nt(left, right):
    return lax.dot_general(left, right, (((1,), (1,)), ((), ())), preferred_element_type=F32)


def build_kernel(
    n_row, n_col, chunks, count, coords_hbm, tiles_hbm, dense_ref, coords, tiles, first, second, sems, coords_sem
):
    slots, block = tiles.shape[0], tiles.shape[1]
    per, part = slots // chunks, block // 2
    copies = [
        pltpu.make_async_copy(
            tiles_hbm.at[pl.ds(i * per, per)], tiles.at[pl.ds(i * per, per)], sems.at[i]
        )
        for i in range(chunks)
    ]
    coords_copy = pltpu.make_async_copy(coords_hbm, coords, coords_sem)
    coords_copy.start()
    live = count[0, 0]
    for i, copy in enumerate(copies):
        pl.when(i * per < live)(copy.start)
    row, col = lax.axis_index("row"), lax.axis_index("col")
    first[...] = jnp.zeros_like(first)
    second[...] = jnp.zeros_like(second)
    coords_copy.wait()

    def place(t):
        at = partner(coords[0, t], col) * n_row + seen(partner(coords[1, t], row), row)
        return jnp.where(t < live, at, n_row * n_col)

    for i in range(chunks):

        @pl.when(i * per < live)
        def _():
            copies[i].wait()

            @pl.loop(0, per, unroll=8)
            def _(step):
                t = i * per + step
                at = place(t)
                first[at] += tiles[t, :part].astype(F32)
                second[at] += tiles[t, part:].astype(F32)

    for k in range(n_col):
        for j, slot in enumerate(column_order(n_row)):
            at = k * n_row + slot
            columns = slice(j * block, (j + 1) * block)
            dense_ref[k * block : k * block + part, columns] = first[at].astype(BF16)
            dense_ref[k * block + part : (k + 1) * block, columns] = second[at].astype(BF16)


def prepare_kernel(mask, bias, history, *refs):
    kept_out, bias_out, wide = refs[-3:]
    block, classes = history.shape[0], bias.shape[1]
    mask_cols = jnp.broadcast_to(mask[...].astype(F32), (block, block)).T
    chosen = jnp.concatenate([mask_cols] * (history.shape[1] // block), axis=1) == 1.0
    kept_out[...] = jnp.where(chosen, -1.0, history[...].astype(F32)).astype(BF16)
    wide[...] = jnp.zeros_like(wide)
    wide[:, :classes] = jnp.broadcast_to(bias[...], (block, classes))
    bias_out[...] = wide[...].T[:classes]


def join_rows_kernel(places, *refs):
    out = refs[-1]
    block = refs[0].shape[0]
    for ref, place in zip(refs, places):
        out[place * block : (place + 1) * block, :] = ref[...]


def half_one_kernel(dense_ref, mine_ref, out):
    half = mine_ref.shape[0]
    out[...] = jnp.dot(dense_ref[:, :half], mine_ref[...], preferred_element_type=F32)


def layer_one_kernel(dense_ref, first_ref, other_ref, *outputs):
    half, block = other_ref.shape[0], dense_ref.shape[0] // len(outputs)
    total = first_ref[...] + jnp.dot(
        dense_ref[:, half:], other_ref[...], preferred_element_type=F32
    )
    for k, out in enumerate(outputs):
        out[...] = total[k * block : (k + 1) * block, :].astype(BF16)


def hidden_kernel(n_col, *refs):
    parts = refs[:n_col]
    feats, w_one, b_one, w_two, kept, pushed_ref, proj_ref = refs[n_col:]
    total = feats[: kept.shape[0], :].astype(F32)
    for part in parts:
        total += part[...].astype(F32)
    pre = jnp.dot(total.astype(BF16), w_one[...], preferred_element_type=F32) + b_one[...]
    hidden = jnp.maximum(pre, 0.0)
    old = kept[...].astype(F32)
    pushed = jnp.where(old < 0.0, hidden, old).astype(BF16)
    pushed_ref[...] = pushed
    proj_ref[...] = dot_nt(w_two[...], pushed).astype(BF16)


def write_kernel(value, out):
    out[...] = value[...]


def late_kernel(value, after, out):
    del after
    out[...] = value[...]


def lanes(refs, scratch, places=None):
    block = refs[0].shape[1]
    for i, ref in zip(places or range(len(refs)), refs):
        scratch[:, i * block : (i + 1) * block] = ref[...]
    return scratch[...]


def half_two_kernel(places, dense_ref, *refs):
    blocks, (out, scratch) = refs[:-2], refs[-2:]
    half = dense_ref.shape[1] // 2
    out[...] = dot_nt(
        lanes(blocks, scratch, places), dense_ref[:, half : half + scratch.shape[1]]
    )


def layer_two_kernel(slots, dense_ref, first_ref, near_ref, rest_ref, *refs):
    outputs = refs[-len(slots) :]
    block, half = near_ref.shape[1], rest_ref.shape[1]
    at = slice(slots[0] * block, (slots[-1] + 1) * block)
    total = first_ref[:, at] + dot_nt(rest_ref[...], dense_ref[at, :half])
    total += dot_nt(near_ref[...], dense_ref[at, dense_ref.shape[1] - block :])
    for i, out in enumerate(outputs):
        out[...] = total[:, i * block : (i + 1) * block].astype(BF16)


def sent_two_kernel(slots, dense_ref, first_ref, own_ref, near_ref, *refs):
    rest = refs[-1]
    blocks, outputs = refs[: -len(slots) - 1], refs[-len(slots) - 1 : -1]
    lanes([own_ref, *blocks], rest)
    layer_two_kernel(slots, dense_ref, first_ref, near_ref, rest, *outputs)


def begin_kernel(*refs):
    total = refs[0][...].astype(F32)
    for ref in refs[1:-1]:
        total += ref[...].astype(F32)
    refs[-1][...] = total


def logits_kernel(pieces, begun, *refs):
    parts, (out_hbm, staged, sems) = refs[:-3], refs[-3:]
    step = -(-staged.shape[0] // pieces // 16) * 16
    copies = []
    for i in range(pieces):
        rows = slice(i * step, (i + 1) * step if i < pieces - 1 else staged.shape[0])
        total = begun[rows, :]
        for part in parts:
            total += part[rows, :].astype(F32)
        staged[rows, 0, :] = total
        copies.append(pltpu.make_async_copy(staged.at[rows], out_hbm.at[rows], sems.at[i]))
        copies[-1].start()
    for copy in copies:
        copy.wait()


def tiles_kernel(
    n_row, n_col, transposed, coords_ref, count_ref, tiles_ref, stacked_ref, out_ref, total
):
    row, col = lax.axis_index("row"), lax.axis_index("col")
    total[...] = jnp.zeros_like(total)

    @pl.loop(0, count_ref[0, 0])
    def _(t):
        k = partner(coords_ref[0, t], col)
        j = seen(partner(coords_ref[1, t], row), row)
        if transposed:
            total[k] += dot_nt(stacked_ref[j], tiles_ref[t])
        else:
            total[k] += jnp.dot(tiles_ref[t], stacked_ref[j], preferred_element_type=F32)

    out_ref[...] = total[...].astype(BF16)


def on_device(
    n_row, n_col,
    features, tiles, tile_coords, tile_count, batch_mask, history,
    weight_one, bias_one, weight_two, bias_two,
):
    feat, tile_set, hist = features[0, 0], tiles[0, 0], history[0, 0]
    coords = tile_coords[0, 0].T
    slots, block = tile_set.shape[0], tile_set.shape[1]
    f_in, hid, classes = feat.shape[1], weight_one.shape[1], weight_two.shape[1]
    w_two_t = weight_two.T
    dense_form = n_row * n_col <= slots
    smem = pl.BlockSpec(memory_space=pltpu.SMEM)
    vmem = pl.BlockSpec(memory_space=pltpu.VMEM)
    hbm = pl.BlockSpec(memory_space=pltpu.HBM)
    shape = jax.ShapeDtypeStruct

    def prepare(*after):
        return call(
            prepare_kernel,
            (shape((block, hid), BF16), shape((classes, block), F32)),
            (batch_mask[0], bias_two[None], hist, *after),
            specs=[vmem] * 3 + [pl.BlockSpec(memory_space=pl.ANY)] * len(after),
            scratch=[pltpu.VMEM((block, -(-classes // 128) * 128), F32)],
        )

    chips_one = [feat, *fetch_chips(feat, "row", n_row)]

    if dense_form:
        anywhere = pl.BlockSpec(memory_space=pl.ANY)
        chunks = 8
        dense = call(
            functools.partial(build_kernel, n_row, n_col, chunks),
            shape((n_col * block, n_row * block), BF16),
            (
                tile_count,
                pltpu.with_memory_space_constraint(coords, pltpu.HBM),
                pltpu.with_memory_space_constraint(tile_set, pltpu.HBM),
            ),
            specs=[smem, hbm, hbm],
            scratch=[
                pltpu.SMEM((2, slots), jnp.int32),
                pltpu.VMEM((slots, block, block), BF16),
                pltpu.VMEM((n_row * n_col + 1, block // 2, block), F32),
                pltpu.VMEM((n_row * n_col + 1, block // 2, block), F32),
                pltpu.SemaphoreType.DMA((chunks,)),
                pltpu.SemaphoreType.DMA(()),
            ],
            cost=pl.CostEstimate(
                flops=slots * block * block,
                bytes_accessed=2 * slots * block * block,
                transcendentals=0,
            ),
        )
        names = order(n_row)
        places_one = [0, *sorted(range(1, n_row // 2), key=lambda i: (names[i] != 5, names[i]))]
        mine_one = call(
            functools.partial(join_rows_kernel, places_one),
            shape((n_row // 2 * block, f_in), BF16),
            (*[chips_one[i] for i in places_one], dense),
            specs=[vmem] * len(chips_one) + [anywhere],
        )
        other_one = fetch_core(mine_one, "row", n_row)
        kept, bias_cols = prepare(mine_one)
        half_one = call(half_one_kernel, shape((n_col * block, f_in), F32), (dense, mine_one))
        parts_one = call(
            layer_one_kernel,
            [shape((block, f_in), BF16)] * n_col,
            (dense, half_one, other_one),
        )
    else:
        kept, bias_cols = prepare()
        summed = call(
            functools.partial(tiles_kernel, n_row, n_col, False),
            shape((n_col, block, f_in), BF16),
            (coords, tile_count, tile_set, both_cores(jnp.stack(chips_one), "row", n_row)),
            specs=[smem, smem, vmem, vmem],
            scratch=[pltpu.VMEM((n_col, block, f_in), F32)],
        )
        parts_one = [summed[k] for k in range(n_col)]
        other_one = fetch_core(feat, "row", n_row)

    arrived_one = send_across(parts_one, n_row, n_col)
    kept = fetch_core(kept, "row", n_row)
    pushed, proj = call(
        functools.partial(hidden_kernel, n_col),
        (shape((block, hid), BF16), shape((classes, block), BF16)),
        (*arrived_one, other_one, weight_one, bias_one[None], w_two_t, kept),
    )
    chips_two = [proj, *fetch_chips(proj, "row", n_row)]
    if dense_form:
        near = chips_two[order(n_row).index(5)]
        early = [x for x in chips_two if x is not near]
        near_other = fetched(proj, "row", n_row, 2)
        others_two = [fetch_core(x, "row", n_row) for x in early] + [near_other]
        own_proj = others_two[0]
    else:
        own_proj = fetch_core(proj, "row", n_row)

    if dense_form:
        late = others_two
        places_two = [0, *reversed(range(1, len(early)))]
        half_two = call(
            functools.partial(half_two_kernel, places_two),
            shape((classes, n_col * block), F32),
            (dense, *[early[i] for i in places_two]),
            scratch=[pltpu.VMEM((classes, len(early) * block), BF16)],
        )
        pushed = call(
            late_kernel, shape((block, hid), BF16), (pushed, half_two), specs=[vmem, anywhere]
        )
        sent = range(1, n_col)
        *sent_two, rest = call(
            functools.partial(sent_two_kernel, sent),
            [shape((classes, block), BF16)] * len(sent)
            + [shape((classes, len(late) * block), BF16)],
            (dense, half_two, late[0], near, *late[1:]),
        )
        own_two = call(
            functools.partial(layer_two_kernel, [0]),
            [shape((classes, block), BF16)],
            (dense, half_two, near, rest, sent_two[0]),
            specs=[vmem] * 4 + [anywhere],
        )
        parts_two = [*own_two, *sent_two]
    else:
        other_slots = jnp.arange(n_row) ^ 1
        summed = call(
            functools.partial(tiles_kernel, n_row, n_col, True),
            shape((n_col, classes, block), BF16),
            (coords, tile_count, tile_set, both_cores(jnp.stack(chips_two), "row", n_row)[other_slots]),
            specs=[smem, smem, vmem, vmem],
            scratch=[pltpu.VMEM((n_col, classes, block), F32)],
        )
        parts_two = [summed[k] for k in range(n_col)]

    arrived_two = send_each(parts_two, "col", n_col)
    pushed = call(write_kernel, shape((block, hid), BF16), (fetch_core(pushed, "row", n_row),))
    pieces = 4
    begun_two = call(
        begin_kernel,
        shape((classes, block), F32),
        (bias_cols, own_proj, parts_two[0], arrived_two[0]),
    )
    scores = call(
        functools.partial(logits_kernel, pieces),
        shape((classes, 1, block), F32),
        (begun_two, *arrived_two[1:]),
        scratch=[pltpu.VMEM((classes, 1, block), F32), pltpu.SemaphoreType.DMA((pieces,))],
        out_specs=pl.BlockSpec(memory_space=pl.ANY),
    )
    return pushed[None, None], scores.transpose(1, 2, 0)[None]


def solution(mesh):
    sizes = mesh.shape
    return jax.shard_map(
        functools.partial(on_device, sizes["row"], sizes["col"]),
        mesh=mesh,
        in_specs=(
            P("row", "col", None, None),
            P("row", "col", None, None, None),
            P("row", "col", None, None),
            P("row", "col"),
            P("row", "col", None),
            P("row", "col", None, None),
            P(),
            P(),
            P(),
            P(),
        ),
        out_specs=(P("row", "col", None, None), P("row", "col", None, None)),
        check_vma=False,
    )
```

```python
import functools

import jax
import jax.numpy as jnp
from jax import lax
from jax.experimental import pallas as pl
from jax.experimental.pallas import tpu as pltpu
from jax.sharding import PartitionSpec as P

BF16 = jnp.bfloat16
F32 = jnp.float32
VMEM_LIMIT = 48 * 1024 * 1024


def partner(index, slot):
    return index ^ slot


def turned(slot):
    return slot ^ (((slot >> 1) ^ (slot >> 2)) & 1) * 6


def seen(slot, index):
    return slot ^ (index & 1) * (turned(slot) ^ slot)


def order(size):
    return [0, *reversed(range(3, size, 2))]


def column_order(size):
    return order(size) + [turned(slot) ^ 1 for slot in order(size)]


def permuted(block, axis, size, slot):
    return lax.ppermute(block, axis, [(i, partner(i, slot)) for i in range(size)])


def fetched(block, axis, size, slot):
    return lax.ppermute(block, axis, [(partner(i, seen(slot, i)), i) for i in range(size)])


def fetch_chips(block, axis, size):
    return [fetched(block, axis, size, slot) for slot in order(size)[1:]]


def fetch_core(blocks, axis, size):
    return permuted(blocks, axis, size, 1)


def both_cores(blocks, axis, size):
    found = jnp.concatenate([blocks, fetch_core(blocks, axis, size)])
    return found[jnp.argsort(jnp.array(column_order(size)))]


def send_across(blocks, n_row, n_col):
    arrived = []
    for slot in reversed(range(n_col)):
        pairs = [
            (row * n_col + col, partner(row, 1) * n_col + partner(col, slot))
            for row in range(n_row)
            for col in range(n_col)
        ]
        arrived.append(lax.ppermute(blocks[slot], ("row", "col"), pairs))
    return arrived


def send_each(blocks, axis, size):
    return [permuted(blocks[slot], axis, size, slot) for slot in reversed(range(1, size))]


def call(kernel, out_shape, operands, specs=None, scratch=(), cost=None, out_specs=None):
    vmem = pl.BlockSpec(memory_space=pltpu.VMEM)
    return pl.pallas_call(
        kernel,
        out_shape=out_shape,
        in_specs=specs or [vmem] * len(operands),
        out_specs=out_specs or jax.tree.map(lambda _: vmem, out_shape),
        scratch_shapes=list(scratch),
        cost_estimate=cost,
        compiler_params=pltpu.CompilerParams(vmem_limit_bytes=VMEM_LIMIT),
    )(*operands)


def dot_nt(left, right):
    return lax.dot_general(left, right, (((1,), (1,)), ((), ())), preferred_element_type=F32)


def build_kernel(
    n_row, n_col, chunks, count, coords_hbm, tiles_hbm, dense_ref, coords, tiles, first, second, sems, coords_sem
):
    slots, block = tiles.shape[0], tiles.shape[1]
    per, part = slots // chunks, block // 2
    copies = [
        pltpu.make_async_copy(
            tiles_hbm.at[pl.ds(i * per, per)], tiles.at[pl.ds(i * per, per)], sems.at[i]
        )
        for i in range(chunks)
    ]
    coords_copy = pltpu.make_async_copy(coords_hbm, coords, coords_sem)
    coords_copy.start()
    live = count[0, 0]
    for i, copy in enumerate(copies):
        pl.when(i * per < live)(copy.start)
    row, col = lax.axis_index("row"), lax.axis_index("col")
    first[...] = jnp.zeros_like(first)
    second[...] = jnp.zeros_like(second)
    coords_copy.wait()

    def place(t):
        at = partner(coords[0, t], col) * n_row + seen(partner(coords[1, t], row), row)
        return jnp.where(t < live, at, n_row * n_col)

    for i in range(chunks):

        @pl.when(i * per < live)
        def _():
            copies[i].wait()

            @pl.loop(0, per, unroll=8)
            def _(step):
                t = i * per + step
                at = place(t)
                first[at] += tiles[t, :part].astype(F32)
                second[at] += tiles[t, part:].astype(F32)

    for k in range(n_col):
        for j, slot in enumerate(column_order(n_row)):
            at = k * n_row + slot
            columns = slice(j * block, (j + 1) * block)
            dense_ref[k * block : k * block + part, columns] = first[at].astype(BF16)
            dense_ref[k * block + part : (k + 1) * block, columns] = second[at].astype(BF16)


def prepare_kernel(mask, bias, history, *refs):
    kept_out, bias_out, wide = refs[-3:]
    block, classes = history.shape[0], bias.shape[1]
    mask_cols = jnp.broadcast_to(mask[...].astype(F32), (block, block)).T
    chosen = jnp.concatenate([mask_cols] * (history.shape[1] // block), axis=1) == 1.0
    kept_out[...] = jnp.where(chosen, -1.0, history[...].astype(F32)).astype(BF16)
    wide[...] = jnp.zeros_like(wide)
    wide[:, :classes] = jnp.broadcast_to(bias[...], (block, classes))
    bias_out[...] = wide[...].T[:classes]


def join_rows_kernel(places, *refs):
    out = refs[-1]
    block = refs[0].shape[0]
    for ref, place in zip(refs, places):
        out[place * block : (place + 1) * block, :] = ref[...]


def half_one_kernel(dense_ref, mine_ref, out):
    half = mine_ref.shape[0]
    out[...] = jnp.dot(dense_ref[:, :half], mine_ref[...], preferred_element_type=F32)


def layer_one_kernel(dense_ref, first_ref, other_ref, *outputs):
    half, block = other_ref.shape[0], dense_ref.shape[0] // len(outputs)
    total = first_ref[...] + jnp.dot(
        dense_ref[:, half:], other_ref[...], preferred_element_type=F32
    )
    for k, out in enumerate(outputs):
        out[...] = total[k * block : (k + 1) * block, :].astype(BF16)


def hidden_kernel(n_col, *refs):
    parts = refs[:n_col]
    feats, w_one, b_one, w_two, kept, pushed_ref, proj_ref = refs[n_col:]
    total = feats[: kept.shape[0], :].astype(F32)
    for part in parts:
        total += part[...].astype(F32)
    pre = jnp.dot(total.astype(BF16), w_one[...], preferred_element_type=F32) + b_one[...]
    hidden = jnp.maximum(pre, 0.0)
    old = kept[...].astype(F32)
    pushed = jnp.where(old < 0.0, hidden, old).astype(BF16)
    pushed_ref[...] = pushed
    proj_ref[...] = dot_nt(w_two[...], pushed).astype(BF16)


def write_kernel(value, out):
    out[...] = value[...]


def late_kernel(value, after, out):
    del after
    out[...] = value[...]


def lanes(refs, scratch, places=None):
    block = refs[0].shape[1]
    for i, ref in zip(places or range(len(refs)), refs):
        scratch[:, i * block : (i + 1) * block] = ref[...]
    return scratch[...]


def half_two_kernel(places, dense_ref, *refs):
    blocks, (out, scratch) = refs[:-2], refs[-2:]
    half = dense_ref.shape[1] // 2
    out[...] = dot_nt(
        lanes(blocks, scratch, places), dense_ref[:, half : half + scratch.shape[1]]
    )


def layer_two_kernel(n_col, dense_ref, first_ref, own_ref, near_ref, *refs):
    blocks, outputs, scratch = refs[: -n_col - 1], refs[-n_col - 1 : -1], refs[-1]
    block, half = near_ref.shape[1], scratch.shape[1]
    rest = lanes([own_ref, *blocks], scratch)
    total = first_ref[...] + dot_nt(rest, dense_ref[:, :half])
    total += dot_nt(near_ref[...], dense_ref[:, dense_ref.shape[1] - block :])
    for k, out in enumerate(outputs):
        out[...] = total[:, k * block : (k + 1) * block].astype(BF16)


def logits_kernel(n_col, pieces, *refs):
    parts = refs[:n_col]
    proj, bias, out_hbm, staged, sems = refs[n_col:]
    step = -(-staged.shape[0] // pieces // 16) * 16
    copies = []
    for i in range(pieces):
        rows = slice(i * step, (i + 1) * step if i < pieces - 1 else staged.shape[0])
        total = proj[rows, :].astype(F32) + bias[rows, :]
        for part in parts:
            total += part[rows, :].astype(F32)
        staged[rows, 0, :] = total
        copies.append(pltpu.make_async_copy(staged.at[rows], out_hbm.at[rows], sems.at[i]))
        copies[-1].start()
    for copy in copies:
        copy.wait()


def tiles_kernel(
    n_row, n_col, transposed, coords_ref, count_ref, tiles_ref, stacked_ref, out_ref, total
):
    row, col = lax.axis_index("row"), lax.axis_index("col")
    total[...] = jnp.zeros_like(total)

    @pl.loop(0, count_ref[0, 0])
    def _(t):
        k = partner(coords_ref[0, t], col)
        j = seen(partner(coords_ref[1, t], row), row)
        if transposed:
            total[k] += dot_nt(stacked_ref[j], tiles_ref[t])
        else:
            total[k] += jnp.dot(tiles_ref[t], stacked_ref[j], preferred_element_type=F32)

    out_ref[...] = total[...].astype(BF16)


def on_device(
    n_row, n_col,
    features, tiles, tile_coords, tile_count, batch_mask, history,
    weight_one, bias_one, weight_two, bias_two,
):
    feat, tile_set, hist = features[0, 0], tiles[0, 0], history[0, 0]
    coords = tile_coords[0, 0].T
    slots, block = tile_set.shape[0], tile_set.shape[1]
    f_in, hid, classes = feat.shape[1], weight_one.shape[1], weight_two.shape[1]
    w_two_t = weight_two.T
    dense_form = n_row * n_col <= slots
    smem = pl.BlockSpec(memory_space=pltpu.SMEM)
    vmem = pl.BlockSpec(memory_space=pltpu.VMEM)
    hbm = pl.BlockSpec(memory_space=pltpu.HBM)
    shape = jax.ShapeDtypeStruct

    def prepare(*after):
        return call(
            prepare_kernel,
            (shape((block, hid), BF16), shape((classes, block), F32)),
            (batch_mask[0], bias_two[None], hist, *after),
            specs=[vmem] * 3 + [pl.BlockSpec(memory_space=pl.ANY)] * len(after),
            scratch=[pltpu.VMEM((block, -(-classes // 128) * 128), F32)],
        )

    chips_one = [feat, *fetch_chips(feat, "row", n_row)]

    if dense_form:
        anywhere = pl.BlockSpec(memory_space=pl.ANY)
        chunks = 16
        dense = call(
            functools.partial(build_kernel, n_row, n_col, chunks),
            shape((n_col * block, n_row * block), BF16),
            (
                tile_count,
                pltpu.with_memory_space_constraint(coords, pltpu.HBM),
                pltpu.with_memory_space_constraint(tile_set, pltpu.HBM),
            ),
            specs=[smem, hbm, hbm],
            scratch=[
                pltpu.SMEM((2, slots), jnp.int32),
                pltpu.VMEM((slots, block, block), BF16),
                pltpu.VMEM((n_row * n_col + 1, block // 2, block), F32),
                pltpu.VMEM((n_row * n_col + 1, block // 2, block), F32),
                pltpu.SemaphoreType.DMA((chunks,)),
                pltpu.SemaphoreType.DMA(()),
            ],
            cost=pl.CostEstimate(
                flops=slots * block * block,
                bytes_accessed=2 * slots * block * block,
                transcendentals=0,
            ),
        )
        names = order(n_row)
        places_one = [0, *sorted(range(1, n_row // 2), key=lambda i: (names[i] != 5, names[i]))]
        mine_one = call(
            functools.partial(join_rows_kernel, places_one),
            shape((n_row // 2 * block, f_in), BF16),
            (*[chips_one[i] for i in places_one], dense),
            specs=[vmem] * len(chips_one) + [anywhere],
        )
        other_one = fetch_core(mine_one, "row", n_row)
        kept, bias_cols = prepare(mine_one)
        half_one = call(half_one_kernel, shape((n_col * block, f_in), F32), (dense, mine_one))
        parts_one = call(
            layer_one_kernel,
            [shape((block, f_in), BF16)] * n_col,
            (dense, half_one, other_one),
        )
    else:
        kept, bias_cols = prepare()
        summed = call(
            functools.partial(tiles_kernel, n_row, n_col, False),
            shape((n_col, block, f_in), BF16),
            (coords, tile_count, tile_set, both_cores(jnp.stack(chips_one), "row", n_row)),
            specs=[smem, smem, vmem, vmem],
            scratch=[pltpu.VMEM((n_col, block, f_in), F32)],
        )
        parts_one = [summed[k] for k in range(n_col)]
        other_one = fetch_core(feat, "row", n_row)

    arrived_one = send_across(parts_one, n_row, n_col)
    kept = fetch_core(kept, "row", n_row)
    pushed, proj = call(
        functools.partial(hidden_kernel, n_col),
        (shape((block, hid), BF16), shape((classes, block), BF16)),
        (*arrived_one, other_one, weight_one, bias_one[None], w_two_t, kept),
    )
    chips_two = [proj, *fetch_chips(proj, "row", n_row)]
    if dense_form:
        near = chips_two[order(n_row).index(5)]
        early = [x for x in chips_two if x is not near]
        near_other = fetched(proj, "row", n_row, 2)
        others_two = [fetch_core(x, "row", n_row) for x in early] + [near_other]
        own_proj = others_two[0]
    else:
        own_proj = fetch_core(proj, "row", n_row)

    if dense_form:
        late = others_two
        places_two = [0, *reversed(range(1, len(early)))]
        half_two = call(
            functools.partial(half_two_kernel, places_two),
            shape((classes, n_col * block), F32),
            (dense, *[early[i] for i in places_two]),
            scratch=[pltpu.VMEM((classes, len(early) * block), BF16)],
        )
        pushed = call(
            late_kernel, shape((block, hid), BF16), (pushed, half_two), specs=[vmem, anywhere]
        )
        parts_two = call(
            functools.partial(layer_two_kernel, n_col),
            [shape((classes, block), BF16)] * n_col,
            (dense, half_two, late[0], near, *late[1:]),
            scratch=[pltpu.VMEM((classes, len(late) * block), BF16)],
        )
    else:
        other_slots = jnp.arange(n_row) ^ 1
        summed = call(
            functools.partial(tiles_kernel, n_row, n_col, True),
            shape((n_col, classes, block), BF16),
            (coords, tile_count, tile_set, both_cores(jnp.stack(chips_two), "row", n_row)[other_slots]),
            specs=[smem, smem, vmem, vmem],
            scratch=[pltpu.VMEM((n_col, classes, block), F32)],
        )
        parts_two = [summed[k] for k in range(n_col)]

    arrived_two = send_each(parts_two, "col", n_col)
    pushed = call(write_kernel, shape((block, hid), BF16), (fetch_core(pushed, "row", n_row),))
    pieces = 4
    scores = call(
        functools.partial(logits_kernel, n_col, pieces),
        shape((classes, 1, block), F32),
        (parts_two[0], *arrived_two, own_proj, bias_cols),
        scratch=[pltpu.VMEM((classes, 1, block), F32), pltpu.SemaphoreType.DMA((pieces,))],
        out_specs=pl.BlockSpec(memory_space=pl.ANY),
    )
    return pushed[None, None], scores.transpose(1, 2, 0)[None]


def solution(mesh):
    sizes = mesh.shape
    return jax.shard_map(
        functools.partial(on_device, sizes["row"], sizes["col"]),
        mesh=mesh,
        in_specs=(
            P("row", "col", None, None),
            P("row", "col", None, None, None),
            P("row", "col", None, None),
            P("row", "col"),
            P("row", "col", None),
            P("row", "col", None, None),
            P(),
            P(),
            P(),
            P(),
        ),
        out_specs=(P("row", "col", None, None), P("row", "col", None, None)),
        check_vma=False,
    )
```

```python
import functools

import jax
import jax.numpy as jnp
from jax import lax
from jax.experimental import pallas as pl
from jax.experimental.pallas import tpu as pltpu
from jax.sharding import PartitionSpec as P

BF16 = jnp.bfloat16
F32 = jnp.float32
VMEM_LIMIT = 48 * 1024 * 1024


def partner(index, slot):
    return index ^ slot


def turned(slot):
    return slot ^ (((slot >> 1) ^ (slot >> 2)) & 1) * 6


def seen(slot, index):
    return slot ^ (index & 1) * (turned(slot) ^ slot)


def order(size):
    return [0, *reversed(range(3, size, 2))]


def column_order(size):
    return order(size) + [turned(slot) ^ 1 for slot in order(size)]


def permuted(block, axis, size, slot):
    return lax.ppermute(block, axis, [(i, partner(i, slot)) for i in range(size)])


def fetched(block, axis, size, slot):
    return lax.ppermute(block, axis, [(partner(i, seen(slot, i)), i) for i in range(size)])


def fetch_chips(block, axis, size):
    return [fetched(block, axis, size, slot) for slot in order(size)[1:]]


def fetch_core(blocks, axis, size):
    return permuted(blocks, axis, size, 1)


def both_cores(blocks, axis, size):
    found = jnp.concatenate([blocks, fetch_core(blocks, axis, size)])
    return found[jnp.argsort(jnp.array(column_order(size)))]


def send_across(blocks, n_row, n_col):
    arrived = []
    for slot in reversed(range(n_col)):
        pairs = [
            (row * n_col + col, partner(row, 1) * n_col + partner(col, slot))
            for row in range(n_row)
            for col in range(n_col)
        ]
        arrived.append(lax.ppermute(blocks[slot], ("row", "col"), pairs))
    return arrived


def send_each(blocks, axis, size):
    return [permuted(blocks[slot], axis, size, slot) for slot in reversed(range(1, size))]


def call(kernel, out_shape, operands, specs=None, scratch=(), cost=None, out_specs=None):
    vmem = pl.BlockSpec(memory_space=pltpu.VMEM)
    return pl.pallas_call(
        kernel,
        out_shape=out_shape,
        in_specs=specs or [vmem] * len(operands),
        out_specs=out_specs or jax.tree.map(lambda _: vmem, out_shape),
        scratch_shapes=list(scratch),
        cost_estimate=cost,
        compiler_params=pltpu.CompilerParams(vmem_limit_bytes=VMEM_LIMIT),
    )(*operands)


def dot_nt(left, right):
    return lax.dot_general(left, right, (((1,), (1,)), ((), ())), preferred_element_type=F32)


def build_kernel(
    n_row, n_col, chunks, count, coords_hbm, tiles_hbm, dense_ref, coords, tiles, first, second, sems, coords_sem
):
    slots, block = tiles.shape[0], tiles.shape[1]
    per, part = slots // chunks, block // 2
    copies = [
        pltpu.make_async_copy(
            tiles_hbm.at[pl.ds(i * per, per)], tiles.at[pl.ds(i * per, per)], sems.at[i]
        )
        for i in range(chunks)
    ]
    coords_copy = pltpu.make_async_copy(coords_hbm, coords, coords_sem)
    coords_copy.start()
    live = count[0, 0]
    for i, copy in enumerate(copies):
        pl.when(i * per < live)(copy.start)
    row, col = lax.axis_index("row"), lax.axis_index("col")
    first[...] = jnp.zeros_like(first)
    second[...] = jnp.zeros_like(second)
    coords_copy.wait()

    def place(t):
        at = partner(coords[0, t], col) * n_row + seen(partner(coords[1, t], row), row)
        return jnp.where(t < live, at, n_row * n_col)

    for i in range(chunks):

        @pl.when(i * per < live)
        def _():
            copies[i].wait()

            @pl.loop(0, per, unroll=8)
            def _(step):
                t = i * per + step
                at = place(t)
                first[at] += tiles[t, :part].astype(F32)
                second[at] += tiles[t, part:].astype(F32)

    for k in range(n_col):
        for j, slot in enumerate(column_order(n_row)):
            at = k * n_row + slot
            columns = slice(j * block, (j + 1) * block)
            dense_ref[k * block : k * block + part, columns] = first[at].astype(BF16)
            dense_ref[k * block + part : (k + 1) * block, columns] = second[at].astype(BF16)


def prepare_kernel(mask, bias, history, *refs):
    kept_out, bias_out, wide = refs[-3:]
    block, classes = history.shape[0], bias.shape[1]
    mask_cols = jnp.broadcast_to(mask[...].astype(F32), (block, block)).T
    chosen = jnp.concatenate([mask_cols] * (history.shape[1] // block), axis=1) == 1.0
    kept_out[...] = jnp.where(chosen, -1.0, history[...].astype(F32)).astype(BF16)
    wide[...] = jnp.zeros_like(wide)
    wide[:, :classes] = jnp.broadcast_to(bias[...], (block, classes))
    bias_out[...] = wide[...].T[:classes]


def join_rows_kernel(places, *refs):
    out = refs[-1]
    block = refs[0].shape[0]
    for ref, place in zip(refs, places):
        out[place * block : (place + 1) * block, :] = ref[...]


def half_one_kernel(dense_ref, mine_ref, out):
    half = mine_ref.shape[0]
    out[...] = jnp.dot(dense_ref[:, :half], mine_ref[...], preferred_element_type=F32)


def layer_one_kernel(dense_ref, first_ref, other_ref, *outputs):
    half, block = other_ref.shape[0], dense_ref.shape[0] // len(outputs)
    total = first_ref[...] + jnp.dot(
        dense_ref[:, half:], other_ref[...], preferred_element_type=F32
    )
    for k, out in enumerate(outputs):
        out[...] = total[k * block : (k + 1) * block, :].astype(BF16)


def hidden_kernel(n_col, *refs):
    parts = refs[:n_col]
    feats, w_one, b_one, w_two, kept, pushed_ref, proj_ref = refs[n_col:]
    total = feats[: kept.shape[0], :].astype(F32)
    for part in parts:
        total += part[...].astype(F32)
    pre = jnp.dot(total.astype(BF16), w_one[...], preferred_element_type=F32) + b_one[...]
    hidden = jnp.maximum(pre, 0.0)
    old = kept[...].astype(F32)
    pushed = jnp.where(old < 0.0, hidden, old).astype(BF16)
    pushed_ref[...] = pushed
    proj_ref[...] = dot_nt(w_two[...], pushed).astype(BF16)


def write_kernel(value, out):
    out[...] = value[...]


def late_kernel(value, after, out):
    del after
    out[...] = value[...]


def lanes(refs, scratch, places=None):
    block = refs[0].shape[1]
    for i, ref in zip(places or range(len(refs)), refs):
        scratch[:, i * block : (i + 1) * block] = ref[...]
    return scratch[...]


def half_two_kernel(places, dense_ref, *refs):
    blocks, (out, scratch) = refs[:-2], refs[-2:]
    half = dense_ref.shape[1] // 2
    out[...] = dot_nt(
        lanes(blocks, scratch, places), dense_ref[:, half : half + scratch.shape[1]]
    )


def layer_two_kernel(slots, dense_ref, first_ref, near_ref, rest_ref, *refs):
    outputs = refs[-len(slots) :]
    block, half = near_ref.shape[1], rest_ref.shape[1]
    at = slice(slots[0] * block, (slots[-1] + 1) * block)
    total = first_ref[:, at] + dot_nt(rest_ref[...], dense_ref[at, :half])
    total += dot_nt(near_ref[...], dense_ref[at, dense_ref.shape[1] - block :])
    for i, out in enumerate(outputs):
        out[...] = total[:, i * block : (i + 1) * block].astype(BF16)


def sent_two_kernel(slots, dense_ref, first_ref, own_ref, near_ref, *refs):
    rest = refs[-1]
    blocks, outputs = refs[: -len(slots) - 1], refs[-len(slots) - 1 : -1]
    lanes([own_ref, *blocks], rest)
    layer_two_kernel(slots, dense_ref, first_ref, near_ref, rest, *outputs)


def begin_kernel(*refs):
    total = refs[0][...].astype(F32)
    for ref in refs[1:-1]:
        total += ref[...].astype(F32)
    refs[-1][...] = total


def logits_kernel(pieces, begun, *refs):
    parts, (out_hbm, staged, sems) = refs[:-3], refs[-3:]
    step = -(-staged.shape[0] // pieces // 16) * 16
    copies = []
    for i in range(pieces):
        rows = slice(i * step, (i + 1) * step if i < pieces - 1 else staged.shape[0])
        total = begun[rows, :]
        for part in parts:
            total += part[rows, :].astype(F32)
        staged[rows, 0, :] = total
        copies.append(pltpu.make_async_copy(staged.at[rows], out_hbm.at[rows], sems.at[i]))
        copies[-1].start()
    for copy in copies:
        copy.wait()


def tiles_kernel(
    n_row, n_col, transposed, coords_ref, count_ref, tiles_ref, stacked_ref, out_ref, total
):
    row, col = lax.axis_index("row"), lax.axis_index("col")
    total[...] = jnp.zeros_like(total)

    @pl.loop(0, count_ref[0, 0])
    def _(t):
        k = partner(coords_ref[0, t], col)
        j = seen(partner(coords_ref[1, t], row), row)
        if transposed:
            total[k] += dot_nt(stacked_ref[j], tiles_ref[t])
        else:
            total[k] += jnp.dot(tiles_ref[t], stacked_ref[j], preferred_element_type=F32)

    out_ref[...] = total[...].astype(BF16)


def on_device(
    n_row, n_col,
    features, tiles, tile_coords, tile_count, batch_mask, history,
    weight_one, bias_one, weight_two, bias_two,
):
    feat, tile_set, hist = features[0, 0], tiles[0, 0], history[0, 0]
    coords = tile_coords[0, 0].T
    slots, block = tile_set.shape[0], tile_set.shape[1]
    f_in, hid, classes = feat.shape[1], weight_one.shape[1], weight_two.shape[1]
    w_two_t = weight_two.T
    dense_form = n_row * n_col <= slots
    smem = pl.BlockSpec(memory_space=pltpu.SMEM)
    vmem = pl.BlockSpec(memory_space=pltpu.VMEM)
    hbm = pl.BlockSpec(memory_space=pltpu.HBM)
    shape = jax.ShapeDtypeStruct

    def prepare(*after):
        return call(
            prepare_kernel,
            (shape((block, hid), BF16), shape((classes, block), F32)),
            (batch_mask[0], bias_two[None], hist, *after),
            specs=[vmem] * 3 + [pl.BlockSpec(memory_space=pl.ANY)] * len(after),
            scratch=[pltpu.VMEM((block, -(-classes // 128) * 128), F32)],
        )

    chips_one = [feat, *fetch_chips(feat, "row", n_row)]

    if dense_form:
        anywhere = pl.BlockSpec(memory_space=pl.ANY)
        chunks = 16
        dense = call(
            functools.partial(build_kernel, n_row, n_col, chunks),
            shape((n_col * block, n_row * block), BF16),
            (
                tile_count,
                pltpu.with_memory_space_constraint(coords, pltpu.HBM),
                pltpu.with_memory_space_constraint(tile_set, pltpu.HBM),
            ),
            specs=[smem, hbm, hbm],
            scratch=[
                pltpu.SMEM((2, slots), jnp.int32),
                pltpu.VMEM((slots, block, block), BF16),
                pltpu.VMEM((n_row * n_col + 1, block // 2, block), F32),
                pltpu.VMEM((n_row * n_col + 1, block // 2, block), F32),
                pltpu.SemaphoreType.DMA((chunks,)),
                pltpu.SemaphoreType.DMA(()),
            ],
            cost=pl.CostEstimate(
                flops=slots * block * block,
                bytes_accessed=2 * slots * block * block,
                transcendentals=0,
            ),
        )
        names = order(n_row)
        places_one = [0, *sorted(range(1, n_row // 2), key=lambda i: (names[i] != 5, names[i]))]
        mine_one = call(
            functools.partial(join_rows_kernel, places_one),
            shape((n_row // 2 * block, f_in), BF16),
            (*[chips_one[i] for i in places_one], dense),
            specs=[vmem] * len(chips_one) + [anywhere],
        )
        other_one = fetch_core(mine_one, "row", n_row)
        kept, bias_cols = prepare(mine_one)
        half_one = call(half_one_kernel, shape((n_col * block, f_in), F32), (dense, mine_one))
        parts_one = call(
            layer_one_kernel,
            [shape((block, f_in), BF16)] * n_col,
            (dense, half_one, other_one),
        )
    else:
        kept, bias_cols = prepare()
        summed = call(
            functools.partial(tiles_kernel, n_row, n_col, False),
            shape((n_col, block, f_in), BF16),
            (coords, tile_count, tile_set, both_cores(jnp.stack(chips_one), "row", n_row)),
            specs=[smem, smem, vmem, vmem],
            scratch=[pltpu.VMEM((n_col, block, f_in), F32)],
        )
        parts_one = [summed[k] for k in range(n_col)]
        other_one = fetch_core(feat, "row", n_row)

    arrived_one = send_across(parts_one, n_row, n_col)
    kept = fetch_core(kept, "row", n_row)
    pushed, proj = call(
        functools.partial(hidden_kernel, n_col),
        (shape((block, hid), BF16), shape((classes, block), BF16)),
        (*arrived_one, other_one, weight_one, bias_one[None], w_two_t, kept),
    )
    chips_two = [proj, *fetch_chips(proj, "row", n_row)]
    if dense_form:
        near = chips_two[order(n_row).index(5)]
        early = [x for x in chips_two if x is not near]
        near_other = fetched(proj, "row", n_row, 2)
        others_two = [fetch_core(x, "row", n_row) for x in early] + [near_other]
        own_proj = others_two[0]
    else:
        own_proj = fetch_core(proj, "row", n_row)

    if dense_form:
        late = others_two
        places_two = [0, *reversed(range(1, len(early)))]
        half_two = call(
            functools.partial(half_two_kernel, places_two),
            shape((classes, n_col * block), F32),
            (dense, *[early[i] for i in places_two]),
            scratch=[pltpu.VMEM((classes, len(early) * block), BF16)],
        )
        pushed = call(
            late_kernel, shape((block, hid), BF16), (pushed, half_two), specs=[vmem, anywhere]
        )
        sent = range(1, n_col)
        *sent_two, rest = call(
            functools.partial(sent_two_kernel, sent),
            [shape((classes, block), BF16)] * len(sent)
            + [shape((classes, len(late) * block), BF16)],
            (dense, half_two, late[0], near, *late[1:]),
        )
        own_two = call(
            functools.partial(layer_two_kernel, [0]),
            [shape((classes, block), BF16)],
            (dense, half_two, near, rest, sent_two[0]),
            specs=[vmem] * 4 + [anywhere],
        )
        parts_two = [*own_two, *sent_two]
    else:
        other_slots = jnp.arange(n_row) ^ 1
        summed = call(
            functools.partial(tiles_kernel, n_row, n_col, True),
            shape((n_col, classes, block), BF16),
            (coords, tile_count, tile_set, both_cores(jnp.stack(chips_two), "row", n_row)[other_slots]),
            specs=[smem, smem, vmem, vmem],
            scratch=[pltpu.VMEM((n_col, classes, block), F32)],
        )
        parts_two = [summed[k] for k in range(n_col)]

    arrived_two = send_each(parts_two, "col", n_col)
    pushed = call(write_kernel, shape((block, hid), BF16), (fetch_core(pushed, "row", n_row),))
    pieces = 4
    begun_two = call(
        begin_kernel,
        shape((classes, block), F32),
        (bias_cols, own_proj, parts_two[0], arrived_two[0]),
    )
    scores = call(
        functools.partial(logits_kernel, pieces),
        shape((classes, 1, block), F32),
        (begun_two, *arrived_two[1:]),
        scratch=[pltpu.VMEM((classes, 1, block), F32), pltpu.SemaphoreType.DMA((pieces,))],
        out_specs=pl.BlockSpec(memory_space=pl.ANY),
    )
    return pushed[None, None], scores.transpose(1, 2, 0)[None]


def solution(mesh):
    sizes = mesh.shape
    return jax.shard_map(
        functools.partial(on_device, sizes["row"], sizes["col"]),
        mesh=mesh,
        in_specs=(
            P("row", "col", None, None),
            P("row", "col", None, None, None),
            P("row", "col", None, None),
            P("row", "col"),
            P("row", "col", None),
            P("row", "col", None, None),
            P(),
            P(),
            P(),
            P(),
        ),
        out_specs=(P("row", "col", None, None), P("row", "col", None, None)),
        check_vma=False,
    )
```

```python
import functools

import jax
import jax.numpy as jnp
from jax import lax
from jax.experimental import pallas as pl
from jax.experimental.pallas import tpu as pltpu
from jax.sharding import PartitionSpec as P

BF16 = jnp.bfloat16
F32 = jnp.float32
VMEM_LIMIT = 48 * 1024 * 1024


def partner(index, slot):
    return index ^ slot


def turned(slot):
    return slot ^ (((slot >> 1) ^ (slot >> 2)) & 1) * 6


def seen(slot, index):
    return slot ^ (index & 1) * (turned(slot) ^ slot)


def order(size):
    return [0, *reversed(range(3, size, 2))]


def column_order(size):
    return order(size) + [turned(slot) ^ 1 for slot in order(size)]


def permuted(block, axis, size, slot):
    return lax.ppermute(block, axis, [(i, partner(i, slot)) for i in range(size)])


def fetched(block, axis, size, slot):
    return lax.ppermute(block, axis, [(partner(i, seen(slot, i)), i) for i in range(size)])


def fetch_chips(block, axis, size):
    return [fetched(block, axis, size, slot) for slot in order(size)[1:]]


def fetch_core(blocks, axis, size):
    return permuted(blocks, axis, size, 1)


def both_cores(blocks, axis, size):
    found = jnp.concatenate([blocks, fetch_core(blocks, axis, size)])
    return found[jnp.argsort(jnp.array(column_order(size)))]


def send_across(blocks, n_row, n_col):
    arrived = []
    for slot in reversed(range(n_col)):
        pairs = [
            (row * n_col + col, partner(row, 1) * n_col + partner(col, slot))
            for row in range(n_row)
            for col in range(n_col)
        ]
        arrived.append(lax.ppermute(blocks[slot], ("row", "col"), pairs))
    return arrived


def send_each(blocks, axis, size):
    return [permuted(blocks[slot], axis, size, slot) for slot in reversed(range(1, size))]


def call(kernel, out_shape, operands, specs=None, scratch=(), cost=None, out_specs=None):
    vmem = pl.BlockSpec(memory_space=pltpu.VMEM)
    return pl.pallas_call(
        kernel,
        out_shape=out_shape,
        in_specs=specs or [vmem] * len(operands),
        out_specs=out_specs or jax.tree.map(lambda _: vmem, out_shape),
        scratch_shapes=list(scratch),
        cost_estimate=cost,
        compiler_params=pltpu.CompilerParams(vmem_limit_bytes=VMEM_LIMIT),
    )(*operands)


def dot_nt(left, right):
    return lax.dot_general(left, right, (((1,), (1,)), ((), ())), preferred_element_type=F32)


def build_kernel(
    n_row, n_col, chunks, count, coords_hbm, tiles_hbm, dense_ref, coords, tiles, first, second, sems, coords_sem
):
    slots, block = tiles.shape[0], tiles.shape[1]
    per, part = slots // chunks, block // 2
    copies = [
        pltpu.make_async_copy(
            tiles_hbm.at[pl.ds(i * per, per)], tiles.at[pl.ds(i * per, per)], sems.at[i]
        )
        for i in range(chunks)
    ]
    coords_copy = pltpu.make_async_copy(coords_hbm, coords, coords_sem)
    coords_copy.start()
    live = count[0, 0]
    for i, copy in enumerate(copies):
        pl.when(i * per < live)(copy.start)
    row, col = lax.axis_index("row"), lax.axis_index("col")
    first[...] = jnp.zeros_like(first)
    second[...] = jnp.zeros_like(second)
    coords_copy.wait()

    def place(t):
        at = partner(coords[0, t], col) * n_row + seen(partner(coords[1, t], row), row)
        return jnp.where(t < live, at, n_row * n_col)

    for i in range(chunks):

        @pl.when(i * per < live)
        def _():
            copies[i].wait()

            @pl.loop(0, per, unroll=16)
            def _(step):
                t = i * per + step
                at = place(t)
                first[at] += tiles[t, :part].astype(F32)
                second[at] += tiles[t, part:].astype(F32)

    for k in range(n_col):
        for j, slot in enumerate(column_order(n_row)):
            at = k * n_row + slot
            columns = slice(j * block, (j + 1) * block)
            dense_ref[k * block : k * block + part, columns] = first[at].astype(BF16)
            dense_ref[k * block + part : (k + 1) * block, columns] = second[at].astype(BF16)


def prepare_kernel(mask, bias, history, *refs):
    kept_out, bias_out, wide = refs[-3:]
    block, classes = history.shape[0], bias.shape[1]
    mask_cols = jnp.broadcast_to(mask[...].astype(F32), (block, block)).T
    chosen = jnp.concatenate([mask_cols] * (history.shape[1] // block), axis=1) == 1.0
    kept_out[...] = jnp.where(chosen, -1.0, history[...].astype(F32)).astype(BF16)
    wide[...] = jnp.zeros_like(wide)
    wide[:, :classes] = jnp.broadcast_to(bias[...], (block, classes))
    bias_out[...] = wide[...].T[:classes]


def join_rows_kernel(places, *refs):
    out = refs[-1]
    block = refs[0].shape[0]
    for ref, place in zip(refs, places):
        out[place * block : (place + 1) * block, :] = ref[...]


def half_one_kernel(dense_ref, mine_ref, out):
    half = mine_ref.shape[0]
    out[...] = jnp.dot(dense_ref[:, :half], mine_ref[...], preferred_element_type=F32)


def layer_one_kernel(dense_ref, first_ref, other_ref, *outputs):
    half, block = other_ref.shape[0], dense_ref.shape[0] // len(outputs)
    total = first_ref[...] + jnp.dot(
        dense_ref[:, half:], other_ref[...], preferred_element_type=F32
    )
    for k, out in enumerate(outputs):
        out[...] = total[k * block : (k + 1) * block, :].astype(BF16)


def hidden_kernel(n_col, *refs):
    parts = refs[:n_col]
    feats, w_one, b_one, w_two, kept, pushed_ref, proj_ref = refs[n_col:]
    total = feats[: kept.shape[0], :].astype(F32)
    for part in parts:
        total += part[...].astype(F32)
    pre = jnp.dot(total.astype(BF16), w_one[...], preferred_element_type=F32) + b_one[...]
    hidden = jnp.maximum(pre, 0.0)
    old = kept[...].astype(F32)
    pushed = jnp.where(old < 0.0, hidden, old).astype(BF16)
    pushed_ref[...] = pushed
    proj_ref[...] = dot_nt(w_two[...], pushed).astype(BF16)


def write_kernel(value, out):
    out[...] = value[...]


def late_kernel(value, after, out):
    del after
    out[...] = value[...]


def lanes(refs, scratch, places=None):
    block = refs[0].shape[1]
    for i, ref in zip(places or range(len(refs)), refs):
        scratch[:, i * block : (i + 1) * block] = ref[...]
    return scratch[...]


def half_two_kernel(places, dense_ref, *refs):
    blocks, (out, scratch) = refs[:-2], refs[-2:]
    half = dense_ref.shape[1] // 2
    out[...] = dot_nt(
        lanes(blocks, scratch, places), dense_ref[:, half : half + scratch.shape[1]]
    )


def layer_two_kernel(n_col, dense_ref, first_ref, own_ref, near_ref, *refs):
    blocks, outputs, scratch = refs[: -n_col - 1], refs[-n_col - 1 : -1], refs[-1]
    block, half = near_ref.shape[1], scratch.shape[1]
    rest = lanes([own_ref, *blocks], scratch)
    total = first_ref[...] + dot_nt(rest, dense_ref[:, :half])
    total += dot_nt(near_ref[...], dense_ref[:, dense_ref.shape[1] - block :])
    for k, out in enumerate(outputs):
        out[...] = total[:, k * block : (k + 1) * block].astype(BF16)


def logits_kernel(n_col, pieces, *refs):
    parts = refs[:n_col]
    proj, bias, out_hbm, staged, sems = refs[n_col:]
    step = -(-staged.shape[0] // pieces // 16) * 16
    copies = []
    for i in range(pieces):
        rows = slice(i * step, (i + 1) * step if i < pieces - 1 else staged.shape[0])
        total = proj[rows, :].astype(F32) + bias[rows, :]
        for part in parts:
            total += part[rows, :].astype(F32)
        staged[rows, 0, :] = total
        copies.append(pltpu.make_async_copy(staged.at[rows], out_hbm.at[rows], sems.at[i]))
        copies[-1].start()
    for copy in copies:
        copy.wait()


def tiles_kernel(
    n_row, n_col, transposed, coords_ref, count_ref, tiles_ref, stacked_ref, out_ref, total
):
    row, col = lax.axis_index("row"), lax.axis_index("col")
    total[...] = jnp.zeros_like(total)

    @pl.loop(0, count_ref[0, 0])
    def _(t):
        k = partner(coords_ref[0, t], col)
        j = seen(partner(coords_ref[1, t], row), row)
        if transposed:
            total[k] += dot_nt(stacked_ref[j], tiles_ref[t])
        else:
            total[k] += jnp.dot(tiles_ref[t], stacked_ref[j], preferred_element_type=F32)

    out_ref[...] = total[...].astype(BF16)


def on_device(
    n_row, n_col,
    features, tiles, tile_coords, tile_count, batch_mask, history,
    weight_one, bias_one, weight_two, bias_two,
):
    feat, tile_set, hist = features[0, 0], tiles[0, 0], history[0, 0]
    coords = tile_coords[0, 0].T
    slots, block = tile_set.shape[0], tile_set.shape[1]
    f_in, hid, classes = feat.shape[1], weight_one.shape[1], weight_two.shape[1]
    w_two_t = weight_two.T
    dense_form = n_row * n_col <= slots
    smem = pl.BlockSpec(memory_space=pltpu.SMEM)
    vmem = pl.BlockSpec(memory_space=pltpu.VMEM)
    hbm = pl.BlockSpec(memory_space=pltpu.HBM)
    shape = jax.ShapeDtypeStruct

    def prepare(*after):
        return call(
            prepare_kernel,
            (shape((block, hid), BF16), shape((classes, block), F32)),
            (batch_mask[0], bias_two[None], hist, *after),
            specs=[vmem] * 3 + [pl.BlockSpec(memory_space=pl.ANY)] * len(after),
            scratch=[pltpu.VMEM((block, -(-classes // 128) * 128), F32)],
        )

    chips_one = [feat, *fetch_chips(feat, "row", n_row)]

    if dense_form:
        anywhere = pl.BlockSpec(memory_space=pl.ANY)
        chunks = 8
        dense = call(
            functools.partial(build_kernel, n_row, n_col, chunks),
            shape((n_col * block, n_row * block), BF16),
            (
                tile_count,
                pltpu.with_memory_space_constraint(coords, pltpu.HBM),
                pltpu.with_memory_space_constraint(tile_set, pltpu.HBM),
            ),
            specs=[smem, hbm, hbm],
            scratch=[
                pltpu.SMEM((2, slots), jnp.int32),
                pltpu.VMEM((slots, block, block), BF16),
                pltpu.VMEM((n_row * n_col + 1, block // 2, block), F32),
                pltpu.VMEM((n_row * n_col + 1, block // 2, block), F32),
                pltpu.SemaphoreType.DMA((chunks,)),
                pltpu.SemaphoreType.DMA(()),
            ],
            cost=pl.CostEstimate(
                flops=slots * block * block,
                bytes_accessed=2 * slots * block * block,
                transcendentals=0,
            ),
        )
        names = order(n_row)
        places_one = [0, *sorted(range(1, n_row // 2), key=lambda i: (names[i] != 5, names[i]))]
        mine_one = call(
            functools.partial(join_rows_kernel, places_one),
            shape((n_row // 2 * block, f_in), BF16),
            (*[chips_one[i] for i in places_one], dense),
            specs=[vmem] * len(chips_one) + [anywhere],
        )
        other_one = fetch_core(mine_one, "row", n_row)
        kept, bias_cols = prepare(mine_one)
        half_one = call(half_one_kernel, shape((n_col * block, f_in), F32), (dense, mine_one))
        parts_one = call(
            layer_one_kernel,
            [shape((block, f_in), BF16)] * n_col,
            (dense, half_one, other_one),
        )
    else:
        kept, bias_cols = prepare()
        summed = call(
            functools.partial(tiles_kernel, n_row, n_col, False),
            shape((n_col, block, f_in), BF16),
            (coords, tile_count, tile_set, both_cores(jnp.stack(chips_one), "row", n_row)),
            specs=[smem, smem, vmem, vmem],
            scratch=[pltpu.VMEM((n_col, block, f_in), F32)],
        )
        parts_one = [summed[k] for k in range(n_col)]
        other_one = fetch_core(feat, "row", n_row)

    arrived_one = send_across(parts_one, n_row, n_col)
    kept = fetch_core(kept, "row", n_row)
    pushed, proj = call(
        functools.partial(hidden_kernel, n_col),
        (shape((block, hid), BF16), shape((classes, block), BF16)),
        (*arrived_one, other_one, weight_one, bias_one[None], w_two_t, kept),
    )
    chips_two = [proj, *fetch_chips(proj, "row", n_row)]
    if dense_form:
        near = chips_two[order(n_row).index(5)]
        early = [x for x in chips_two if x is not near]
        near_other = fetched(proj, "row", n_row, 2)
        others_two = [fetch_core(x, "row", n_row) for x in early] + [near_other]
        own_proj = others_two[0]
    else:
        own_proj = fetch_core(proj, "row", n_row)

    if dense_form:
        late = others_two
        places_two = [0, *reversed(range(1, len(early)))]
        half_two = call(
            functools.partial(half_two_kernel, places_two),
            shape((classes, n_col * block), F32),
            (dense, *[early[i] for i in places_two]),
            scratch=[pltpu.VMEM((classes, len(early) * block), BF16)],
        )
        pushed = call(
            late_kernel, shape((block, hid), BF16), (pushed, half_two), specs=[vmem, anywhere]
        )
        parts_two = call(
            functools.partial(layer_two_kernel, n_col),
            [shape((classes, block), BF16)] * n_col,
            (dense, half_two, late[0], near, *late[1:]),
            scratch=[pltpu.VMEM((classes, len(late) * block), BF16)],
        )
    else:
        other_slots = jnp.arange(n_row) ^ 1
        summed = call(
            functools.partial(tiles_kernel, n_row, n_col, True),
            shape((n_col, classes, block), BF16),
            (coords, tile_count, tile_set, both_cores(jnp.stack(chips_two), "row", n_row)[other_slots]),
            specs=[smem, smem, vmem, vmem],
            scratch=[pltpu.VMEM((n_col, classes, block), F32)],
        )
        parts_two = [summed[k] for k in range(n_col)]

    arrived_two = send_each(parts_two, "col", n_col)
    pushed = call(write_kernel, shape((block, hid), BF16), (fetch_core(pushed, "row", n_row),))
    pieces = 4
    scores = call(
        functools.partial(logits_kernel, n_col, pieces),
        shape((classes, 1, block), F32),
        (parts_two[0], *arrived_two, own_proj, bias_cols),
        scratch=[pltpu.VMEM((classes, 1, block), F32), pltpu.SemaphoreType.DMA((pieces,))],
        out_specs=pl.BlockSpec(memory_space=pl.ANY),
    )
    return pushed[None, None], scores.transpose(1, 2, 0)[None]


def solution(mesh):
    sizes = mesh.shape
    return jax.shard_map(
        functools.partial(on_device, sizes["row"], sizes["col"]),
        mesh=mesh,
        in_specs=(
            P("row", "col", None, None),
            P("row", "col", None, None, None),
            P("row", "col", None, None),
            P("row", "col"),
            P("row", "col", None),
            P("row", "col", None, None),
            P(),
            P(),
            P(),
            P(),
        ),
        out_specs=(P("row", "col", None, None), P("row", "col", None, None)),
        check_vma=False,
    )
```
